128 devices in a mesh: ctx: 32 (over z_lo, y, x), fsdp: 4 (over z_hi, core).
Axes of the slice: x: 4, y: 4, z: 4 (z_hi: 2, z_lo: 2; z = z_hi * 2 + z_lo), core: 2. Of those that a mesh axis runs over, the one named last changes fastest.
Arguments:
- tokens: bfloat16 [4, 4096, 1024], P('fsdp', 'ctx'), may hold values from -6 to 6
- query_weight: bfloat16 [1024, 2048], P('fsdp'), may hold values from -0.1875 to 0.1875
- key_weight: bfloat16 [1024, 1024], P('fsdp'), may hold values from -0.1875 to 0.1875
- value_weight: bfloat16 [1024, 1024], P('fsdp'), may hold values from -0.1875 to 0.1875
- out_weight: bfloat16 [1024, 2048], P('fsdp'), may hold values from -3 to 3
- gate_weight: bfloat16 [1024, 3072], P('fsdp'), may hold values from -0.1875 to 0.1875
- up_weight: bfloat16 [1024, 3072], P('fsdp'), may hold values from -0.1875 to 0.1875
- down_weight: bfloat16 [1024, 3072], P('fsdp'), may hold values from -0.21875 to 0.21875
- attn_gain: float32 [1024], replicated, may hold values from 0.5 to 1.5
- mlp_gain: float32 [1024], replicated, may hold values from 0.5 to 1.5
- query_gain: float32 [128], replicated, may hold values from 1 to 1.6
- key_gain: float32 [128], replicated, may hold values from 1 to 1.6
- pair_order: int32 [4, 32], P('fsdp'), may hold values from 0 to 31, each once within a row
- out_grad: bfloat16 [4, 4096, 1024], P('fsdp', 'ctx'), may hold values from -6 to 6
Outputs:
- output: bfloat16 [4, 4096, 1024], P('fsdp', 'ctx')
- input_grad: float32 [4, 4096, 1024], P('fsdp', 'ctx')
- query_weight_grad: float32 [1024, 2048], P('fsdp')
- key_weight_grad: float32 [1024, 1024], P('fsdp')
- value_weight_grad: float32 [1024, 1024], P('fsdp')
- out_weight_grad: float32 [1024, 2048], P('fsdp')
- gate_weight_grad: float32 [1024, 3072], P('fsdp')
- up_weight_grad: float32 [1024, 3072], P('fsdp')
- down_weight_grad: float32 [1024, 3072], P('fsdp')
- attn_gain_grad: float32 [1024], replicated
- mlp_gain_grad: float32 [1024], replicated
- query_gain_grad: float32 [128], replicated
- key_gain_grad: float32 [128], replicated
The draws below stay inside these ranges and needn't reach their ends.
Inputs may be any that keep to these rules, and one draw needn't show every extreme that they name: Each row is a permutation of 0 to 31; device c of the context axis holds blocks pair_order[s, c] and 63 - pair_order[s, c] of sequence s, each of 64 tokens, in that order.
All inputs are finite; a program needn't handle non-finite values.
Results may differ from the reference program's by a relative error of at most 0.035.
Values may be sent and summed in bfloat16 or wider, within the bound.
A program may use at most 256 MiB of HBM per device.

```python
import jax
import jax.numpy as jnp
from jax import lax

D = 1024
HEADS = 16
KV_HEADS = 8
HEAD_DIM = 128
FF = 3072
HALF = 64
QW = 2048
KW = 1024
SEQS = 4
SEQ_TOK = 4096
N_CTX = 32


def block_levels(key, dims, cuts, least, largest):
    level = 1.0
    for position, shards_of in cuts:
        draws = jax.random.uniform(jax.random.fold_in(jax.random.fold_in(key, 6), position), (shards_of,), jnp.float32, least / len(cuts), largest / len(cuts))
        level = level * jnp.repeat(jnp.exp(draws), dims[position] // shards_of).reshape((-1,) + (1,) * (len(dims) - 1 - position))
    return level


def bell_draw(key, dims, width, reach, shards=(), kind=jnp.bfloat16):
    drawn = width * jax.random.normal(key, dims, jnp.float32)
    if shards:
        drawn = drawn * block_levels(key, dims, shards, -0.22, 0.18)
    return jnp.clip(drawn, -reach, reach).astype(kind)


def setup_inputs(seed: int = 0) -> dict:
    seeds = jax.random.split(jax.random.key(seed), 15)
    tokens = bell_draw(seeds[0], (SEQS, SEQ_TOK, D), 1.0, 6.0, ((0, 4), (1, 32)))
    query_weight = bell_draw(seeds[1], (D, QW), D ** -0.5, 0.1875, ((0, 4),))
    key_weight = bell_draw(seeds[2], (D, KW), D ** -0.5, 0.1875, ((0, 4),))
    value_weight = bell_draw(seeds[3], (D, KW), D ** -0.5, 0.1875, ((0, 4),))
    out_weight = bell_draw(seeds[4], (D, QW), (max(1, QW * 8 // SEQ_TOK)) ** -0.5, 3.0, ((0, 4),))
    gate_weight = bell_draw(seeds[5], (D, FF), D ** -0.5, 0.1875, ((0, 4),))
    up_weight = bell_draw(seeds[6], (D, FF), D ** -0.5, 0.1875, ((0, 4),))
    down_weight = bell_draw(seeds[7], (D, FF), (FF // 4) ** -0.5, 0.21875, ((0, 4),))
    attn_gain = jnp.clip(1.0 + 0.1 * jax.random.normal(seeds[8], (D,), jnp.float32), 0.5, 1.5)
    mlp_gain = jnp.clip(1.0 + 0.1 * jax.random.normal(seeds[9], (D,), jnp.float32), 0.5, 1.5)
    query_gain = jnp.clip(jax.random.uniform(seeds[10], (HEAD_DIM,), jnp.float32, 1.0, 1.6), 1.0, 1.6)
    key_gain = jnp.clip(jax.random.uniform(seeds[11], (HEAD_DIM,), jnp.float32, 1.0, 1.6), 1.0, 1.6)
    pair_order = jax.vmap(lambda own: jax.random.permutation(own, N_CTX))(jax.random.split(seeds[12], SEQS)).reshape((SEQS, N_CTX)).astype(jnp.int32)
    out_grad = bell_draw(seeds[13], (SEQS, SEQ_TOK, D), 1.0, 6.0, ((0, 4), (1, 32)))
    return dict(tokens=tokens, query_weight=query_weight, key_weight=key_weight, value_weight=value_weight, out_weight=out_weight, gate_weight=gate_weight, up_weight=up_weight, down_weight=down_weight, attn_gain=attn_gain, mlp_gain=mlp_gain, query_gain=query_gain, key_gain=key_gain, pair_order=pair_order, out_grad=out_grad)


@jax.custom_vjp
def low(v):
    return lax.optimization_barrier(v.astype(jnp.bfloat16)).astype(jnp.float32)

@jax.custom_vjp
def low_back(v):
    return v

def low_keep(v):
    return (low(v), None)

def low_pass(kept, grad):
    return (grad,)

def back_keep(v):
    return (v, None)

def back_low(kept, grad):
    return (low(grad),)
low.defvjp(low_keep, low_pass)
low_back.defvjp(back_keep, back_low)
EPSILON = 1e-06
ROPE_BASE = 1000000.0
MASKED = -1e+30

def matmul(matrix, second):
    return jnp.dot(matrix, second, precision=lax.Precision.HIGHEST, preferred_element_type=jnp.float32)

def matmul_rows(matrix, second):
    return lax.dot_general(matrix, second, (((1,), (1,)), ((), ())), precision=lax.Precision.HIGHEST, preferred_element_type=jnp.float32)

def token_positions(pair_row, row_index, half_len, ctx_count):
    owner_dev = row_index // (2 * half_len)
    inner_row = row_index % (2 * half_len)
    matches = owner_dev[:, None] == jnp.arange(ctx_count, dtype=jnp.int32)[None, :]
    first_block = lax.optimization_barrier(jnp.sum(jnp.where(matches, pair_row[None, :], 0), axis=1)).astype(jnp.int32)
    block_index = jnp.where(inner_row < half_len, first_block, 2 * ctx_count - 1 - first_block)
    return (block_index * half_len + inner_row % half_len).astype(jnp.int32)

def rms_scale(values):
    return lax.rsqrt(lax.optimization_barrier(jnp.mean(values * values, axis=-1, keepdims=True)) + EPSILON)

def rotate(values, positions):
    extent = values.shape[-1]
    frequency = jnp.power(ROPE_BASE, -jnp.arange(0, extent, 2, dtype=jnp.float32) / extent)
    angles = positions.astype(jnp.float32)[:, None] * frequency[None, :]
    cosine = jnp.concatenate([jnp.cos(angles), jnp.cos(angles)], -1)[:, None, :]
    sine_rows = jnp.concatenate([jnp.sin(angles), jnp.sin(angles)], -1)[:, None, :]
    lower_half = values[..., :extent // 2]
    upper_half = values[..., extent // 2:]
    return values * cosine + jnp.concatenate([-upper_half, lower_half], -1) * sine_rows

def attention(queries, key_rows, value_rows, positions):
    group_size = HEADS // KV_HEADS
    block_rows = min(512, SEQ_TOK)
    count_blocks = SEQ_TOK // block_rows
    score_scale = HEAD_DIM ** (-0.5)

    def one_block(inputs):
        query_block, query_pos = inputs
        grouped = query_block.reshape(block_rows, KV_HEADS, group_size, HEAD_DIM)
        scores = jnp.einsum('qkgd,tkd->kgqt', grouped, key_rows, precision=lax.Precision.HIGHEST) * score_scale
        scores = low_back(scores)
        allowed = query_pos[:, None] >= positions[None, :]
        masked = jnp.where(allowed, scores, MASKED)
        row_peak = lax.optimization_barrier(jnp.max(masked, axis=-1, keepdims=True))
        denominator = lax.optimization_barrier(jnp.sum(jnp.where(allowed, jnp.exp(masked - row_peak), 0.0), axis=-1, keepdims=True))
        log_total = row_peak + jnp.log(denominator)
        prob_rows = jnp.where(allowed, jnp.exp(masked - log_total), 0.0)
        mixture = jnp.einsum('kgqt,tkd->qkgd', low(prob_rows), value_rows, precision=lax.Precision.HIGHEST)
        return mixture.reshape(block_rows, HEADS * HEAD_DIM)
    outputs = lax.map(jax.checkpoint(one_block), (queries.reshape(count_blocks, block_rows, HEADS, HEAD_DIM), positions.reshape(count_blocks, block_rows)))
    return outputs.reshape(SEQ_TOK, HEADS * HEAD_DIM)

def layer_forward(inputs, query_weight, key_weight, value_weight, out_weight, gate_weight, up_weight, down_weight, attn_gain, mlp_gain, query_gain, key_gain, positions):
    attn_normed = inputs * rms_scale(inputs)
    attn_in = low(attn_normed * attn_gain)
    query_raw = low_back(matmul(attn_in, query_weight)).reshape(SEQ_TOK, HEADS, HEAD_DIM)
    key_raw = low_back(matmul(attn_in, key_weight)).reshape(SEQ_TOK, KV_HEADS, HEAD_DIM)
    value_rows = low(low_back(matmul(attn_in, value_weight))).reshape(SEQ_TOK, KV_HEADS, HEAD_DIM)
    query_rot = low(rotate(query_raw * rms_scale(query_raw) * query_gain, positions))
    key_rot = low(rotate(key_raw * rms_scale(key_raw) * key_gain, positions))
    attended = low(low_back(attention(query_rot, key_rot, value_rows, positions)))
    middle = inputs + low_back(matmul_rows(attended, out_weight))
    mlp_in = low(middle * rms_scale(middle) * mlp_gain)
    gate_pre = low_back(matmul(mlp_in, gate_weight))
    up_pre = low_back(matmul(mlp_in, up_weight))
    hidden = low(jax.nn.silu(gate_pre) * up_pre)
    return middle + low_back(matmul_rows(hidden, down_weight))

def reference(tokens, query_weight, key_weight, value_weight, out_weight, gate_weight, up_weight, down_weight, attn_gain, mlp_gain, query_gain, key_gain, pair_order, out_grad):
    weight_set = tuple((matrix.astype(jnp.float32) for matrix in (query_weight, key_weight, value_weight, out_weight, gate_weight, up_weight, down_weight)))
    gain_set = (attn_gain, mlp_gain, query_gain, key_gain)

    def forward(inputs, weights_in, gains_in):

        def one_sequence(scan_carry, scan_item):
            sequence, pair_row = scan_item
            positions = token_positions(pair_row, jnp.arange(SEQ_TOK, dtype=jnp.int32), HALF, N_CTX)
            return (scan_carry, layer_forward(sequence, *weights_in, *gains_in, positions))
        unused, result = lax.scan(one_sequence, jnp.zeros((), jnp.float32), (inputs, pair_order))
        return result
    result, pullback = jax.vjp(forward, tokens.astype(jnp.float32), weight_set, gain_set)
    input_grad, weight_grads, gain_grads = pullback(out_grad.astype(jnp.float32))
    return (result.astype(jnp.bfloat16), input_grad, weight_grads[0], weight_grads[1], weight_grads[2], weight_grads[3], weight_grads[4], weight_grads[5], weight_grads[6], gain_grads[0], gain_grads[1], gain_grads[2], gain_grads[3])
```

```python
import functools

import jax
import jax.numpy as jnp
from jax import lax
from jax.experimental import pallas as pl
from jax.experimental.pallas import tpu as pltpu
from jax.sharding import PartitionSpec as P

EPSILON = 1e-06
ROPE_BASE = 1000000.0
MESH = pl.DeviceIdType.MESH
HBM = pl.BlockSpec(memory_space=pltpu.HBM)
VMEM = pl.BlockSpec(memory_space=pltpu.VMEM)
SMEM = pl.BlockSpec(memory_space=pltpu.SMEM)
LOG2E = 1.4426950408889634
VMEM_LIMIT = 56 * 1024 * 1024
BF16 = jnp.bfloat16
F32 = jnp.float32


class Spot:
    def __init__(self, a, b, zl, zh, core):
        self.a, self.b, self.zl, self.zh, self.core = a, b, zl, zh, core

    def move(self, a=None, b=None, zl=None, zh=None):
        return Spot(
            self.a if a is None else a,
            self.b if b is None else b,
            self.zl if zl is None else zl,
            self.zh if zh is None else zh,
            self.core,
        )

    def id(self):
        first = self.core == 0
        x = jnp.where(first, self.a, self.b)
        y = jnp.where(first, self.b, self.a)
        return (self.zl * 16 + y * 4 + x, self.zh * 2 + self.core)

    def sibling(self):
        return Spot(self.b, self.a, self.zl, self.zh, 1 - self.core)

    def across(self):
        return self.move(zl=1 - self.zl, zh=1 - self.zh)


def here():
    ctx = lax.axis_index("ctx")
    fsdp = lax.axis_index("fsdp")
    x = lax.rem(ctx, 4)
    y = lax.rem(ctx // 4, 4)
    core = lax.rem(fsdp, 2)
    first = core == 0
    return Spot(jnp.where(first, x, y), jnp.where(first, y, x), ctx // 16, fsdp // 2, core)


def ring(position, step):
    return lax.rem(position + step + 4, 4)


def greet(spots):
    barrier = pltpu.get_barrier_semaphore()
    for spot in spots:
        pl.semaphore_signal(barrier, inc=1, device_id=spot.id(), device_id_type=MESH)
    pl.semaphore_wait(barrier, len(spots))


def remote(src, dst, send_sem, recv_sem, spot):
    return pltpu.make_async_remote_copy(
        src_ref=src,
        dst_ref=dst,
        send_sem=send_sem,
        recv_sem=recv_sem,
        device_id=spot.id(),
        device_id_type=MESH,
    )


def comm_params(collective_id):
    return pltpu.CompilerParams(
        collective_id=collective_id, has_side_effects=True, vmem_limit_bytes=VMEM_LIMIT
    )


def gather_body(count, *refs):
    ins, outs = refs[:count], refs[count : 2 * count]
    send, recv, local_sem = refs[2 * count :]
    me = here()
    mine = me.zh * 2 + me.core
    other = (1 - me.zh) * 2 + me.core
    twin_mine = me.zh * 2 + 1 - me.core
    twin_other = (1 - me.zh) * 2 + 1 - me.core
    twin, across = me.sibling(), me.across()
    a_next, a_prev = me.move(a=ring(me.a, 1)), me.move(a=ring(me.a, -1))
    b_next, b_prev = me.move(b=ring(me.b, 1)), me.move(b=ring(me.b, -1))
    greet([twin, across, a_next, a_prev, b_next, b_prev])
    sent = []

    def piece(m, a, half=None):
        rows = pl.ds(pl.multiple_of((me.b * 4 + a) * 16, 16), 16)
        return cut(m, rows, half)

    def block(m, b, half=None):
        rows = pl.ds(pl.multiple_of(b * 64, 64), 64)
        return cut(m, rows, half)

    def cut(m, rows, half):
        width = ins[m].shape[1] // 2
        if half is None:
            return outs[m].at[other, rows]
        return outs[m].at[other, rows, pl.ds(half * width, width)]

    def push(m, slot, src, dst, spot):
        copy = remote(src, dst, send.at[m, slot], recv.at[m, slot], spot)
        copy.start()
        sent.append(copy)

    def await_in(m, slot, dst):
        remote(dst, dst, send.at[m, slot], recv.at[m, slot], twin).wait_recv()

    for m in range(count):
        rows = pl.ds(pl.multiple_of((me.b * 4 + me.a) * 16, 16), 16)
        push(m, 0, ins[m].at[rows], outs[m].at[mine, rows], across)
    locals_ = []
    for m in range(count):
        push(m, 9, ins[m], outs[m].at[mine], twin)
        copy = pltpu.make_async_copy(ins[m], outs[m].at[mine], local_sem.at[m])
        copy.start()
        locals_.append(copy)
    for m in range(count):
        await_in(m, 0, piece(m, me.a))
        push(m, 1, piece(m, me.a), piece(m, me.a), a_next)
        push(m, 2, piece(m, me.a), piece(m, me.a), a_prev)

    def stage_a(m):
        left, right, far = ring(me.a, -1), ring(me.a, 1), ring(me.a, 2)
        await_in(m, 1, piece(m, left))
        push(m, 3, piece(m, left, 0), piece(m, left, 0), a_next)
        await_in(m, 2, piece(m, right))
        push(m, 4, piece(m, right, 1), piece(m, right, 1), a_prev)

    def stage_b(m):
        far = ring(me.a, 2)
        await_in(m, 3, piece(m, far, 0))
        await_in(m, 4, piece(m, far, 1))
        push(m, 5, block(m, me.b), block(m, me.b), b_next)
        push(m, 6, block(m, me.b), block(m, me.b), b_prev)
        push(m, 10, block(m, me.b), block(m, me.b), twin)

    def stage_c(m):
        left, right = ring(me.b, -1), ring(me.b, 1)
        await_in(m, 5, block(m, left))
        push(m, 7, block(m, left, 0), block(m, left, 0), b_next)
        push(m, 11, block(m, left), block(m, left), twin)
        await_in(m, 6, block(m, right))
        push(m, 8, block(m, right, 1), block(m, right, 1), b_prev)
        push(m, 12, block(m, right), block(m, right), twin)

    def stage_d(m):
        far = ring(me.b, 2)
        await_in(m, 7, block(m, far, 0))
        await_in(m, 8, block(m, far, 1))
        push(m, 13, block(m, far), block(m, far), twin)

    stages = (stage_a, stage_b, stage_c, stage_d)
    for step in range(count + len(stages) - 1):
        for depth, stage in enumerate(stages):
            if 0 <= step - depth < count:
                stage(step - depth)

    def twin_block(m, b):
        return outs[m].at[twin_other, pl.ds(pl.multiple_of(b * 64, 64), 64)]

    for m in range(count):
        await_in(m, 9, outs[m].at[twin_mine])
        for slot, step in ((10, 0), (11, -1), (12, 1), (13, 2)):
            await_in(m, slot, twin_block(m, ring(me.a, step)))
    for copy in locals_:
        copy.wait()
    for copy in sent:
        copy.wait_send()


def gather_weights(weights):
    count = len(weights)
    outs = pl.pallas_call(
        functools.partial(gather_body, count),
        out_shape=[jax.ShapeDtypeStruct((4,) + w.shape, w.dtype) for w in weights],
        in_specs=[HBM] * count,
        out_specs=[HBM] * count,
        scratch_shapes=[
            pltpu.SemaphoreType.DMA((count, 14)),
            pltpu.SemaphoreType.DMA((count, 14)),
            pltpu.SemaphoreType.DMA((count,)),
        ],
        compiler_params=comm_params(1),
        name="weight_gather",
    )(*weights)
    return [out.reshape(4 * out.shape[1], out.shape[2]) for out in outs]


def group_spot(me, head):
    return me.move(a=lax.rem(head, 4), zl=head // 4)


def swap_body(src, dst, send, recv, local_sem):
    me = here()
    head = me.a + 4 * me.zl
    peers = [lax.rem(head + k, 8) for k in range(1, 8)]
    greet([group_spot(me, peer) for peer in peers])
    own = pltpu.make_async_copy(src.at[head], dst.at[head], local_sem)
    own.start()
    copies = []
    for k, peer in enumerate(peers):
        copy = remote(src.at[peer], dst.at[head], send.at[k], recv.at[k], group_spot(me, peer))
        copy.start()
        copies.append(copy)
    own.wait()
    for k in range(7):
        origin = lax.rem(head + 7 - k, 8)
        remote(src.at[head], dst.at[origin], send.at[k], recv.at[k], group_spot(me, origin)).wait_recv()
    for copy in copies:
        copy.wait_send()


def swap_heads(parts, collective_id):
    return pl.pallas_call(
        swap_body,
        out_shape=jax.ShapeDtypeStruct(parts.shape, parts.dtype),
        in_specs=[HBM],
        out_specs=HBM,
        scratch_shapes=[
            pltpu.SemaphoreType.DMA((7,)),
            pltpu.SemaphoreType.DMA((7,)),
            pltpu.SemaphoreType.DMA,
        ],
        compiler_params=comm_params(collective_id),
        name="head_swap",
    )(parts)


def spread_body(src, rows_out, kv_out, send, recv, kv_send, kv_recv, local_sem):
    me = here()
    head = me.a + 4 * me.zl
    peers = [lax.rem(head + k, 8) for k in range(1, 8)]
    others = [me.move(b=ring(me.b, d)) for d in (1, 2, 3)]
    greet([group_spot(me, peer) for peer in peers] + others)
    sent = []
    for k, peer in enumerate(peers):
        copy = remote(src.at[peer], rows_out.at[head], send.at[k], recv.at[k], group_spot(me, peer))
        copy.start()
        sent.append(copy)
    own = pltpu.make_async_copy(src.at[head], rows_out.at[head], local_sem.at[8])
    own.start()
    locals_ = [own]

    def kv_part(ref):
        return ref.at[:, pl.ds(256, 256)]

    def pass_on(slot, origin, part):
        keep = pltpu.make_async_copy(part, kv_out.at[me.b, origin], local_sem.at[slot])
        keep.start()
        locals_.append(keep)
        for d in range(3):
            copy = remote(
                part, kv_out.at[me.b, origin], kv_send.at[slot, d], kv_recv.at[slot, d], others[d]
            )
            copy.start()
            sent.append(copy)

    pass_on(7, head, kv_part(src.at[head]))
    for k in range(7):
        origin = lax.rem(head + 7 - k, 8)
        remote(
            src.at[head], rows_out.at[origin], send.at[k], recv.at[k], group_spot(me, origin)
        ).wait_recv()
        pass_on(k, origin, kv_part(rows_out.at[origin]))
    for slot in (7, 0, 1, 2, 3, 4, 5, 6):
        origin = head if slot == 7 else lax.rem(head + 7 - slot, 8)
        for d in range(3):
            land = kv_out.at[ring(me.b, -d - 1), origin]
            remote(land, land, kv_send.at[slot, d], kv_recv.at[slot, d], others[d]).wait_recv()
    for copy in locals_:
        copy.wait()
    for copy in sent:
        copy.wait_send()


def spread_rows(parts):
    return pl.pallas_call(
        spread_body,
        out_shape=[
            jax.ShapeDtypeStruct((8, 128, 512), BF16),
            jax.ShapeDtypeStruct((4, 8, 128, 256), BF16),
        ],
        in_specs=[HBM],
        out_specs=[HBM, HBM],
        scratch_shapes=[
            pltpu.SemaphoreType.DMA((7,)),
            pltpu.SemaphoreType.DMA((7,)),
            pltpu.SemaphoreType.DMA((8, 3)),
            pltpu.SemaphoreType.DMA((8, 3)),
            pltpu.SemaphoreType.DMA((9,)),
        ],
        compiler_params=comm_params(2),
        name="qkv_spread",
    )(parts)


def collect_body(dq, dkv, dq_out, dkv_out, held, own, total, q_send, q_recv, p_send, p_recv, t_send, t_recv, local_sem):
    me = here()
    head = me.a + 4 * me.zl
    peers = [lax.rem(head + k, 8) for k in range(1, 8)]
    others = [me.move(b=ring(me.b, d)) for d in (1, 2, 3)]
    greet([group_spot(me, peer) for peer in peers] + others)
    load = pltpu.make_async_copy(dkv.at[me.b], own, local_sem.at[0])
    load.start()
    order = [lax.rem(head + k, 8) for k in (1, 2, 3, 4, 5, 6, 7, 0)]
    sent = []
    for k, peer in enumerate(order):
        for d in range(3):
            copy = remote(
                dkv.at[ring(me.b, d + 1), peer], held.at[d, peer], p_send.at[k, d], p_recv.at[k, d], others[d]
            )
            copy.start()
            sent.append(copy)
    keep = pltpu.make_async_copy(dq.at[head], dq_out.at[head], local_sem.at[1])
    keep.start()
    for k, peer in enumerate(peers):
        copy = remote(dq.at[peer], dq_out.at[head], q_send.at[k], q_recv.at[k], group_spot(me, peer))
        copy.start()
        sent.append(copy)
    load.wait()
    for k, peer in enumerate(order):
        for d in range(3):
            land = held.at[d, peer]
            remote(land, land, p_send.at[k, d], p_recv.at[k, d], others[d]).wait_recv()
        total[peer] = (
            own[peer].astype(F32)
            + held[0, peer].astype(F32)
            + held[1, peer].astype(F32)
            + held[2, peer].astype(F32)
        ).astype(BF16)
        if k < 7:
            copy = remote(total.at[peer], dkv_out.at[head], t_send.at[k], t_recv.at[k], group_spot(me, peer))
            copy.start()
            sent.append(copy)
    mine = pltpu.make_async_copy(total.at[head], dkv_out.at[head], local_sem.at[2])
    mine.start()
    keep.wait()
    mine.wait()
    for k in range(7):
        origin = lax.rem(head + 7 - k, 8)
        remote(dq.at[head], dq_out.at[origin], q_send.at[k], q_recv.at[k], group_spot(me, origin)).wait_recv()
        remote(total.at[head], dkv_out.at[origin], t_send.at[k], t_recv.at[k], group_spot(me, origin)).wait_recv()
    for copy in sent:
        copy.wait_send()


def collect_rows(dq, dkv):
    dma = pltpu.SemaphoreType.DMA
    return pl.pallas_call(
        collect_body,
        out_shape=[
            jax.ShapeDtypeStruct((8, 128, 256), BF16),
            jax.ShapeDtypeStruct((8, 128, 256), BF16),
        ],
        in_specs=[HBM, HBM],
        out_specs=[HBM, HBM],
        scratch_shapes=[
            pltpu.VMEM((3, 8, 128, 256), BF16),
            pltpu.VMEM((8, 128, 256), BF16),
            pltpu.VMEM((8, 128, 256), BF16),
            dma((7,)),
            dma((7,)),
            dma((8, 3)),
            dma((8, 3)),
            dma((7,)),
            dma((7,)),
            dma((3,)),
        ],
        compiler_params=comm_params(3),
        name="qkv_collect",
    )(dq, dkv)


TILE = 512
TILE_BLOCKS = TILE // 64


def dot_nt(left, right):
    return lax.dot_general(left, right, (((1,), (1,)), ((), ())), preferred_element_type=F32)


def dot_nn(left, right):
    return lax.dot_general(left, right, (((1,), (0,)), ((), ())), preferred_element_type=F32)


def stack_heads(rows):
    return jnp.concatenate(
        [rows[:64, :128], rows[:64, 128:256], rows[64:, :128], rows[64:, 128:256]], axis=0
    )


def unstack_heads(stacked):
    return jnp.concatenate(
        [
            jnp.concatenate([stacked[:64], stacked[64:128]], axis=1),
            jnp.concatenate([stacked[128:192], stacked[192:]], axis=1),
        ],
        axis=0,
    )


def sort_rows(order, kv, keys, values):
    @pl.loop(0, 32)
    def _(i):
        low = order[i]
        j, s = i // 8, lax.rem(i, 8)
        rows = kv[j, s]
        at_low = pl.ds(pl.multiple_of(low * 64, 64), 64)
        at_high = pl.ds(pl.multiple_of((63 - low) * 64, 64), 64)
        keys[at_low, :] = rows[:64, :128]
        keys[at_high, :] = rows[64:, :128]
        values[at_low, :] = rows[:64, 128:]
        values[at_high, :] = rows[64:, 128:]


def query_limits(low, columns, start):
    column = lax.broadcasted_iota(jnp.int32, (1, columns), 1) + start
    block = jnp.where(column < 128, low, 63 - low)
    return block * 64 + lax.rem(column, 64)


def mix_body(order, own_order, rows, kv, out, mixed_t, log_total, keys, values, values_t, acc, total):
    sort_rows(order, kv, keys, values)

    @pl.loop(0, 4096 // TILE)
    def _(t):
        at = pl.ds(pl.multiple_of(t * TILE, TILE), TILE)
        values_t[t] = values[at, :].T

    scale = LOG2E * 128.0**-0.5

    @pl.loop(0, 8)
    def _(s):
        low = own_order[s]
        queries = stack_heads(rows[s, :, :256])
        acc[...] = jnp.zeros_like(acc)
        total[...] = jnp.zeros_like(total)

        def tile_step(t, start):
            width = 256 - start
            at = pl.ds(pl.multiple_of(t * TILE, TILE), TILE)
            scores = dot_nt(keys[at, :], queries[start:])
            key_pos = lax.broadcasted_iota(jnp.int32, (TILE, width), 0)
            allowed = key_pos <= query_limits(low, width, start) - t * TILE
            probs = jnp.where(allowed, jnp.exp2(scores * scale), 0.0)
            total[:, start:] += jnp.sum(probs.reshape(TILE // 8, 8, width), axis=0)
            acc[:, start:] += dot_nn(values_t[t], probs.astype(BF16))

        split = low // TILE_BLOCKS + 1
        end = (63 - low) // TILE_BLOCKS + 1

        @pl.loop(0, split)
        def _(t):
            tile_step(t, 0)

        @pl.loop(split, end)
        def _(t):
            tile_step(t, 128)

        full = jnp.sum(total[...], axis=0, keepdims=True)
        mixed = acc[...] / full
        mixed_t[s] = mixed
        log_total[s] = jnp.broadcast_to(jnp.log2(full), (8, 256))
        out[s] = unstack_heads(mixed.T).astype(BF16)


def attention_mix(order, own_order, rows, kv):
    return pl.pallas_call(
        mix_body,
        out_shape=[
            jax.ShapeDtypeStruct((8, 128, 256), BF16),
            jax.ShapeDtypeStruct((8, 128, 256), F32),
            jax.ShapeDtypeStruct((8, 8, 256), F32),
        ],
        in_specs=[SMEM, SMEM, VMEM, VMEM],
        out_specs=[VMEM, VMEM, VMEM],
        scratch_shapes=[
            pltpu.VMEM((4096, 128), BF16),
            pltpu.VMEM((4096, 128), BF16),
            pltpu.VMEM((4096 // TILE, 128, TILE), BF16),
            pltpu.VMEM((128, 256), F32),
            pltpu.VMEM((8, 256), F32),
        ],
        compiler_params=pltpu.CompilerParams(vmem_limit_bytes=VMEM_LIMIT),
        name="attention_mix",
    )(order, own_order, rows, kv)


def grad_body(
    order, own_order, rows, kv, mixed_t, log_total, cots, dq, dkv,
    keys, values, keys_t, key_grad, value_grad, acc,
):
    sort_rows(order, kv, keys, values)

    @pl.loop(0, 4096 // TILE)
    def _(t):
        at = pl.ds(pl.multiple_of(t * TILE, TILE), TILE)
        keys_t[t] = keys[at, :].T

    key_grad[...] = jnp.zeros_like(key_grad)
    value_grad[...] = jnp.zeros_like(value_grad)
    scale = LOG2E * 128.0**-0.5

    @pl.loop(0, 8)
    def _(s):
        low = own_order[s]
        queries = stack_heads(rows[s, :, :256])
        cot = stack_heads(cots[s])
        delta = jnp.sum(cot.astype(F32).T * mixed_t[s], axis=0, keepdims=True)
        logs = log_total[s, 0:1, :]
        acc[...] = jnp.zeros_like(acc)

        def tile_step(t, start):
            width = 256 - start
            at = pl.ds(pl.multiple_of(t * TILE, TILE), TILE)
            scores = dot_nt(keys[at, :], queries[start:])
            prob_cot = dot_nt(values[at, :], cot[start:])
            key_pos = lax.broadcasted_iota(jnp.int32, (TILE, width), 0)
            allowed = key_pos <= query_limits(low, width, start) - t * TILE
            probs = jnp.where(allowed, jnp.exp2(scores * scale - logs[:, start:]), 0.0)
            score_cot = (probs * (prob_cot - delta[:, start:])).astype(BF16)
            value_grad[at, :] += dot_nn(probs.astype(BF16), cot[start:])
            key_grad[at, :] += dot_nn(score_cot, queries[start:])
            acc[:, start:] += dot_nn(keys_t[t], score_cot)

        split = low // TILE_BLOCKS + 1
        end = (63 - low) // TILE_BLOCKS + 1

        @pl.loop(0, split)
        def _(t):
            tile_step(t, 0)

        @pl.loop(split, end)
        def _(t):
            tile_step(t, 128)

        dq[s] = unstack_heads((acc[...] * 128.0**-0.5).T).astype(BF16)

    @pl.loop(0, 32)
    def _(i):
        low = order[i]
        j, s = i // 8, lax.rem(i, 8)
        for first, block in ((0, low), (64, 63 - low)):
            at = pl.ds(pl.multiple_of(block * 64, 64), 64)
            dkv[j, s, pl.ds(first, 64), 0:128] = (key_grad[at, :] * 128.0**-0.5).astype(BF16)
            dkv[j, s, pl.ds(first, 64), 128:256] = value_grad[at, :].astype(BF16)


def attention_grad(order, own_order, rows, kv, mixed_t, log_total, cots):
    return pl.pallas_call(
        grad_body,
        out_shape=[
            jax.ShapeDtypeStruct((8, 128, 256), BF16),
            jax.ShapeDtypeStruct((4, 8, 128, 256), BF16),
        ],
        in_specs=[SMEM, SMEM] + [VMEM] * 5,
        out_specs=[VMEM, VMEM],
        scratch_shapes=[
            pltpu.VMEM((4096, 128), BF16),
            pltpu.VMEM((4096, 128), BF16),
            pltpu.VMEM((4096 // TILE, 128, TILE), BF16),
            pltpu.VMEM((4096, 128), F32),
            pltpu.VMEM((4096, 128), F32),
            pltpu.VMEM((128, 256), F32),
        ],
        compiler_params=pltpu.CompilerParams(vmem_limit_bytes=VMEM_LIMIT),
        name="attention_grad",
    )(order, own_order, rows, kv, mixed_t, log_total, cots)


def reduce_body(chunks, count, *refs):
    ins, gains = refs[:count], refs[count]
    outs, gains_out = refs[count + 1 : 2 * count + 1], refs[2 * count + 1]
    scratch = refs[2 * count + 2 :]
    per_chunk = 15
    send, recv, load, gain_slots, gain_send, gain_recv = scratch[per_chunk * len(chunks) :]
    me = here()
    twin, across = me.sibling(), me.across()
    a_next, a_prev = me.move(a=ring(me.a, 1)), me.move(a=ring(me.a, -1))
    b_next, b_prev = me.move(b=ring(me.b, 1)), me.move(b=ring(me.b, -1))
    z_low = me.move(zl=1 - me.zl)
    a_far, b_far = me.move(a=ring(me.a, 2)), me.move(b=ring(me.b, 2))
    z_high = me.move(zh=1 - me.zh)
    greet([twin, across, a_next, a_prev, b_next, b_prev, z_low, a_far, b_far, z_high])
    sent = []

    def push(k, slot, src, dst, spot):
        copy = remote(src, dst, send.at[k, slot], recv.at[k, slot], spot)
        copy.start()
        sent.append(copy)

    def await_in(k, slot, dst):
        remote(dst, dst, send.at[k, slot], recv.at[k, slot], twin).wait_recv()

    def names(k):
        which, start, width = chunks[k]
        return ins[which], outs[which], start, width, scratch[per_chunk * k : per_chunk * (k + 1)]

    def big(ref, start, width, b, half=None):
        rows = pl.ds(pl.multiple_of(b * 64, 64), 64)
        if half is None:
            return ref.at[:, rows, pl.ds(start, width)]
        return ref.at[:, rows, pl.ds(start + half * (width // 2), width // 2)]

    def small(ref, width, a, half=None):
        rows = pl.ds(pl.multiple_of(a * 16, 16), 16)
        if half is None:
            return ref.at[:, rows]
        return ref.at[:, rows, pl.ds(half * (width // 2), width // 2)]

    def add_rows(dst, sources, rows):
        for zh in range(2):

            @pl.loop(0, rows // 16)
            def _(r):
                at = pl.ds(pl.multiple_of(r * 16, 16), 16)
                total = sources[0][zh, at].astype(F32)
                for source in sources[1:]:
                    total = total + source[zh, at].astype(F32)
                dst[zh, at] = total.astype(BF16)

    loads = {}

    def step0(k):
        src, _, start, width, bufs = names(k)
        far_a, far_b, in_a, in_b, own_a, own_b, own, sum1 = bufs[:8]
        left, right, far = ring(me.b, -1), ring(me.b, 1), ring(me.b, 2)
        half = width // 2
        push(k, 0, big(src, start, width, far, 0), far_a, b_next)
        push(k, 1, big(src, start, width, far, 1), far_b, b_prev)
        push(k, 2, big(src, start, width, right, 1), in_a.at[:, :, pl.ds(half, half)], b_next)
        push(k, 3, big(src, start, width, left, 0), in_b.at[:, :, pl.ds(0, half)], b_prev)
        items = (
            (big(src, start, width, right, 0), own_a),
            (big(src, start, width, left, 1), own_b),
            (big(src, start, width, me.b), own),
        )
        for i, (source, target) in enumerate(items):
            copy = pltpu.make_async_copy(source, target, load.at[k, i])
            copy.start()
            loads[k, i] = copy

    def step1(k):
        _, _, _, width, bufs = names(k)
        far_a, far_b, in_a, in_b, own_a, own_b, own, sum1 = bufs[:8]
        half = width // 2
        await_in(k, 0, far_a)
        loads[k, 0].wait()
        add_rows(own_a, [own_a, far_a], 64)
        push(k, 4, own_a, in_a.at[:, :, pl.ds(0, half)], b_next)
        await_in(k, 1, far_b)
        loads[k, 1].wait()
        add_rows(own_b, [own_b, far_b], 64)
        push(k, 5, own_b, in_b.at[:, :, pl.ds(half, half)], b_prev)

    def step2(k):
        _, _, _, width, bufs = names(k)
        far_a, far_b, in_a, in_b, own_a, own_b, own, sum1 = bufs[:8]
        far2_a, far2_b, in2_a, in2_b = bufs[8:12]
        half = width // 2
        loads[k, 2].wait()
        await_in(k, 2, in_a.at[:, :, pl.ds(half, half)])
        await_in(k, 4, in_a.at[:, :, pl.ds(0, half)])
        await_in(k, 3, in_b.at[:, :, pl.ds(0, half)])
        await_in(k, 5, in_b.at[:, :, pl.ds(half, half)])
        add_rows(sum1, [own, in_a, in_b], 64)
        left, right, far = ring(me.a, -1), ring(me.a, 1), ring(me.a, 2)
        push(k, 6, small(sum1, width, far, 0), far2_a, a_next)
        push(k, 7, small(sum1, width, far, 1), far2_b, a_prev)
        push(k, 8, small(sum1, width, right, 1), in2_a.at[:, :, pl.ds(half, half)], a_next)
        push(k, 9, small(sum1, width, left, 0), in2_b.at[:, :, pl.ds(0, half)], a_prev)

    def step3(k):
        _, _, _, width, bufs = names(k)
        sum1 = bufs[7]
        far2_a, far2_b, in2_a, in2_b, sum2, from_z, from_low = bufs[8:]
        left, right = ring(me.a, -1), ring(me.a, 1)
        half = width // 2
        await_in(k, 6, far2_a)
        far2_a[...] = (
            far2_a[...].astype(F32)
            + sum1[:, pl.ds(pl.multiple_of(right * 16, 16), 16), pl.ds(0, half)].astype(F32)
        ).astype(BF16)
        push(k, 10, far2_a, in2_a.at[:, :, pl.ds(0, half)], a_next)
        await_in(k, 7, far2_b)
        far2_b[...] = (
            far2_b[...].astype(F32)
            + sum1[:, pl.ds(pl.multiple_of(left * 16, 16), 16), pl.ds(half, half)].astype(F32)
        ).astype(BF16)
        push(k, 11, far2_b, in2_b.at[:, :, pl.ds(half, half)], a_prev)

    def step4(k):
        _, _, _, width, bufs = names(k)
        sum1 = bufs[7]
        far2_a, far2_b, in2_a, in2_b, sum2, from_z, from_low = bufs[8:]
        half = width // 2
        await_in(k, 8, in2_a.at[:, :, pl.ds(half, half)])
        await_in(k, 10, in2_a.at[:, :, pl.ds(0, half)])
        await_in(k, 9, in2_b.at[:, :, pl.ds(0, half)])
        await_in(k, 11, in2_b.at[:, :, pl.ds(half, half)])
        sum2[...] = (
            sum1[:, pl.ds(pl.multiple_of(me.a * 16, 16), 16), :].astype(F32)
            + in2_a[...].astype(F32)
            + in2_b[...].astype(F32)
        ).astype(BF16)
        push(k, 12, sum2.at[1 - me.zh], from_z, across)

    def step5(k):
        _, _, _, width, bufs = names(k)
        far2_a, far2_b, in2_a, in2_b, sum2, from_z, from_low = bufs[8:]
        await_in(k, 12, from_z)
        from_z[...] = (from_z[...].astype(F32) + sum2[me.zh].astype(F32)).astype(BF16)
        push(k, 13, from_z, from_low, z_low)

    def out_cut(ref, start, width, row, rows, half=None):
        at = pl.ds(pl.multiple_of(row, 16), rows)
        if half is None:
            return ref.at[at, pl.ds(start, width)]
        return ref.at[at, pl.ds(start + half * (width // 2), width // 2)]

    def step6(k):
        _, out, start, width, bufs = names(k)
        far2_a, far2_b, in2_a, in2_b, sum2, from_z, from_low = bufs[8:]
        await_in(k, 13, from_low)
        final = in2_a.at[0]
        final[...] = (from_z[...].astype(F32) + from_low[...].astype(F32)).astype(BF16)
        row = (me.b * 4 + me.a) * 16
        place = out_cut(out, start, width, row, 16)
        push(k, 14, final, place, a_next)
        push(k, 15, final, place, a_prev)
        copy = pltpu.make_async_copy(final, place, load.at[k, 3])
        copy.start()
        loads[k, 3] = copy

    def step7(k):
        _, out, start, width, _ = names(k)
        left, right = ring(me.a, -1), ring(me.a, 1)
        row_l, row_r = (me.b * 4 + left) * 16, (me.b * 4 + right) * 16
        await_in(k, 14, out_cut(out, start, width, row_l, 16))
        push(k, 16, out_cut(out, start, width, row_l, 16, 0), out_cut(out, start, width, row_l, 16, 0), a_next)
        await_in(k, 15, out_cut(out, start, width, row_r, 16))
        push(k, 17, out_cut(out, start, width, row_r, 16, 1), out_cut(out, start, width, row_r, 16, 1), a_prev)

    def step8(k):
        _, out, start, width, _ = names(k)
        row_f = (me.b * 4 + ring(me.a, 2)) * 16
        await_in(k, 16, out_cut(out, start, width, row_f, 16, 0))
        await_in(k, 17, out_cut(out, start, width, row_f, 16, 1))
        loads[k, 3].wait()
        mine = out_cut(out, start, width, me.b * 64, 64)
        push(k, 18, mine, mine, b_next)
        push(k, 19, mine, mine, b_prev)

    def step9(k):
        _, out, start, width, _ = names(k)
        row_l, row_r = ring(me.b, -1) * 64, ring(me.b, 1) * 64
        await_in(k, 18, out_cut(out, start, width, row_l, 64))
        push(k, 20, out_cut(out, start, width, row_l, 64, 0), out_cut(out, start, width, row_l, 64, 0), b_next)
        await_in(k, 19, out_cut(out, start, width, row_r, 64))
        push(k, 21, out_cut(out, start, width, row_r, 64, 1), out_cut(out, start, width, row_r, 64, 1), b_prev)

    def step10(k):
        _, out, start, width, _ = names(k)
        row_f = ring(me.b, 2) * 64
        await_in(k, 20, out_cut(out, start, width, row_f, 64, 0))
        await_in(k, 21, out_cut(out, start, width, row_f, 64, 1))

    gain_copies = []
    x_ring = [(me.move(a=ring(me.a, d)), me.move(b=ring(me.b, d))) for d in (1, 2, 3)]
    first = me.core == 0
    x, y = jnp.where(first, me.a, me.b), jnp.where(first, me.b, me.a)
    z = me.zh * 2 + me.zl

    def pick(d, on_x):
        along_a, along_b = x_ring[d - 1]
        use_a = first if on_x else jnp.logical_not(first)
        return Spot(
            jnp.where(use_a, along_a.a, along_b.a),
            jnp.where(use_a, along_a.b, along_b.b),
            me.zl, me.zh, me.core,
        )

    def z_spot(d):
        far = lax.rem(z + d, 4)
        return me.move(zl=lax.rem(far, 2), zh=far // 2)

    def gain_push(stage, slot, position, spots):
        for d, spot in enumerate(spots):
            copy = remote(
                gain_slots.at[stage, position], gain_slots.at[stage, position],
                gain_send.at[stage, d], gain_recv.at[stage, d], spot,
            )
            copy.start()
            gain_copies.append(copy)

    def gain_wait(stage, position, size):
        for d in range(size - 1):
            land = gain_slots.at[stage, lax.rem(position + size - 1 - d, size)]
            remote(land, land, gain_send.at[stage, d], gain_recv.at[stage, d], twin).wait_recv()

    def gain0():
        gain_slots[0, me.core] = gains[...]
        gain_push(0, 0, me.core, [twin])

    def gain1():
        gain_wait(0, me.core, 2)
        gain_slots[1, x] = gain_slots[0, 0] + gain_slots[0, 1]
        gain_push(1, 0, x, [pick(d, True) for d in (1, 2, 3)])

    def gain_sum(stage):
        return (gain_slots[stage, 0] + gain_slots[stage, 1]) + (gain_slots[stage, 2] + gain_slots[stage, 3])

    def gain2():
        gain_wait(1, x, 4)
        gain_slots[2, y] = gain_sum(1)
        gain_push(2, 0, y, [pick(d, False) for d in (1, 2, 3)])

    def gain3():
        gain_wait(2, y, 4)
        gain_slots[3, z] = gain_sum(2)
        gain_push(3, 0, z, [z_spot(d) for d in (1, 2, 3)])

    def gain4():
        gain_wait(3, z, 4)
        gains_out[...] = gain_sum(3)

    steps = (step0, step1, step2, step3, step4, step5, step6, step7, step8, step9, step10)
    gain_steps = {1: gain0, 3: gain1, 5: gain2, 7: gain3, 9: gain4}
    for turn in range(len(chunks) + len(steps) - 1):
        for depth, step in enumerate(steps):
            if 0 <= turn - depth < len(chunks):
                step(turn - depth)
        if turn in gain_steps:
            gain_steps[turn]()
    for copy in sent + gain_copies:
        copy.wait_send()


def reduce_gradients(parts, chunks, gains, collective_id):
    count = len(parts)
    scratch = []
    for _, _, width in chunks:
        half = width // 2
        scratch += [
            pltpu.VMEM((2, 64, half), BF16),
            pltpu.VMEM((2, 64, half), BF16),
            pltpu.VMEM((2, 64, width), BF16),
            pltpu.VMEM((2, 64, width), BF16),
            pltpu.VMEM((2, 64, half), BF16),
            pltpu.VMEM((2, 64, half), BF16),
            pltpu.VMEM((2, 64, width), BF16),
            pltpu.VMEM((2, 64, width), BF16),
            pltpu.VMEM((2, 16, half), BF16),
            pltpu.VMEM((2, 16, half), BF16),
            pltpu.VMEM((2, 16, width), BF16),
            pltpu.VMEM((2, 16, width), BF16),
            pltpu.VMEM((2, 16, width), BF16),
            pltpu.VMEM((16, width), BF16),
            pltpu.VMEM((16, width), BF16),
        ]
    dma = pltpu.SemaphoreType.DMA
    scratch += [
        dma((len(chunks), 22)),
        dma((len(chunks), 22)),
        dma((len(chunks), 4)),
        pltpu.VMEM((4, 4) + gains.shape, F32),
        dma((4, 3)),
        dma((4, 3)),
    ]
    return pl.pallas_call(
        functools.partial(reduce_body, chunks, count),
        out_shape=[jax.ShapeDtypeStruct(part.shape[1:], BF16) for part in parts]
        + [jax.ShapeDtypeStruct(gains.shape, F32)],
        in_specs=[HBM] * count + [VMEM],
        out_specs=[HBM] * count + [VMEM],
        scratch_shapes=scratch,
        compiler_params=comm_params(collective_id),
        name="gradient_reduce",
    )(*parts, gains)


def rms_scale(values):
    return lax.rsqrt(jnp.mean(values * values, axis=-1, keepdims=True) + EPSILON)


def rope_tables(extent, positions):
    frequency = jnp.power(ROPE_BASE, -jnp.arange(0, extent, 2, dtype=F32) / extent)
    angles = positions.astype(F32)[:, None] * frequency[None, :]
    cosine = jnp.concatenate([jnp.cos(angles), jnp.cos(angles)], -1)[:, None, :]
    sine_rows = jnp.concatenate([jnp.sin(angles), jnp.sin(angles)], -1)[:, None, :]
    return cosine, sine_rows


def rotate(values, tables):
    cosine, sine_rows = tables
    half = values.shape[-1] // 2
    turned = jnp.concatenate([-values[..., half:], values[..., :half]], -1)
    return values * cosine + turned * sine_rows


def rotate_back(grads, tables):
    cosine, sine_rows = tables
    half = grads.shape[-1] // 2
    scaled = grads * sine_rows
    return grads * cosine + jnp.concatenate([scaled[..., half:], -scaled[..., :half]], -1)


def norm_back(grad_out, normed, scale_inv):
    return scale_inv * (grad_out - normed * jnp.mean(grad_out * normed, axis=-1, keepdims=True))


def matmul(matrix, second):
    return jnp.dot(matrix, second, preferred_element_type=F32)


def matmul_rows(matrix, second):
    return lax.dot_general(matrix, second, (((1,), (1,)), ((), ())), preferred_element_type=F32)


def twin_swap(value):
    return lax.ppermute(value, "fsdp", [(0, 1), (1, 0), (2, 3), (3, 2)])


def pair_grad(left, right, core):
    tokens = left.shape[0]
    split = left.reshape(tokens, 2, 2, 256)
    keep = lax.dynamic_index_in_dim(split, core, 2, keepdims=False)
    give = lax.dynamic_index_in_dim(split, 1 - core, 2, keepdims=False)
    left_pair = jnp.concatenate([keep, twin_swap(give)], 0).reshape(2 * tokens, 512)
    right_pair = jnp.concatenate([right, twin_swap(right)], 0)
    grad = lax.dot_general(left_pair, right_pair, (((0,), (0,)), ((), ())), preferred_element_type=F32)
    return grad.astype(BF16).reshape(2, 256, right.shape[1])


def shards(
    tokens,
    query_weight,
    key_weight,
    value_weight,
    out_weight,
    gate_weight,
    up_weight,
    down_weight,
    attn_gain,
    mlp_gain,
    query_gain,
    key_gain,
    pair_order,
    out_grad,
):
    inputs = tokens[0].astype(F32)
    rows = inputs.shape[0]
    pair_row = pair_order[0]
    ctx = lax.axis_index("ctx")
    core = lax.rem(lax.axis_index("fsdp"), 2)
    first = lax.dynamic_index_in_dim(pair_row, ctx, 0, keepdims=False)
    inner = jnp.arange(rows, dtype=jnp.int32)
    own_pos = jnp.where(inner < 64, first, 63 - first) * 64 + inner % 64
    tables = rope_tables(128, own_pos)
    spots = pair_row.reshape(2, 4, 4)
    order = jnp.where(core == 0, spots.transpose(1, 0, 2), spots.transpose(2, 0, 1))
    x, y = ctx % 4, (ctx // 4) % 4
    own_order = lax.dynamic_index_in_dim(order, jnp.where(core == 0, y, x), 0, keepdims=False).reshape(8)
    order = order.reshape(32)

    full_query, full_key, full_value, full_out, full_gate, full_up, full_down = gather_weights(
        [query_weight, key_weight, value_weight, out_weight, gate_weight, up_weight, down_weight]
    )
    attn_scale = rms_scale(inputs)
    attn_normed = inputs * attn_scale
    attn_in = (attn_normed * attn_gain).astype(BF16)
    query_raw = matmul(attn_in, full_query).reshape(rows, 16, 128)
    key_raw = matmul(attn_in, full_key).reshape(rows, 8, 128)
    value_rows = matmul(attn_in, full_value).astype(BF16)
    query_inv = rms_scale(query_raw)
    query_hat = query_raw * query_inv
    key_inv = rms_scale(key_raw)
    key_hat = key_raw * key_inv
    query_rot = rotate(query_hat * query_gain, tables).astype(BF16).reshape(rows, 8, 256)
    key_rot = rotate(key_hat * key_gain, tables).astype(BF16)
    packed = jnp.concatenate([query_rot, key_rot, value_rows.reshape(rows, 8, 128)], -1).transpose(1, 0, 2)
    head_rows, head_kv = spread_rows(packed)
    mixed, mixed_t, log_total = attention_mix(order, own_order, head_rows, head_kv)
    attn_out = swap_heads(mixed, 4).transpose(1, 0, 2).reshape(rows, 2048)

    middle = inputs + matmul_rows(attn_out, full_out)
    mlp_scale = rms_scale(middle)
    mlp_normed = middle * mlp_scale
    mlp_in = (mlp_normed * mlp_gain).astype(BF16)
    gate_pre = matmul(mlp_in, full_gate)
    up_pre = matmul(mlp_in, full_up)
    sigmoid_gate = jax.nn.sigmoid(gate_pre)
    silu_gate = gate_pre * sigmoid_gate
    hidden = (silu_gate * up_pre).astype(BF16)
    result = middle + matmul_rows(hidden, full_down)
    down_cot = out_grad[0]
    hidden_cot = matmul(down_cot, full_down)
    gate_cot = (hidden_cot * up_pre * sigmoid_gate * (1.0 + gate_pre * (1.0 - sigmoid_gate))).astype(BF16)
    up_cot = (hidden_cot * silu_gate).astype(BF16)
    mlp_in_cot = matmul_rows(gate_cot, full_gate) + matmul_rows(up_cot, full_up)
    mlp_gain_part = jnp.sum(mlp_in_cot * mlp_normed, axis=0)
    middle_cot = down_cot.astype(F32) + norm_back(mlp_in_cot * mlp_gain, mlp_normed, mlp_scale)
    branch_cot = middle_cot.astype(BF16)
    attended_cot = matmul(branch_cot, full_out).astype(BF16).reshape(rows, 8, 256).transpose(1, 0, 2)
    head_cots = swap_heads(attended_cot, 4)
    dq, dkv = attention_grad(order, own_order, head_rows, head_kv, mixed_t, log_total, head_cots)
    dq, dkv = collect_rows(dq, dkv)
    query_rot_cot = dq.astype(F32).transpose(1, 0, 2).reshape(rows, 16, 128)
    key_value_cot = dkv.transpose(1, 0, 2)
    value_raw_cot = key_value_cot[..., 128:].reshape(rows, 1024)
    key_hat_cot = rotate_back(key_value_cot[..., :128].astype(F32), tables)
    key_gain_part = jnp.sum(key_hat_cot * key_hat, axis=(0, 1))
    key_raw_cot = norm_back(key_hat_cot * key_gain, key_hat, key_inv).astype(BF16).reshape(rows, 1024)
    query_hat_cot = rotate_back(query_rot_cot, tables)
    query_gain_part = jnp.sum(query_hat_cot * query_hat, axis=(0, 1))
    query_raw_cot = norm_back(query_hat_cot * query_gain, query_hat, query_inv).astype(BF16).reshape(rows, 2048)
    attn_in_cot = (
        matmul_rows(query_raw_cot, full_query)
        + matmul_rows(key_raw_cot, full_key)
        + matmul_rows(value_raw_cot, full_value)
    )
    attn_gain_part = jnp.sum(attn_in_cot * attn_normed, axis=0)
    input_cot = middle_cot + norm_back(attn_in_cot * attn_gain, attn_normed, attn_scale)

    grads = [
        pair_grad(mlp_in, jnp.concatenate([gate_cot, up_cot], 1), core),
        pair_grad(down_cot, hidden, core),
        pair_grad(attn_in, jnp.concatenate([query_raw_cot, key_raw_cot, value_raw_cot], 1), core),
        pair_grad(branch_cot, attn_out, core),
    ]
    gains = jnp.concatenate(
        [attn_gain_part, mlp_gain_part, query_gain_part, key_gain_part, jnp.zeros(768, F32)]
    ).reshape(24, 128)
    chunks = ((0, 0, 3072), (0, 3072, 3072), (1, 0, 3072), (2, 0, 4096), (3, 0, 2048))
    gate_up, down, qkv, out, gains = reduce_gradients(grads, chunks, gains, 5)
    gate_up, down, qkv, out = (value.astype(F32) for value in (gate_up, down, qkv, out))
    gains = gains.reshape(-1)
    return (
        result.astype(BF16)[None],
        input_cot[None],
        qkv[:, :2048],
        qkv[:, 2048:3072],
        qkv[:, 3072:],
        out,
        gate_up[:, :3072],
        gate_up[:, 3072:],
        down,
        gains[:1024],
        gains[1024:2048],
        gains[2048:2176],
        gains[2176:2304],
    )


def solution(mesh):
    rows, split, whole = P("fsdp", None), P("fsdp", "ctx", None), P()
    return jax.shard_map(
        shards,
        mesh=mesh,
        in_specs=(split,) + (rows,) * 7 + (whole,) * 4 + (rows, split),
        out_specs=(split, split) + (rows,) * 7 + (whole,) * 4,
        check_vma=False,
    )
```

```python
import functools

import jax
import jax.numpy as jnp
import numpy as np
from jax import lax
from jax.experimental import pallas as pl
from jax.experimental.pallas import tpu as pltpu
from jax.sharding import PartitionSpec as P

EPSILON = 1e-06
ROPE_BASE = 1000000.0
MESH = pl.DeviceIdType.MESH
HBM = pl.BlockSpec(memory_space=pltpu.HBM)
VMEM = pl.BlockSpec(memory_space=pltpu.VMEM)
SMEM = pl.BlockSpec(memory_space=pltpu.SMEM)
LOG2E = 1.4426950408889634
VMEM_LIMIT = 56 * 1024 * 1024
BF16 = jnp.bfloat16
F32 = jnp.float32


class Spot:
    def __init__(self, a, b, zl, zh, core):
        self.a, self.b, self.zl, self.zh, self.core = a, b, zl, zh, core

    def move(self, a=None, b=None, zl=None, zh=None):
        return Spot(
            self.a if a is None else a,
            self.b if b is None else b,
            self.zl if zl is None else zl,
            self.zh if zh is None else zh,
            self.core,
        )

    def id(self):
        first = self.core == 0
        x = jnp.where(first, self.a, self.b)
        y = jnp.where(first, self.b, self.a)
        return (self.zl * 16 + y * 4 + x, self.zh * 2 + self.core)

    def sibling(self):
        return Spot(self.b, self.a, self.zl, self.zh, 1 - self.core)

    def across(self):
        return self.move(zl=1 - self.zl, zh=1 - self.zh)


def here():
    ctx = lax.axis_index("ctx")
    fsdp = lax.axis_index("fsdp")
    x = lax.rem(ctx, 4)
    y = lax.rem(ctx // 4, 4)
    core = lax.rem(fsdp, 2)
    first = core == 0
    return Spot(jnp.where(first, x, y), jnp.where(first, y, x), ctx // 16, fsdp // 2, core)


def ring(position, step):
    return lax.rem(position + step + 4, 4)


def greet(spots):
    barrier = pltpu.get_barrier_semaphore()
    for spot in spots:
        pl.semaphore_signal(barrier, inc=1, device_id=spot.id(), device_id_type=MESH)
    pl.semaphore_wait(barrier, len(spots))


def remote(src, dst, send_sem, recv_sem, spot):
    return pltpu.make_async_remote_copy(
        src_ref=src,
        dst_ref=dst,
        send_sem=send_sem,
        recv_sem=recv_sem,
        device_id=spot.id(),
        device_id_type=MESH,
    )


def comm_params(collective_id):
    return pltpu.CompilerParams(
        collective_id=collective_id, has_side_effects=True, vmem_limit_bytes=VMEM_LIMIT
    )


class Wire:
    def __init__(self, send, recv, spot):
        self.send, self.recv, self.spot, self.sent = send, recv, spot, []

    def push(self, slot, src, dst, spot):
        copy = remote(src, dst, self.send.at[slot], self.recv.at[slot], spot)
        copy.start()
        self.sent.append(copy)

    def take(self, slot, dst):
        remote(dst, dst, self.send.at[slot], self.recv.at[slot], self.spot).wait_recv()

    def close(self):
        for copy in self.sent:
            copy.wait_send()


def pipeline(stages, count):
    def turn(t):
        for depth, stage in enumerate(stages):
            if 0 <= t - depth < count:
                stage(t - depth)

    return [functools.partial(turn, t) for t in range(count + len(stages) - 1)]


GATHER_SLOTS = 14


def gather_scratch(weights):
    count = len(weights)
    return [pltpu.VMEM(w.shape, w.dtype) for w in weights] + [
        pltpu.SemaphoreType.DMA((count, GATHER_SLOTS)),
        pltpu.SemaphoreType.DMA((count, GATHER_SLOTS)),
        pltpu.SemaphoreType.DMA((2, count)),
    ]


def gather_turns(me, ins, outs, scratch):
    count = len(ins)
    held, (send, recv, local_sem) = scratch[:count], scratch[count:]
    mine = me.zh * 2 + me.core
    other = (1 - me.zh) * 2 + me.core
    twin_mine = me.zh * 2 + 1 - me.core
    twin_other = (1 - me.zh) * 2 + 1 - me.core
    twin, across = me.sibling(), me.across()
    a_next, a_prev = me.move(a=ring(me.a, 1)), me.move(a=ring(me.a, -1))
    b_next, b_prev = me.move(b=ring(me.b, 1)), me.move(b=ring(me.b, -1))
    wire = Wire(send, recv, twin)

    def cut(m, rows, half):
        width = ins[m].shape[1] // 2
        if half is None:
            return outs[m].at[other, rows]
        return outs[m].at[other, rows, pl.ds(half * width, width)]

    def piece(m, a, half=None):
        return cut(m, pl.ds(pl.multiple_of((me.b * 4 + a) * 16, 16), 16), half)

    def block(m, b, half=None):
        return cut(m, pl.ds(pl.multiple_of(b * 64, 64), 64), half)

    def push(m, slot, src, dst, spot):
        wire.push((m, slot), src, dst, spot)

    def take(m, slot, dst):
        wire.take((m, slot), dst)

    loads = [pltpu.make_async_copy(ins[m], held[m], local_sem.at[0, m]) for m in range(count)]
    stores = [pltpu.make_async_copy(held[m], outs[m].at[mine], local_sem.at[1, m]) for m in range(count)]

    def start():
        for m in range(count):
            rows = pl.ds(pl.multiple_of((me.b * 4 + me.a) * 16, 16), 16)
            push(m, 0, ins[m].at[rows], outs[m].at[mine, rows], across)
        for load in loads:
            load.start()

    def spread_own():
        for m in range(count):
            loads[m].wait()
            stores[m].start()
            push(m, 9, ins[m], outs[m].at[mine], twin)

    def stage_z(m):
        take(m, 0, piece(m, me.a))
        push(m, 1, piece(m, me.a), piece(m, me.a), a_next)
        push(m, 2, piece(m, me.a), piece(m, me.a), a_prev)

    def stage_a(m):
        left, right = ring(me.a, -1), ring(me.a, 1)
        take(m, 1, piece(m, left))
        push(m, 3, piece(m, left, 0), piece(m, left, 0), a_next)
        take(m, 2, piece(m, right))
        push(m, 4, piece(m, right, 1), piece(m, right, 1), a_prev)

    def stage_b(m):
        far = ring(me.a, 2)
        take(m, 3, piece(m, far, 0))
        take(m, 4, piece(m, far, 1))
        push(m, 5, block(m, me.b), block(m, me.b), b_next)
        push(m, 6, block(m, me.b), block(m, me.b), b_prev)
        push(m, 10, block(m, me.b), block(m, me.b), twin)

    def stage_c(m):
        left, right = ring(me.b, -1), ring(me.b, 1)
        take(m, 5, block(m, left))
        push(m, 7, block(m, left, 0), block(m, left, 0), b_next)
        push(m, 11, block(m, left), block(m, left), twin)
        take(m, 6, block(m, right))
        push(m, 8, block(m, right, 1), block(m, right, 1), b_prev)
        push(m, 12, block(m, right), block(m, right), twin)

    def stage_d(m):
        far = ring(me.b, 2)
        take(m, 7, block(m, far, 0))
        take(m, 8, block(m, far, 1))
        push(m, 13, block(m, far), block(m, far), twin)

    def finish():
        for m in range(count):
            take(m, 9, outs[m].at[twin_mine])
            for slot, step in ((10, 0), (11, -1), (12, 1), (13, 2)):
                rows = pl.ds(pl.multiple_of(ring(me.a, step) * 64, 64), 64)
                take(m, slot, outs[m].at[twin_other, rows])
        for store in stores:
            store.wait()
        wire.close()

    turns = pipeline((stage_z, stage_a, stage_b, stage_c, stage_d), count)
    return start, spread_own, turns, finish


def group_spot(me, head):
    return me.move(a=lax.rem(head, 4), zl=head // 4)


def group_head(me):
    return me.a + 4 * me.zl


def peer_of(head, k):
    return lax.rem(head + k, 8)


def group_neighbours(me):
    head = group_head(me)
    return [group_spot(me, peer_of(head, k)) for k in range(1, 8)] + [
        me.move(b=ring(me.b, d)) for d in (1, 2, 3)
    ]


def dma(*shape):
    return pltpu.SemaphoreType.DMA(shape)


TILE = 512
CHUNK = 256
SCORE_SCALE = 128.0**-0.5


def dot_nt(left, right):
    return lax.dot_general(left, right, (((1,), (1,)), ((), ())), preferred_element_type=F32)


def dot_nn(left, right):
    return lax.dot_general(left, right, (((1,), (0,)), ((), ())), preferred_element_type=F32)


def stack_heads(read, target):
    for s in range(8):
        rows = read(s)
        for part in range(2):
            for head in range(2):
                at = part * 1024 + s * 128 + head * 64
                target[at : at + 64, :] = rows[part * 64 : part * 64 + 64, head * 128 : head * 128 + 128]


def unstack_heads(stacked, s, out):
    for part in range(2):
        for head in range(2):
            at = part * 1024 + s * 128 + head * 64
            out[s, part * 64 : part * 64 + 64, head * 128 : head * 128 + 128] = stacked[at : at + 64, :]


def low_block(pair, me, j, s):
    a = lax.rem(s, 4)
    first = me.core == 0
    return pair[0, (s // 4) * 16 + jnp.where(first, j * 4 + a, a * 4 + j)]


def key_positions(pair, me, j, part, target):
    line = lax.broadcasted_iota(jnp.int32, (64, CHUNK), 0)
    for s in range(8):
        low = low_block(pair, me, j, s)
        block = low if part == 0 else 63 - low
        target[s * 64 : s * 64 + 64, :] = line + block * 64


def query_positions(pair, me, target):
    line = lax.rem(lax.broadcasted_iota(jnp.int32, (8, 128), 1), 64)
    for s in range(8):
        low = low_block(pair, me, me.b, s)
        target[:, s * 128 : s * 128 + 128] = line + low * 64
        target[:, 1024 + s * 128 : 1152 + s * 128] = line + (63 - low) * 64


def rope_tables():
    frequency = ROPE_BASE ** (-np.arange(0, 128, 2, dtype=np.float64) / 128)
    frequency = np.concatenate([frequency, frequency])
    sign = np.where(np.arange(128) < 64, -1.0, 1.0)
    inner = np.arange(64, dtype=np.float64)[:, None] * frequency
    outer = inner * 64.0
    make = lambda angles: jnp.asarray(np.stack([np.cos(angles), np.sin(angles) * sign]), F32)
    return make(inner), make(outer)


def rope_rows(inner, outer, low):
    cosines, sines = [], []
    for block in (low, 63 - low):
        cos_b, sin_b = outer[0, pl.ds(block, 1), :], outer[1, pl.ds(block, 1), :]
        cosines.append(cos_b * inner[0] - sin_b * inner[1])
        sines.append(sin_b * inner[0] + cos_b * inner[1])
    return jnp.concatenate(cosines, axis=0), jnp.concatenate(sines, axis=0)


def mean_last(value):
    return jnp.mean(value, axis=-1, keepdims=True)


def norm_scale(value):
    return lax.rsqrt(mean_last(value * value) + EPSILON)


def tile_rows(kv, j, part, start):
    return kv[j, :, part * 64 : part * 64 + 64, start : start + 128].reshape(TILE, 128)


def tile_probs(scores, masked, key_pos, query_pos, columns, shift=None):
    logits = scores * (LOG2E * SCORE_SCALE)
    if shift is not None:
        logits = logits - shift
    probs = jnp.exp2(logits)
    if masked:
        probs = jnp.where(key_pos[...] <= query_pos[0:1, columns], probs, 0.0)
    return probs


def mix_tile(me, j, part, pair, kv, query_pos, queries, key_pos, acc, total):
    key_positions(pair, me, j, part, key_pos)
    keys = tile_rows(kv, j, part, 0)
    values_t = tile_rows(kv, j, part, 128).T
    for chunk in range(4 * part, 8):
        columns = pl.ds(chunk * CHUNK, CHUNK)
        masked = part == 1 or chunk < 4
        probs = tile_probs(dot_nt(keys, queries[columns, :]), masked, key_pos, query_pos, columns)
        total[:, columns] += jnp.sum(probs.reshape(TILE // 8, 8, CHUNK), axis=0)
        acc[:, columns] += dot_nn(values_t, probs.astype(BF16))


def finish_mix(out, mixed_t, log_total, stacked, total):
    for chunk in range(8):
        columns = pl.ds(chunk * CHUNK, CHUNK)
        full = jnp.sum(total[:, columns], axis=0, keepdims=True)
        log_total[:, columns] = jnp.broadcast_to(jnp.log2(full), (8, CHUNK))
        mixed = mixed_t[:, columns] / full
        mixed_t[:, columns] = mixed
        stacked[columns, :] = mixed.T.astype(BF16)
    for s in range(8):
        unstack_heads(stacked, s, out)


def grad_tile(
    me, j, part, pair, kv, query_pos, queries, cots, deltas, log_total, key_pos, probs_all, score_cots, acc, dkv
):
    key_positions(pair, me, j, part, key_pos)
    keys = tile_rows(kv, j, part, 0)
    values = tile_rows(kv, j, part, 128)
    keys_t = keys.T
    for chunk in range(4 * part, 8):
        columns = pl.ds(chunk * CHUNK, CHUNK)
        masked = part == 1 or chunk < 4
        scores = dot_nt(keys, queries[columns, :])
        prob_cot = dot_nt(values, cots[columns, :])
        probs = tile_probs(scores, masked, key_pos, query_pos, columns, log_total[0:1, columns])
        score_cot = (probs * (prob_cot - deltas[0:1, columns])).astype(BF16)
        probs_all[:, columns] = probs.astype(BF16)
        score_cots[:, columns] = score_cot
        acc[:, columns] += dot_nn(keys_t, score_cot)
    first = 1024 * part
    key_cot = dot_nn(score_cots[:, first:], queries[first:, :]) * SCORE_SCALE
    value_cot = dot_nn(probs_all[:, first:], cots[first:, :])
    at = part * 64
    dkv[j, :, at : at + 64, 0:128] = key_cot.astype(BF16).reshape(8, 64, 128)
    dkv[j, :, at : at + 64, 128:256] = value_cot.astype(BF16).reshape(8, 64, 128)


def start_grad(rows, mixed_t, cots_in, queries, cots, deltas, acc):
    stack_heads(lambda s: rows[s, :, :256], queries)
    stack_heads(lambda s: cots_in[s], cots)
    for chunk in range(8):
        columns = pl.ds(chunk * CHUNK, CHUNK)
        product = cots[columns, :].astype(F32).T * mixed_t[:, columns]
        deltas[:, columns] = jnp.broadcast_to(jnp.sum(product, axis=0, keepdims=True), (8, CHUNK))
    acc[...] = jnp.zeros_like(acc)


def head_columns(head):
    return (
        (pl.ds(pl.multiple_of(head * 256, 256), 256), pl.ds(0, 256)),
        (pl.ds(pl.multiple_of(head * 128, 128), 128), pl.ds(256, 128)),
        (pl.ds(pl.multiple_of(head * 128, 128), 128), pl.ds(384, 128)),
    )


def project_rows(s, low, xs, heads_w, inner, outer, query_gain, key_gain, raw, rows):
    product = dot_nn(xs[s], heads_w[...].reshape(1024, 512))
    cosine, sine = rope_rows(inner, outer, low)
    raw[s] = product[:, :384]
    for i, gain in enumerate((query_gain, query_gain, key_gain)):
        value = product[:, i * 128 : i * 128 + 128]
        value = value * norm_scale(value) * gain[...]
        value = value * cosine + pltpu.roll(value, 64, 1) * sine
        rows[s, :, i * 128 : i * 128 + 128] = value.astype(BF16)
    rows[s, :, 384:] = product[:, 384:].astype(BF16)


def forward_body(
    pair, x, attn_gain, query_gain, key_gain, inner, outer, *refs
):
    shards, refs = refs[:7], refs[7:]
    (attn_out, rows, raw, kv, mixed_t, log_total), refs = refs[:6], refs[6:]
    full, refs = refs[:7], refs[7:]
    (
        xs, heads_w, queries, stacked, query_pos, key_pos, total, mixed,
        x_send, x_recv, w_send, w_recv, w_load, kv_send, kv_recv, back_send, back_recv,
    ), scratch = refs[:17], refs[17:]
    me = here()
    head = group_head(me)
    twin, across = me.sibling(), me.across()
    across_twin = across.sibling()
    others = [me.move(b=ring(me.b, d)) for d in (1, 2, 3)]
    along = [me.move(a=ring(me.a, d)) for d in (1, 2, 3)]
    z_low = me.move(zl=1 - me.zl)
    greet([twin, across, across_twin] + group_neighbours(me))
    start, spread_own, turns, finish = gather_turns(me, shards, full, scratch)
    turns = list(turns)

    def step():
        if turns:
            turns.pop(0)()

    x_wire = Wire(x_send, x_recv, twin)
    w_wire = Wire(w_send, w_recv, twin)
    kv_wire = Wire(kv_send, kv_recv, twin)
    back_wire = Wire(back_send, back_recv, twin)
    mine = me.zh * 2 + me.core
    qkv_shards = shards[4:]
    loads = []
    for i, (source, target) in enumerate(head_columns(head)):
        load = pltpu.make_async_copy(qkv_shards[i].at[:, source], heads_w.at[mine, :, target], w_load.at[i])
        load.start()
        loads.append(load)
    for t, spot in enumerate((across, across_twin, twin)):
        for i, (source, target) in enumerate(head_columns(group_head(spot))):
            w_wire.push((t, i), qkv_shards[i].at[:, source], heads_w.at[mine, :, target], spot)
    inputs = x[...].astype(F32)
    xs[head] = (inputs * norm_scale(inputs) * attn_gain[...]).astype(BF16)
    x_wire.push(3, xs.at[head], xs.at[head], z_low)
    for d in (1, 3, 2):
        x_wire.push(d - 1, xs.at[head], xs.at[head], along[d - 1])
    start()
    query_positions(pair, me, query_pos)
    mixed_t[...] = jnp.zeros_like(mixed_t)
    total[...] = jnp.zeros_like(total)
    low_head = me.a + 4 * (1 - me.zl)
    x_wire.take(3, xs.at[low_head])
    for d in (1, 3, 2):
        x_wire.push(3 + d, xs.at[low_head], xs.at[low_head], along[d - 1])
    spread_own()
    for load in loads:
        load.wait()
    for t, f in enumerate(
        ((1 - me.zh) * 2 + me.core, (1 - me.zh) * 2 + 1 - me.core, me.zh * 2 + 1 - me.core)
    ):
        for i, (_, target) in enumerate(head_columns(head)):
            w_wire.take((t, i), heads_w.at[f, :, target])
    arrivals = [(None, head), (None, low_head)]
    for zl, first in ((me.zl, 0), (1 - me.zl, 4)):
        for d in (1, 3, 2):
            arrivals.append((first + d - 1, ring(me.a, -d) + 4 * zl))
    for k, (slot, s) in enumerate(arrivals):
        if slot is not None:
            x_wire.take(slot, xs.at[s])
        project_rows(
            s, low_block(pair, me, me.b, s), xs, heads_w, inner, outer, query_gain, key_gain, raw, rows
        )
        for d in range(3):
            kv_wire.push((k, d), rows.at[s, :, pl.ds(256, 256)], kv.at[me.b, s], others[d])
        kv[me.b, s] = rows[s, :, 256:]
        step()
    stack_heads(lambda s: rows[s, :, :256], queries)
    for d in (0, 1, 3, 2):
        j = ring(me.b, -d)
        if d:
            for k, (_, s) in enumerate(arrivals):
                kv_wire.take((k, d - 1), kv.at[j, s])
        for part in range(2):
            mix_tile(me, j, part, pair, kv, query_pos, queries, key_pos, mixed_t, total)
            step()
    finish_mix(mixed, mixed_t, log_total, stacked, total)

    def place(origin):
        return attn_out.at[:, pl.ds(pl.multiple_of(origin * 256, 256), 256)]

    for k in range(1, 8):
        peer = peer_of(head, k)
        back_wire.push(k - 1, mixed.at[peer], place(head), group_spot(me, peer))
    attn_out[:, pl.ds(pl.multiple_of(head * 256, 256), 256)] = mixed[head]
    while turns:
        step()
    for k in range(7):
        back_wire.take(k, place(peer_of(head, 7 - k)))
    finish()
    for wire in (x_wire, w_wire, kv_wire, back_wire):
        wire.close()


def attention_forward(pair, x, gains, tables, weights):
    outs = pl.pallas_call(
        forward_body,
        out_shape=[
            jax.ShapeDtypeStruct((128, 2048), BF16),
            jax.ShapeDtypeStruct((8, 128, 512), BF16),
            jax.ShapeDtypeStruct((8, 128, 384), F32),
            jax.ShapeDtypeStruct((4, 8, 128, 256), BF16),
            jax.ShapeDtypeStruct((128, 2048), F32),
            jax.ShapeDtypeStruct((8, 2048), F32),
        ]
        + [jax.ShapeDtypeStruct((4,) + w.shape, w.dtype) for w in weights],
        in_specs=[SMEM] + [VMEM] * 6 + [HBM] * 7,
        out_specs=[VMEM] * 6 + [HBM] * 7,
        scratch_shapes=[
            pltpu.VMEM((8, 128, 1024), BF16),
            pltpu.VMEM((4, 256, 512), BF16),
            pltpu.VMEM((2048, 128), BF16),
            pltpu.VMEM((2048, 128), BF16),
            pltpu.VMEM((8, 2048), jnp.int32),
            pltpu.VMEM((TILE, CHUNK), jnp.int32),
            pltpu.VMEM((8, 2048), F32),
            pltpu.VMEM((8, 128, 256), BF16),
            dma(7), dma(7), dma(3, 3), dma(3, 3), dma(3), dma(8, 3), dma(8, 3), dma(7), dma(7),
        ]
        + gather_scratch(weights),
        compiler_params=comm_params(1),
        name="attention_forward",
    )(pair, x, *gains, *tables, *weights)
    return outs[:6], [whole_rows(out) for out in outs[6:]]


def whole_rows(out):
    return out.reshape(4 * out.shape[1], out.shape[2])


PAIR_TILE = 512


def half_of(ref, half):
    width = ref.shape[-1] // 2
    return ref.at[:, :, pl.ds(half * width, width)]


def add_into(target, *sources):
    for zh in range(target.shape[0]):

        @pl.loop(0, target.shape[1] // 16)
        def _(r):
            at = pl.ds(pl.multiple_of(r * 16, 16), 16)
            total = target[zh, at, :].astype(F32)
            for source in sources:
                total = total + source[zh, at, :].astype(F32)
            target[zh, at, :] = total.astype(BF16)


class PairGrad:
    def scratch(width):
        return [
            pltpu.VMEM((2, 128, 256), BF16),
            pltpu.VMEM((512, 256), BF16),
            pltpu.VMEM((256, width), BF16),
            pltpu.VMEM((2, 256, width), BF16),
        ]

    def __init__(self, me, left, right, scratch, wire, slot):
        self.me, self.left, self.right, self.wire, self.slot = me, left, right, wire, slot
        self.landing, self.left_t, self.pair, self.grad = scratch

    def send(self):
        me = self.me
        twin = me.sibling()
        self.wire.push(self.slot + 2, self.right, self.pair.at[pl.ds(128, 128)], twin)
        for zh in range(2):
            columns = pl.ds(pl.multiple_of((zh * 2 + 1 - me.core) * 256, 256), 256)
            self.wire.push(self.slot + zh, self.left.at[:, columns], self.landing.at[zh], twin)

    def multiply(self):
        me = self.me
        self.pair[0:128, :] = self.right[...]
        for zh in range(2):
            columns = pl.ds(pl.multiple_of((zh * 2 + me.core) * 256, 256), 256)
            self.left_t[zh * 256 : zh * 256 + 256, 0:128] = self.left[:, columns].T
            self.wire.take(self.slot + zh, self.landing.at[zh])
            self.left_t[zh * 256 : zh * 256 + 256, 128:256] = self.landing[zh].T
        self.wire.take(self.slot + 2, self.pair.at[pl.ds(128, 128)])

        @pl.loop(0, self.pair.shape[1] // PAIR_TILE)
        def _(t):
            columns = pl.ds(pl.multiple_of(t * PAIR_TILE, PAIR_TILE), PAIR_TILE)
            product = dot_nn(self.left_t[...], self.pair[:, columns]).astype(BF16)
            self.grad[:, :, columns] = product.reshape(2, 256, PAIR_TILE)


REDUCE_SLOTS = 14


def reduce_scratch(widths):
    scratch = []
    for width in widths:
        half = width // 2
        scratch += [
            pltpu.VMEM((2, 64, half), BF16),
            pltpu.VMEM((2, 64, half), BF16),
            pltpu.VMEM((2, 64, width), BF16),
            pltpu.VMEM((2, 64, width), BF16),
            pltpu.VMEM((2, 16, half), BF16),
            pltpu.VMEM((2, 16, half), BF16),
            pltpu.VMEM((2, 16, width), BF16),
            pltpu.VMEM((2, 16, width), BF16),
            pltpu.VMEM((1, 16, width), BF16),
            pltpu.VMEM((1, 16, width), BF16),
        ]
    count = len(widths)
    return scratch + [dma(count, REDUCE_SLOTS), dma(count, REDUCE_SLOTS)]


def reduce_stages(me, grads, pieces, scratch):
    wire = Wire(scratch[-2], scratch[-1], me.sibling())
    buffers = [scratch[10 * k : 10 * k + 10] for k in range(len(grads))]

    def rows(ref, i, size, half=None):
        view = ref.at[:, pl.ds(pl.multiple_of(i * size, size), size)]
        return view if half is None else half_of(view, half)

    def ring_stages(slot, axis, size, source, bufs):
        position = getattr(me, axis)
        ahead = me.move(**{axis: ring(position, 1)})
        behind = me.move(**{axis: ring(position, -1)})
        left, right, far = ring(position, -1), ring(position, 1), ring(position, 2)

        def send(k):
            src = source(k)
            far_a, far_b, in_a, in_b = bufs(k)
            wire.push((k, slot), rows(src, far, size, 0), far_a, ahead)
            wire.push((k, slot + 1), rows(src, far, size, 1), far_b, behind)
            wire.push((k, slot + 2), rows(src, right, size, 1), half_of(in_a, 1), ahead)
            wire.push((k, slot + 3), rows(src, left, size, 0), half_of(in_b, 0), behind)

        def relay(k):
            src = source(k)
            far_a, far_b, in_a, in_b = bufs(k)
            wire.take((k, slot), far_a)
            add_into(far_a, rows(src, right, size, 0))
            wire.push((k, slot + 4), far_a, half_of(in_a, 0), ahead)
            wire.take((k, slot + 1), far_b)
            add_into(far_b, rows(src, left, size, 1))
            wire.push((k, slot + 5), far_b, half_of(in_b, 1), behind)

        def collect(k):
            src = source(k)
            far_a, far_b, in_a, in_b = bufs(k)
            wire.take((k, slot + 2), half_of(in_a, 1))
            wire.take((k, slot + 3), half_of(in_b, 0))
            wire.take((k, slot + 4), half_of(in_a, 0))
            wire.take((k, slot + 5), half_of(in_b, 1))
            add_into(in_a, in_b, rows(src, position, size))

        return send, relay, collect

    b_send, b_relay, b_collect = ring_stages(
        0, "b", 64, lambda k: grads[k], lambda k: buffers[k][0:4]
    )
    a_send, a_relay, a_collect = ring_stages(
        6, "a", 16, lambda k: buffers[k][2], lambda k: buffers[k][4:8]
    )

    def z_send(k):
        wire.push((k, 12), buffers[k][6].at[pl.ds(1 - me.zh, 1)], buffers[k][8], me.across())

    def z_relay(k):
        held = buffers[k][8]
        wire.take((k, 12), held)
        add_into(held, buffers[k][6].at[pl.ds(me.zh, 1)])
        wire.push((k, 13), held, buffers[k][9], me.move(zl=1 - me.zl))

    def z_collect(k):
        held, other = buffers[k][8], buffers[k][9]
        wire.take((k, 13), other)
        pieces[k][...] = (held[...].astype(F32) + other[...].astype(F32)).astype(BF16)

    def both(first, second):
        def stage(k):
            first(k)
            second(k)

        return stage

    stages = [b_send, b_relay, both(b_collect, a_send), a_relay, both(a_collect, z_send), z_relay, z_collect]
    return stages, wire.close


def replicate_stages(me, pieces, outs, send, recv, load_sem):
    wire = Wire(send, recv, me.sibling())
    loads = {}

    def cut(k, row, rows, half=None):
        width = outs[k].shape[1] // 2
        at = pl.ds(pl.multiple_of(row, 16), rows)
        if half is None:
            return outs[k].at[at]
        return outs[k].at[at, pl.ds(half * width, width)]

    a_next, a_prev = me.move(a=ring(me.a, 1)), me.move(a=ring(me.a, -1))
    b_next, b_prev = me.move(b=ring(me.b, 1)), me.move(b=ring(me.b, -1))

    def a_row(step):
        return (me.b * 4 + ring(me.a, step)) * 16

    def b_row(step):
        return ring(me.b, step) * 64

    def a_send(k):
        place = cut(k, a_row(0), 16)
        wire.push((k, 0), pieces[k].at[0], place, a_next)
        wire.push((k, 1), pieces[k].at[0], place, a_prev)
        loads[k] = pltpu.make_async_copy(pieces[k].at[0], place, load_sem.at[k])
        loads[k].start()

    def a_relay(k):
        wire.take((k, 0), cut(k, a_row(-1), 16))
        wire.push((k, 2), cut(k, a_row(-1), 16, 0), cut(k, a_row(-1), 16, 0), a_next)
        wire.take((k, 1), cut(k, a_row(1), 16))
        wire.push((k, 3), cut(k, a_row(1), 16, 1), cut(k, a_row(1), 16, 1), a_prev)

    def b_send(k):
        wire.take((k, 2), cut(k, a_row(2), 16, 0))
        wire.take((k, 3), cut(k, a_row(2), 16, 1))
        loads[k].wait()
        mine = cut(k, b_row(0), 64)
        wire.push((k, 4), mine, mine, b_next)
        wire.push((k, 5), mine, mine, b_prev)

    def b_relay(k):
        wire.take((k, 4), cut(k, b_row(-1), 64))
        wire.push((k, 6), cut(k, b_row(-1), 64, 0), cut(k, b_row(-1), 64, 0), b_next)
        wire.take((k, 5), cut(k, b_row(1), 64))
        wire.push((k, 7), cut(k, b_row(1), 64, 1), cut(k, b_row(1), 64, 1), b_prev)

    def b_collect(k):
        wire.take((k, 6), cut(k, b_row(2), 64, 0))
        wire.take((k, 7), cut(k, b_row(2), 64, 1))

    return [a_send, a_relay, b_send, b_relay, b_collect], wire.close


def gain_turns(me, gains, gains_out, gain_slots, gain_send, gain_recv):
    first = me.core == 0
    x, y = jnp.where(first, me.a, me.b), jnp.where(first, me.b, me.a)
    z = me.zh * 2 + me.zl
    wire = Wire(gain_send, gain_recv, me.sibling())

    def pick(d, on_x):
        use_a = first if on_x else jnp.logical_not(first)
        return me.move(
            a=jnp.where(use_a, ring(me.a, d), me.a), b=jnp.where(use_a, me.b, ring(me.b, d))
        )

    def z_spot(d):
        far = lax.rem(z + d, 4)
        return me.move(zl=lax.rem(far, 2), zh=far // 2)

    def push(stage, position, spots):
        for d, spot in enumerate(spots):
            slot = gain_slots.at[stage, position]
            wire.push((stage, d), slot, slot, spot)

    def take(stage, position, size):
        for d in range(size - 1):
            wire.take((stage, d), gain_slots.at[stage, lax.rem(position + size - 1 - d, size)])

    def total(stage):
        return (gain_slots[stage, 0] + gain_slots[stage, 1]) + (gain_slots[stage, 2] + gain_slots[stage, 3])

    def turn0():
        gain_slots[0, me.core] = gains[...]
        push(0, me.core, [me.sibling()])

    def turn1():
        take(0, me.core, 2)
        gain_slots[1, x] = gain_slots[0, 0] + gain_slots[0, 1]
        push(1, x, [pick(d, True) for d in (1, 2, 3)])

    def turn2():
        take(1, x, 4)
        gain_slots[2, y] = total(1)
        push(2, y, [pick(d, False) for d in (1, 2, 3)])

    def turn3():
        take(2, y, 4)
        gain_slots[3, z] = total(2)
        push(3, z, [z_spot(d) for d in (1, 2, 3)])

    def turn4():
        take(3, z, 4)
        gains_out[...] = total(3)

    return [turn0, turn1, turn2, turn3, turn4], wire.close


def unrope(s, low, grads, raw, inner, outer, gain, column, gain_part):
    cosine, sine = rope_rows(inner, outer, low)
    value = raw[s, :, column : column + 128]
    scale = norm_scale(value)
    hat = value * scale
    hat_cot = grads * cosine - pltpu.roll(grads, 64, 1) * sine
    gain_part[...] += jnp.sum((hat_cot * hat).reshape(16, 8, 128), axis=0)
    scaled = hat_cot * gain[...]
    return (scale * (scaled - hat * mean_last(scaled * hat))).astype(BF16)


EARLY = (3072, 3072, 3072, 2048)


def backward_body(
    pair, query_gain, key_gain, inner, outer, rows, raw, kv, mixed_t, log_total, parts,
    mlp_in, down_cot, branch_cot, gate_cot, up_cot, hidden, attn_out,
    proj, gain_out, p0, p1, p2, p3, *refs,
):
    (
        cots_in, dkv, queries, cots, deltas, query_pos, key_pos, probs_all, score_cots, acc, held, stacked, message,
        cot_send, cot_recv, p_send, p_recv, m_send, m_recv, w_send, w_recv,
    ), refs = refs[:21], refs[21:]
    me = here()
    head = group_head(me)
    twin = me.sibling()
    others = [me.move(b=ring(me.b, d)) for d in (1, 2, 3)]
    greet([twin, me.across()] + group_neighbours(me))
    cot_wire = Wire(cot_send, cot_recv, twin)
    p_wire = Wire(p_send, p_recv, twin)
    m_wire = Wire(m_send, m_recv, twin)
    w_wire = Wire(w_send, w_recv, twin)

    def of_head(ref, h):
        return ref.at[:, pl.ds(pl.multiple_of(h * 256, 256), 256)]

    for k in range(1, 8):
        peer = peer_of(head, k)
        cot_wire.push(k - 1, of_head(parts, peer), cots_in.at[head], group_spot(me, peer))
    lefts = (mlp_in, mlp_in, down_cot, branch_cot)
    rights = (gate_cot, up_cot, hidden, attn_out)
    pairs = []
    for i, (left, right) in enumerate(zip(lefts, rights)):
        pairs.append(PairGrad(me, left, right, refs[4 * i : 4 * i + 4], w_wire, 3 * i))
        pairs[i].send()
    stages, finish = reduce_stages(me, [p.grad for p in pairs], (p0, p1, p2, p3), refs[16:])
    turns = pipeline([lambda k: pairs[k].multiply()] + stages, 4)

    def step():
        if turns:
            turns.pop(0)()

    query_positions(pair, me, query_pos)
    cots_in[head] = parts[:, pl.ds(pl.multiple_of(head * 256, 256), 256)]
    gain_out[...] = jnp.zeros_like(gain_out)
    step()
    step()
    for k in range(7):
        cot_wire.take(k, cots_in.at[peer_of(head, 7 - k)])
    start_grad(rows, mixed_t, cots_in, queries, cots, deltas, acc)
    step()
    for d in (2, 1, 3, 0):
        j = ring(me.b, d)
        for part in range(2):
            grad_tile(
                me, j, part, pair, kv, query_pos, queries, cots, deltas, log_total, key_pos,
                probs_all, score_cots, acc, dkv,
            )
            if part == 1 and d:
                for k in range(8):
                    peer = peer_of(head, k)
                    p_wire.push((k, d - 1), dkv.at[j, peer], held.at[d - 1, peer], others[d - 1])
            step()
    for chunk in range(8):
        columns = pl.ds(chunk * CHUNK, CHUNK)
        stacked[columns, :] = (acc[:, columns] * SCORE_SCALE).T

    def places(h):
        return (
            (pl.ds(0, 256), pl.ds(pl.multiple_of(h * 256, 256), 256)),
            (pl.ds(256, 128), pl.ds(pl.multiple_of(2048 + h * 128, 128), 128)),
            (pl.ds(384, 128), pl.ds(pl.multiple_of(3072 + h * 128, 128), 128)),
        )

    for k in (1, 2, 3, 4, 5, 6, 7, 0):
        s = peer_of(head, k)
        low = low_block(pair, me, me.b, s)
        for d in range(3):
            p_wire.take((k, d), held.at[d, s])
        for h in range(2):
            grads = jnp.concatenate(
                [
                    stacked[pl.ds(pl.multiple_of(part * 1024 + s * 128 + h * 64, 64), 64), :]
                    for part in range(2)
                ],
                axis=0,
            )
            message[s, :, h * 128 : h * 128 + 128] = unrope(
                s, low, grads, raw, inner, outer, query_gain, h * 128, gain_out.at[0]
            )
        total = (
            dkv[me.b, s].astype(F32)
            + held[0, s].astype(F32)
            + held[1, s].astype(F32)
            + held[2, s].astype(F32)
        )
        message[s, :, 256:384] = unrope(
            s, low, total[:, :128], raw, inner, outer, key_gain, 256, gain_out.at[1]
        )
        message[s, :, 384:] = total[:, 128:].astype(BF16)
        if k:
            for i, (source, target) in enumerate(places(head)):
                m_wire.push((k - 1, i), message.at[s, :, source], proj.at[:, target], group_spot(me, s))
    for source, target in places(head):
        proj[:, target] = message[head, :, source]
    while turns:
        step()
    for k in range(7):
        for i, (_, target) in enumerate(places(peer_of(head, 7 - k))):
            m_wire.take((k, i), proj.at[:, target])
    finish()
    for wire in (cot_wire, p_wire, m_wire, w_wire):
        wire.close()


def attention_backward(pair, gains, tables, kept, attended_cot, lefts, rights):
    heads = (8, 128, 256)
    return pl.pallas_call(
        backward_body,
        out_shape=[jax.ShapeDtypeStruct((128, 4096), BF16), jax.ShapeDtypeStruct((2, 8, 128), F32)]
        + [jax.ShapeDtypeStruct((1, 16, width), BF16) for width in EARLY],
        in_specs=[SMEM] + [VMEM] * 17,
        out_specs=[VMEM] * 6,
        scratch_shapes=[
            pltpu.VMEM(heads, BF16),
            pltpu.VMEM((4,) + heads, BF16),
            pltpu.VMEM((2048, 128), BF16),
            pltpu.VMEM((2048, 128), BF16),
            pltpu.VMEM((8, 2048), F32),
            pltpu.VMEM((8, 2048), jnp.int32),
            pltpu.VMEM((TILE, CHUNK), jnp.int32),
            pltpu.VMEM((TILE, 2048), BF16),
            pltpu.VMEM((TILE, 2048), BF16),
            pltpu.VMEM((128, 2048), F32),
            pltpu.VMEM((3,) + heads, BF16),
            pltpu.VMEM((2048, 128), F32),
            pltpu.VMEM((8, 128, 512), BF16),
            dma(7), dma(7), dma(8, 3), dma(8, 3), dma(7, 3), dma(7, 3), dma(12), dma(12),
        ]
        + [item for width in EARLY for item in PairGrad.scratch(width)]
        + reduce_scratch(EARLY),
        compiler_params=comm_params(2),
        name="attention_backward",
    )(pair, *gains, *tables, *kept, attended_cot, *lefts, *rights)


LATE = (2048, 2048)


def final_body(
    x, attn_gain, middle_cot, proj, gain_parts, e0, e1, e2, e3, wq, wk, wv,
    input_cot, gains_out, o0, o1, o2, o3, o4, o5, *refs,
):
    (
        attn_in, gains, fq, fk, fv, piece0, piece1, load_sem, w_send, w_recv,
        e_send, e_recv, e_load, l_send, l_recv, l_load, gain_slots, gain_send, gain_recv,
    ), refs = refs[:19], refs[19:]
    me = here()
    twin = me.sibling()
    greet(
        [twin, me.across(), me.move(zl=1 - me.zl), me.move(zh=1 - me.zh)]
        + [me.move(a=ring(me.a, d)) for d in (1, 2, 3)]
        + [me.move(b=ring(me.b, d)) for d in (1, 2, 3)]
    )
    loads = [
        pltpu.make_async_copy(source, target, load_sem.at[i])
        for i, (source, target) in enumerate(((wq, fq), (wk, fk), (wv, fv)))
    ]
    for load in loads:
        load.start()
    w_wire = Wire(w_send, w_recv, twin)
    inputs = x[...].astype(F32)
    scale = norm_scale(inputs)
    attn_in[...] = (inputs * scale * attn_gain[...]).astype(BF16)
    pairs = [
        PairGrad(me, attn_in, proj.at[:, pl.ds(2048 * i, 2048)], refs[4 * i : 4 * i + 4], w_wire, 3 * i)
        for i in range(2)
    ]
    for pair in pairs:
        pair.send()
    early, early_finish = replicate_stages(me, (e0, e1, e2, e3), (o0, o1, o2, o3), e_send, e_recv, e_load)
    early = pipeline(early, 4)
    stages, late_finish = reduce_stages(me, [p.grad for p in pairs], (piece0, piece1), refs[8:])
    late, out_finish = replicate_stages(me, (piece0, piece1), (o4, o5), l_send, l_recv, l_load)
    turns = pipeline([lambda k: pairs[k].multiply()] + stages + late, 2)
    small, small_finish = gain_turns(me, gains, gains_out, gain_slots, gain_send, gain_recv)

    def step(queue):
        if queue:
            queue.pop(0)()

    step(early)
    step(turns)
    step(turns)
    step(early)
    for load in loads:
        load.wait()
    attn_in_cot = (
        dot_nt(proj[:, :2048], fq[...]) + dot_nt(proj[:, 2048:3072], fk[...]) + dot_nt(proj[:, 3072:], fv[...])
    )
    normed = inputs * scale
    scaled = attn_in_cot * attn_gain[...]
    input_cot[...] = middle_cot[...] + scale * (scaled - normed * mean_last(scaled * normed))
    gains[...] = gain_parts[...]
    gains[0:1, :] = jnp.sum(attn_in_cot * normed, axis=0, keepdims=True)
    while turns or early or small:
        step(turns)
        step(early)
        step(small)
    early_finish()
    late_finish()
    out_finish()
    small_finish()
    w_wire.close()


def final_step(x, attn_gain, middle_cot, proj, gain_parts, pieces, weights):
    outs = pl.pallas_call(
        final_body,
        out_shape=[jax.ShapeDtypeStruct((128, 1024), F32), jax.ShapeDtypeStruct((4, 1024), F32)]
        + [jax.ShapeDtypeStruct((256, width), BF16) for width in EARLY + LATE],
        in_specs=[VMEM] * 9 + [HBM] * 3,
        out_specs=[VMEM] * 2 + [HBM] * 6,
        scratch_shapes=[
            pltpu.VMEM((128, 1024), BF16),
            pltpu.VMEM((4, 1024), F32),
            pltpu.VMEM((1024, 2048), BF16),
            pltpu.VMEM((1024, 1024), BF16),
            pltpu.VMEM((1024, 1024), BF16),
            pltpu.VMEM((1, 16, 2048), BF16),
            pltpu.VMEM((1, 16, 2048), BF16),
            dma(3), dma(6), dma(6), dma(4, 8), dma(4, 8), dma(4), dma(2, 8), dma(2, 8), dma(2),
            pltpu.VMEM((4, 4, 4, 1024), F32), dma(4, 3), dma(4, 3),
        ]
        + [item for width in LATE for item in PairGrad.scratch(width)]
        + reduce_scratch(LATE),
        compiler_params=comm_params(3),
        name="final_step",
    )(x, attn_gain, middle_cot, proj, gain_parts, *pieces, *weights)
    return outs[0], outs[1], outs[2:]


def rms_scale(values):
    return lax.rsqrt(jnp.mean(values * values, axis=-1, keepdims=True) + EPSILON)


def norm_back(grad_out, normed, scale_inv):
    return scale_inv * (grad_out - normed * jnp.mean(grad_out * normed, axis=-1, keepdims=True))


def matmul(matrix, second):
    return jnp.dot(matrix, second, preferred_element_type=F32)


def matmul_rows(matrix, second):
    return lax.dot_general(matrix, second, (((1,), (1,)), ((), ())), preferred_element_type=F32)


def shards(
    tokens,
    query_weight,
    key_weight,
    value_weight,
    out_weight,
    gate_weight,
    up_weight,
    down_weight,
    attn_gain,
    mlp_gain,
    query_gain,
    key_gain,
    pair_order,
    out_grad,
):
    tables = rope_tables()
    attn_row, query_row, key_row = attn_gain[None], query_gain[None], key_gain[None]
    (attn_out, *kept), full = attention_forward(
        pair_order,
        tokens[0],
        (attn_row, query_row, key_row),
        tables,
        [out_weight, gate_weight, up_weight, down_weight, query_weight, key_weight, value_weight],
    )
    full_out, full_gate, full_up, full_down, *full_qkv = full

    middle = tokens[0].astype(F32) + matmul_rows(attn_out, full_out)
    mlp_scale = rms_scale(middle)
    mlp_normed = middle * mlp_scale
    mlp_in = (mlp_normed * mlp_gain).astype(BF16)
    gate_pre = matmul(mlp_in, full_gate)
    up_pre = matmul(mlp_in, full_up)
    sigmoid_gate = jax.nn.sigmoid(gate_pre)
    silu_gate = gate_pre * sigmoid_gate
    hidden = (silu_gate * up_pre).astype(BF16)
    result = middle + matmul_rows(hidden, full_down)
    down_cot = out_grad[0]
    hidden_cot = matmul(down_cot, full_down)
    gate_cot = (hidden_cot * up_pre * sigmoid_gate * (1.0 + gate_pre * (1.0 - sigmoid_gate))).astype(BF16)
    up_cot = (hidden_cot * silu_gate).astype(BF16)
    mlp_in_cot = matmul_rows(gate_cot, full_gate) + matmul_rows(up_cot, full_up)
    mlp_gain_part = jnp.sum(mlp_in_cot * mlp_normed, axis=0)
    middle_cot = down_cot.astype(F32) + norm_back(mlp_in_cot * mlp_gain, mlp_normed, mlp_scale)
    branch_cot = middle_cot.astype(BF16)
    attended_cot = matmul(branch_cot, full_out).astype(BF16)

    proj, head_gains, *pieces = attention_backward(
        pair_order,
        (query_row, key_row),
        tables,
        kept,
        attended_cot,
        (mlp_in, down_cot, branch_cot),
        (gate_cot, up_cot, hidden, attn_out),
    )
    head_gains = jnp.pad(jnp.sum(head_gains, axis=1), ((0, 0), (0, 896)))
    gain_parts = jnp.concatenate([jnp.zeros((1, 1024), F32), mlp_gain_part[None], head_gains], 0)
    input_cot, gains, grads = final_step(tokens[0], attn_row, middle_cot, proj, gain_parts, pieces, full_qkv)
    gate, up, down, out, query, key_value = (grad.astype(F32) for grad in grads)
    return (
        result.astype(BF16)[None],
        input_cot[None],
        query,
        key_value[:, :1024],
        key_value[:, 1024:],
        out,
        gate,
        up,
        down,
        gains[0],
        gains[1],
        gains[2, :128],
        gains[3, :128],
    )


def solution(mesh):
    rows, split, whole = P("fsdp", None), P("fsdp", "ctx", None), P()
    return jax.shard_map(
        shards,
        mesh=mesh,
        in_specs=(split,) + (rows,) * 7 + (whole,) * 4 + (rows, split),
        out_specs=(split, split) + (rows,) * 7 + (whole,) * 4,
        check_vma=False,
    )
```

```python
import functools

import jax
import jax.numpy as jnp
import numpy as np
from jax import lax
from jax.experimental import pallas as pl
from jax.experimental.pallas import tpu as pltpu
from jax.sharding import PartitionSpec as P

EPSILON = 1e-06
ROPE_BASE = 1000000.0
MESH = pl.DeviceIdType.MESH
HBM = pl.BlockSpec(memory_space=pltpu.HBM)
VMEM = pl.BlockSpec(memory_space=pltpu.VMEM)
SMEM = pl.BlockSpec(memory_space=pltpu.SMEM)
LOG2E = 1.4426950408889634
VMEM_LIMIT = 56 * 1024 * 1024
BF16 = jnp.bfloat16
F32 = jnp.float32


class Spot:
    def __init__(self, a, b, zl, zh, core):
        self.a, self.b, self.zl, self.zh, self.core = a, b, zl, zh, core

    def move(self, a=None, b=None, zl=None, zh=None):
        return Spot(
            self.a if a is None else a,
            self.b if b is None else b,
            self.zl if zl is None else zl,
            self.zh if zh is None else zh,
            self.core,
        )

    def id(self):
        first = self.core == 0
        x = jnp.where(first, self.a, self.b)
        y = jnp.where(first, self.b, self.a)
        return (self.zl * 16 + y * 4 + x, self.zh * 2 + self.core)

    def sibling(self):
        return Spot(self.b, self.a, self.zl, self.zh, 1 - self.core)

    def across(self):
        return self.move(zl=1 - self.zl, zh=1 - self.zh)


def here():
    ctx = lax.axis_index("ctx")
    fsdp = lax.axis_index("fsdp")
    x = lax.rem(ctx, 4)
    y = lax.rem(ctx // 4, 4)
    core = lax.rem(fsdp, 2)
    first = core == 0
    return Spot(jnp.where(first, x, y), jnp.where(first, y, x), ctx // 16, fsdp // 2, core)


def ring(position, step):
    return lax.rem(position + step + 4, 4)


def greet(spots):
    barrier = pltpu.get_barrier_semaphore()
    for spot in spots:
        pl.semaphore_signal(barrier, inc=1, device_id=spot.id(), device_id_type=MESH)
    pl.semaphore_wait(barrier, len(spots))


def remote(src, dst, send_sem, recv_sem, spot):
    return pltpu.make_async_remote_copy(
        src_ref=src,
        dst_ref=dst,
        send_sem=send_sem,
        recv_sem=recv_sem,
        device_id=spot.id(),
        device_id_type=MESH,
    )


def comm_params(collective_id, limit=VMEM_LIMIT):
    return pltpu.CompilerParams(
        collective_id=collective_id, has_side_effects=True, vmem_limit_bytes=limit
    )


class Wire:
    def __init__(self, send, recv, spot):
        self.send, self.recv, self.spot, self.sent = send, recv, spot, []

    def push(self, slot, src, dst, spot):
        copy = remote(src, dst, self.send.at[slot], self.recv.at[slot], spot)
        copy.start()
        self.sent.append((slot, copy))

    def take(self, slot, dst):
        remote(dst, dst, self.send.at[slot], self.recv.at[slot], self.spot).wait_recv()

    def settle(self, k):
        for slot, copy in self.sent:
            if slot[0] == k:
                copy.wait_send()
        self.sent = [(slot, copy) for slot, copy in self.sent if slot[0] != k]

    def close(self):
        for _, copy in self.sent:
            copy.wait_send()


def pipeline(stages, count):
    def turn(t):
        for depth, stage in enumerate(stages):
            if 0 <= t - depth < count:
                stage(t - depth)

    return [functools.partial(turn, t) for t in range(count + len(stages) - 1)]


GATHER_SLOTS = 14
DIRECT = 1


def gather_scratch(weights):
    count = len(weights)
    return [pltpu.VMEM(w.shape, w.dtype) for w in weights] + [
        pltpu.SemaphoreType.DMA((count, GATHER_SLOTS)),
        pltpu.SemaphoreType.DMA((count, GATHER_SLOTS)),
        pltpu.SemaphoreType.DMA((2, count)),
    ]


def gather_turns(me, ins, outs, scratch):
    count = len(ins)
    held, (send, recv, local_sem) = scratch[:count], scratch[count:]
    mine = me.zh * 2 + me.core
    other = (1 - me.zh) * 2 + me.core
    twin_mine = me.zh * 2 + 1 - me.core
    twin_other = (1 - me.zh) * 2 + 1 - me.core
    twin, across = me.sibling(), me.across()
    a_next, a_prev = me.move(a=ring(me.a, 1)), me.move(a=ring(me.a, -1))
    b_next, b_prev = me.move(b=ring(me.b, 1)), me.move(b=ring(me.b, -1))
    wire = Wire(send, recv, twin)

    def cut(m, rows, half):
        width = ins[m].shape[1] // 2
        if half is None:
            return outs[m].at[other, rows]
        return outs[m].at[other, rows, pl.ds(half * width, width)]

    def piece(m, a, half=None):
        return cut(m, pl.ds(pl.multiple_of((me.b * 4 + a) * 16, 16), 16), half)

    def block(m, b, half=None):
        return cut(m, pl.ds(pl.multiple_of(b * 64, 64), 64), half)

    def push(m, slot, src, dst, spot):
        wire.push((m, slot), src, dst, spot)

    def take(m, slot, dst):
        wire.take((m, slot), dst)

    loads = [pltpu.make_async_copy(ins[m], held[m], local_sem.at[0, m]) for m in range(count)]
    stores = [pltpu.make_async_copy(held[m], outs[m].at[mine], local_sem.at[1, m]) for m in range(count)]

    ringed = count - DIRECT

    def start():
        for m in range(ringed):
            rows = pl.ds(pl.multiple_of((me.b * 4 + me.a) * 16, 16), 16)
            push(m, 0, ins[m].at[rows], outs[m].at[mine, rows], across)
        for m in range(ringed, count):
            for i in range(4):
                rows = pl.ds(64 * i, 64)
                push(m, i, ins[m].at[rows], outs[m].at[mine, rows], across)
        for load in loads:
            load.start()

    def spread_own():
        for m in range(count):
            loads[m].wait()
            stores[m].start()
            push(m, 9, ins[m], outs[m].at[mine], twin)

    def stage_z(m):
        take(m, 0, piece(m, me.a))
        push(m, 1, piece(m, me.a), piece(m, me.a), a_next)
        push(m, 2, piece(m, me.a), piece(m, me.a), a_prev)

    def stage_a(m):
        left, right = ring(me.a, -1), ring(me.a, 1)
        take(m, 1, piece(m, left))
        push(m, 3, piece(m, left, 0), piece(m, left, 0), a_next)
        take(m, 2, piece(m, right))
        push(m, 4, piece(m, right, 1), piece(m, right, 1), a_prev)

    def stage_b(m):
        far = ring(me.a, 2)
        take(m, 3, piece(m, far, 0))
        take(m, 4, piece(m, far, 1))
        push(m, 5, block(m, me.b), block(m, me.b), b_next)
        push(m, 6, block(m, me.b), block(m, me.b), b_prev)
        push(m, 10, block(m, me.b), block(m, me.b), twin)

    def stage_c(m):
        left, right = ring(me.b, -1), ring(me.b, 1)
        take(m, 5, block(m, left))
        push(m, 7, block(m, left, 0), block(m, left, 0), b_next)
        push(m, 11, block(m, left), block(m, left), twin)
        take(m, 6, block(m, right))
        push(m, 8, block(m, right, 1), block(m, right, 1), b_prev)
        push(m, 12, block(m, right), block(m, right), twin)

    def stage_d(m):
        far = ring(me.b, 2)
        take(m, 7, block(m, far, 0))
        take(m, 8, block(m, far, 1))
        push(m, 13, block(m, far), block(m, far), twin)

    def pass_direct(i):
        for m in range(ringed, count):
            rows = outs[m].at[other, pl.ds(64 * i, 64)]
            take(m, i, rows)
            push(m, 10 + i, rows, rows, twin)

    def finish():
        for m in range(ringed, count):
            take(m, 9, outs[m].at[twin_mine])
            for i in range(4):
                take(m, 10 + i, outs[m].at[twin_other, pl.ds(64 * i, 64)])
        for m in range(ringed):
            take(m, 9, outs[m].at[twin_mine])
            for slot, step in ((10, 0), (11, -1), (12, 1), (13, 2)):
                rows = pl.ds(pl.multiple_of(ring(me.a, step) * 64, 64), 64)
                take(m, slot, outs[m].at[twin_other, rows])
        for store in stores:
            store.wait()
        wire.close()

    turns = pipeline((stage_z, stage_a, stage_b, stage_c, stage_d), ringed)
    turns += [functools.partial(pass_direct, i) for i in range(4)]
    return start, spread_own, turns, finish


def group_spot(me, head):
    return me.move(a=lax.rem(head, 4), zl=head // 4)


def group_head(me):
    return me.a + 4 * me.zl


def peer_of(head, k):
    return lax.rem(head + k, 8)


def group_neighbours(me):
    head = group_head(me)
    return [group_spot(me, peer_of(head, k)) for k in range(1, 8)] + [
        me.move(b=ring(me.b, d)) for d in (1, 2, 3)
    ]


def dma(*shape):
    return pltpu.SemaphoreType.DMA(shape)


TILE = 512
CHUNK = 256
SCORE_SCALE = 128.0**-0.5


def dot_nt(left, right):
    return lax.dot_general(left, right, (((1,), (1,)), ((), ())), preferred_element_type=F32)


def dot_nn(left, right):
    return lax.dot_general(left, right, (((1,), (0,)), ((), ())), preferred_element_type=F32)


def stack_heads(read, target):
    for s in range(8):
        rows = read(s)
        for part in range(2):
            for head in range(2):
                at = part * 1024 + s * 128 + head * 64
                target[at : at + 64, :] = rows[part * 64 : part * 64 + 64, head * 128 : head * 128 + 128]


def unstack_heads(stacked, s, out):
    for part in range(2):
        for head in range(2):
            at = part * 1024 + s * 128 + head * 64
            out[s, part * 64 : part * 64 + 64, head * 128 : head * 128 + 128] = stacked[at : at + 64, :]


def low_block(pair, me, j, s):
    a = lax.rem(s, 4)
    first = me.core == 0
    return pair[0, (s // 4) * 16 + jnp.where(first, j * 4 + a, a * 4 + j)]


def key_positions(pair, me, j, part, target):
    line = lax.broadcasted_iota(jnp.int32, (64, CHUNK), 0)
    for s in range(8):
        low = low_block(pair, me, j, s)
        block = low if part == 0 else 63 - low
        target[s * 64 : s * 64 + 64, :] = line + block * 64


def query_positions(pair, me, target):
    line = lax.rem(lax.broadcasted_iota(jnp.int32, (8, 128), 1), 64)
    for s in range(8):
        low = low_block(pair, me, me.b, s)
        target[:, s * 128 : s * 128 + 128] = line + low * 64
        target[:, 1024 + s * 128 : 1152 + s * 128] = line + (63 - low) * 64


def rope_tables():
    frequency = ROPE_BASE ** (-np.arange(0, 128, 2, dtype=np.float64) / 128)
    frequency = np.concatenate([frequency, frequency])
    sign = np.where(np.arange(128) < 64, -1.0, 1.0)
    inner = np.arange(64, dtype=np.float64)[:, None] * frequency
    outer = inner * 64.0
    make = lambda angles: jnp.asarray(np.stack([np.cos(angles), np.sin(angles) * sign]), F32)
    return make(inner), make(outer)


def rope_rows(inner, outer, low):
    cosines, sines = [], []
    for block in (low, 63 - low):
        cos_b, sin_b = outer[0, pl.ds(block, 1), :], outer[1, pl.ds(block, 1), :]
        cosines.append(cos_b * inner[0] - sin_b * inner[1])
        sines.append(sin_b * inner[0] + cos_b * inner[1])
    return jnp.concatenate(cosines, axis=0), jnp.concatenate(sines, axis=0)


def mean_last(value):
    return jnp.mean(value, axis=-1, keepdims=True)


def norm_scale(value):
    return lax.rsqrt(mean_last(value * value) + EPSILON)


def tile_rows(kv, j, part, start):
    return kv[j, :, part * 64 : part * 64 + 64, start : start + 128].reshape(TILE, 128)


def tile_probs(scores, masked, key_pos, query_pos, columns, shift=None):
    logits = scores * (LOG2E * SCORE_SCALE)
    if shift is not None:
        logits = logits - shift
    probs = jnp.exp2(logits)
    if masked:
        probs = jnp.where(key_pos[...] <= query_pos[0:1, columns], probs, 0.0)
    return probs


def mix_tile(me, j, part, pair, kv, query_pos, queries, key_pos, acc, total):
    key_positions(pair, me, j, part, key_pos)
    keys = tile_rows(kv, j, part, 0)
    values_t = tile_rows(kv, j, part, 128).T
    for chunk in range(4 * part, 8):
        columns = pl.ds(chunk * CHUNK, CHUNK)
        masked = part == 1 or chunk < 4
        probs = tile_probs(dot_nt(keys, queries[columns, :]), masked, key_pos, query_pos, columns)
        total[:, columns] += jnp.sum(probs.reshape(TILE // 8, 8, CHUNK), axis=0)
        acc[:, columns] += dot_nn(values_t, probs.astype(BF16))


def finish_mix(out, mixed_t, log_total, stacked, total):
    for chunk in range(8):
        columns = pl.ds(chunk * CHUNK, CHUNK)
        full = jnp.sum(total[:, columns], axis=0, keepdims=True)
        log_total[:, columns] = jnp.broadcast_to(jnp.log2(full), (8, CHUNK))
        mixed = mixed_t[:, columns] / full
        mixed_t[:, columns] = mixed
        stacked[columns, :] = mixed.T.astype(BF16)
    for s in range(8):
        unstack_heads(stacked, s, out)


def grad_tile(
    me, j, part, pair, kv, query_pos, queries, cots, deltas, log_total, key_pos, probs_all, score_cots, acc, dkv
):
    key_positions(pair, me, j, part, key_pos)
    keys = tile_rows(kv, j, part, 0)
    values = tile_rows(kv, j, part, 128)
    keys_t = keys.T
    key_cot, value_cot = 0.0, 0.0
    for first in range(part, 2):
        for chunk in range(4 * first, 4 * first + 4):
            columns = pl.ds(chunk * CHUNK, CHUNK)
            local = pl.ds((chunk - 4 * first) * CHUNK, CHUNK)
            masked = part == first
            scores = dot_nt(keys, queries[columns, :])
            prob_cot = dot_nt(values, cots[columns, :])
            probs = tile_probs(scores, masked, key_pos, query_pos, columns, log_total[0:1, columns])
            score_cot = (probs * (prob_cot - deltas[0:1, columns])).astype(BF16)
            probs_all[:, local] = probs.astype(BF16)
            score_cots[:, local] = score_cot
            acc[:, columns] += dot_nn(keys_t, score_cot)
        rows = pl.ds(1024 * first, 1024)
        key_cot = key_cot + dot_nn(score_cots[...], queries[rows, :])
        value_cot = value_cot + dot_nn(probs_all[...], cots[rows, :])
    key_cot = key_cot * SCORE_SCALE
    at = part * 64
    dkv[j, :, at : at + 64, 0:128] = key_cot.astype(BF16).reshape(8, 64, 128)
    dkv[j, :, at : at + 64, 128:256] = value_cot.astype(BF16).reshape(8, 64, 128)


def start_grad(rows, mixed_t, cots_in, queries, cots, deltas, acc):
    stack_heads(lambda s: rows[s, :, :256], queries)
    stack_heads(lambda s: cots_in[s], cots)
    for chunk in range(8):
        columns = pl.ds(chunk * CHUNK, CHUNK)
        product = cots[columns, :].astype(F32).T * mixed_t[:, columns]
        deltas[:, columns] = jnp.broadcast_to(jnp.sum(product, axis=0, keepdims=True), (8, CHUNK))
    acc[...] = jnp.zeros_like(acc)


def head_columns(head):
    return (
        (pl.ds(pl.multiple_of(head * 256, 256), 256), pl.ds(0, 256)),
        (pl.ds(pl.multiple_of(head * 128, 128), 128), pl.ds(256, 128)),
        (pl.ds(pl.multiple_of(head * 128, 128), 128), pl.ds(384, 128)),
    )


def project_rows(s, low, xs, heads_w, inner, outer, query_gain, key_gain, raw, rows):
    product = dot_nn(xs[s], heads_w[...].reshape(1024, 512))
    cosine, sine = rope_rows(inner, outer, low)
    raw[s] = product[:, :384]
    for i, gain in enumerate((query_gain, query_gain, key_gain)):
        value = product[:, i * 128 : i * 128 + 128]
        value = value * norm_scale(value) * gain[...]
        value = value * cosine + pltpu.roll(value, 64, 1) * sine
        rows[s, :, i * 128 : i * 128 + 128] = value.astype(BF16)
    rows[s, :, 384:] = product[:, 384:].astype(BF16)


def forward_body(
    pair, x, attn_gain, query_gain, key_gain, inner, outer, *refs
):
    shards, refs = refs[:7], refs[7:]
    (attn_out, rows, raw, kv, mixed_t, log_total), refs = refs[:6], refs[6:]
    full, refs = refs[:7], refs[7:]
    (
        xs, heads_w, queries, stacked, query_pos, key_pos, total, mixed,
        x_send, x_recv, w_send, w_recv, w_load, kv_send, kv_recv, back_send, back_recv,
    ), scratch = refs[:17], refs[17:]
    me = here()
    head = group_head(me)
    twin, across = me.sibling(), me.across()
    across_twin = across.sibling()
    others = [me.move(b=ring(me.b, d)) for d in (1, 2, 3)]
    along = [me.move(a=ring(me.a, d)) for d in (1, 2, 3)]
    z_low = me.move(zl=1 - me.zl)
    greet([twin, across, across_twin] + group_neighbours(me))
    start, spread_own, turns, finish = gather_turns(me, shards, full, scratch)
    turns = list(turns)

    def step():
        if turns:
            turns.pop(0)()

    x_wire = Wire(x_send, x_recv, twin)
    w_wire = Wire(w_send, w_recv, twin)
    kv_wire = Wire(kv_send, kv_recv, twin)
    back_wire = Wire(back_send, back_recv, twin)
    mine = me.zh * 2 + me.core
    qkv_shards = shards[3:6]
    loads = []
    for i, (source, target) in enumerate(head_columns(head)):
        load = pltpu.make_async_copy(qkv_shards[i].at[:, source], heads_w.at[mine, :, target], w_load.at[i])
        load.start()
        loads.append(load)
    for t, spot in enumerate((across, across_twin, twin)):
        for i, (source, target) in enumerate(head_columns(group_head(spot))):
            w_wire.push((t, i), qkv_shards[i].at[:, source], heads_w.at[mine, :, target], spot)
    inputs = x[...].astype(F32)
    xs[head] = (inputs * norm_scale(inputs) * attn_gain[...]).astype(BF16)
    x_wire.push(3, xs.at[head], xs.at[head], z_low)
    for d in (1, 3, 2):
        x_wire.push(d - 1, xs.at[head], xs.at[head], along[d - 1])
    start()
    query_positions(pair, me, query_pos)
    mixed_t[...] = jnp.zeros_like(mixed_t)
    total[...] = jnp.zeros_like(total)
    low_head = me.a + 4 * (1 - me.zl)
    x_wire.take(3, xs.at[low_head])
    for d in (1, 3, 2):
        x_wire.push(3 + d, xs.at[low_head], xs.at[low_head], along[d - 1])
    spread_own()
    for load in loads:
        load.wait()
    for t, f in enumerate(
        ((1 - me.zh) * 2 + me.core, (1 - me.zh) * 2 + 1 - me.core, me.zh * 2 + 1 - me.core)
    ):
        for i, (_, target) in enumerate(head_columns(head)):
            w_wire.take((t, i), heads_w.at[f, :, target])
    arrivals = [(None, head), (None, low_head)]
    for zl, first in ((me.zl, 0), (1 - me.zl, 4)):
        for d in (1, 3, 2):
            arrivals.append((first + d - 1, ring(me.a, -d) + 4 * zl))
    for k, (slot, s) in enumerate(arrivals):
        if slot is not None:
            x_wire.take(slot, xs.at[s])
        project_rows(
            s, low_block(pair, me, me.b, s), xs, heads_w, inner, outer, query_gain, key_gain, raw, rows
        )
        for d in range(3):
            kv_wire.push((k, d), rows.at[s, :, pl.ds(256, 256)], kv.at[me.b, s], others[d])
        kv[me.b, s] = rows[s, :, 256:]
        step()
    stack_heads(lambda s: rows[s, :, :256], queries)
    for d in (0, 1, 3, 2):
        j = ring(me.b, -d)
        if d:
            for k, (_, s) in enumerate(arrivals):
                kv_wire.take((k, d - 1), kv.at[j, s])
        for part in range(2):
            mix_tile(me, j, part, pair, kv, query_pos, queries, key_pos, mixed_t, total)
            step()
    finish_mix(mixed, mixed_t, log_total, stacked, total)

    def place(origin):
        return attn_out.at[:, pl.ds(pl.multiple_of(origin * 256, 256), 256)]

    for k in range(1, 8):
        peer = peer_of(head, k)
        back_wire.push(k - 1, mixed.at[peer], place(head), group_spot(me, peer))
    attn_out[:, pl.ds(pl.multiple_of(head * 256, 256), 256)] = mixed[head]
    while turns:
        step()
    for k in range(7):
        back_wire.take(k, place(peer_of(head, 7 - k)))
    finish()
    for wire in (x_wire, w_wire, kv_wire, back_wire):
        wire.close()


def attention_forward(pair, x, gains, tables, weights):
    outs = pl.pallas_call(
        forward_body,
        out_shape=[
            jax.ShapeDtypeStruct((128, 2048), BF16),
            jax.ShapeDtypeStruct((8, 128, 512), BF16),
            jax.ShapeDtypeStruct((8, 128, 384), F32),
            jax.ShapeDtypeStruct((4, 8, 128, 256), BF16),
            jax.ShapeDtypeStruct((128, 2048), F32),
            jax.ShapeDtypeStruct((8, 2048), F32),
        ]
        + [jax.ShapeDtypeStruct((4,) + w.shape, w.dtype) for w in weights],
        in_specs=[SMEM] + [VMEM] * 6 + [HBM] * 7,
        out_specs=[VMEM] * 6 + [HBM] * 7,
        scratch_shapes=[
            pltpu.VMEM((8, 128, 1024), BF16),
            pltpu.VMEM((4, 256, 512), BF16),
            pltpu.VMEM((2048, 128), BF16),
            pltpu.VMEM((2048, 128), BF16),
            pltpu.VMEM((8, 2048), jnp.int32),
            pltpu.VMEM((TILE, CHUNK), jnp.int32),
            pltpu.VMEM((8, 2048), F32),
            pltpu.VMEM((8, 128, 256), BF16),
            dma(7), dma(7), dma(3, 3), dma(3, 3), dma(3), dma(8, 3), dma(8, 3), dma(7), dma(7),
        ]
        + gather_scratch(weights),
        compiler_params=comm_params(1),
        name="attention_forward",
    )(pair, x, *gains, *tables, *weights)
    return outs[:6], [whole_rows(out) for out in outs[6:]]


def whole_rows(out):
    return out.reshape(4 * out.shape[1], out.shape[2])


PAIR_TILE = 512


def half_of(ref, half):
    width = ref.shape[-1] // 2
    return ref.at[:, :, pl.ds(half * width, width)]


def add_into(target, *sources):
    for zh in range(target.shape[0]):

        @pl.loop(0, target.shape[1] // 16)
        def _(r):
            at = pl.ds(pl.multiple_of(r * 16, 16), 16)
            total = target[zh, at, :].astype(F32)
            for source in sources:
                total = total + source[zh, at, :].astype(F32)
            target[zh, at, :] = total.astype(BF16)


class PairGrad:
    def __init__(self, me, left, right, left_scratch, twin_right, grad, wire, slot):
        self.me, self.left, self.right, self.wire, self.slot = me, left, right, wire, slot
        self.landing, self.left_t = left_scratch
        self.twin_right, self.grad = twin_right, grad

    def send(self):
        me = self.me
        twin = me.sibling()
        self.wire.push(self.slot + 2, self.right, self.twin_right, twin)
        for zh in range(0 if self.left is None else 2):
            columns = pl.ds(pl.multiple_of((zh * 2 + 1 - me.core) * 256, 256), 256)
            self.wire.push(self.slot + zh, self.left.at[:, columns], self.landing.at[zh], twin)

    def multiply(self):
        me = self.me
        for zh in range(0 if self.left is None else 2):
            columns = pl.ds(pl.multiple_of((zh * 2 + me.core) * 256, 256), 256)
            self.left_t[zh * 256 : zh * 256 + 256, 0:128] = self.left[:, columns].T
            self.wire.take(self.slot + zh, self.landing.at[zh])
            self.left_t[zh * 256 : zh * 256 + 256, 128:256] = self.landing[zh].T
        self.wire.take(self.slot + 2, self.twin_right)

        @pl.loop(0, self.twin_right.shape[1] // PAIR_TILE)
        def _(t):
            columns = pl.ds(pl.multiple_of(t * PAIR_TILE, PAIR_TILE), PAIR_TILE)
            right = jnp.concatenate([self.right[:, columns], self.twin_right[:, columns]], axis=0)
            product = dot_nn(self.left_t[...], right).astype(BF16)
            self.grad[:, :, columns] = product.reshape(2, 256, PAIR_TILE)


REDUCE_SLOTS = 13


def reduce_scratch(widths, z_first):
    scratch = []
    for k, width in enumerate(widths):
        half = width // 2
        if k in z_first:
            shapes = [
                (1, 128, half), (1, 128, half), (1, 256, half), (1, 256, half),
                (3, 1, 64, half), (1, 64, half), (3, 1, 16, half), (1, 16, half),
            ]
        else:
            shapes = [
                (2, 64, half), (2, 64, half), (2, 64, width), (2, 64, width),
                (3, 2, 16, width), (2, 16, width), (4, 16, width), (1, 16, width),
            ]
        scratch += [pltpu.VMEM(shape, BF16) for shape in shapes]
    count = len(widths)
    return scratch + [dma(count, REDUCE_SLOTS), dma(count, REDUCE_SLOTS)]


def reduce_stages(me, grads, pieces, scratch, z_first):
    wire = Wire(scratch[-2], scratch[-1], me.sibling())
    z = me.zh * 2 + me.zl
    z_low, across, z_high = me.move(zl=1 - me.zl), me.across(), me.move(zh=1 - me.zh)

    def z_spot(step):
        far = lax.rem(z + step + 4, 4)
        return me.move(zl=lax.rem(far, 2), zh=far // 2)

    def rows(ref, i, size):
        return ref.at[:, pl.ds(pl.multiple_of(i * size, size), size)]

    def ring_stages(k, slot, ahead, behind, block, bufs, half):
        far_a, far_b, in_a, in_b = bufs

        def send():
            wire.push((k, slot), half(block(2), 0), far_a, ahead)
            wire.push((k, slot + 1), half(block(2), 1), far_b, behind)
            wire.push((k, slot + 2), half(block(1), 1), half(in_a, 1), ahead)
            wire.push((k, slot + 3), half(block(-1), 0), half(in_b, 0), behind)

        def relay():
            wire.take((k, slot), far_a)
            add_into(far_a, half(block(1), 0))
            wire.push((k, slot + 4), far_a, half(in_a, 0), ahead)
            wire.take((k, slot + 1), far_b)
            add_into(far_b, half(block(-1), 1))
            wire.push((k, slot + 5), far_b, half(in_b, 1), behind)

        def collect():
            wire.take((k, slot + 2), half(in_a, 1))
            wire.take((k, slot + 3), half(in_b, 0))
            wire.take((k, slot + 4), half(in_a, 0))
            wire.take((k, slot + 5), half(in_b, 1))
            add_into(in_a, in_b, block(0))

        return send, relay, collect

    def direct_send(k, slot, axis, size, source, land):
        position = getattr(me, axis)
        for d in (1, 3, 2):
            spot = me.move(**{axis: ring(position, d)})
            wire.push((k, slot + d - 1), rows(source, ring(position, d), size), land.at[d - 1], spot)

    def direct_sum(k, slot, axis, size, source, land, target):
        for d in (1, 3, 2):
            wire.take((k, slot + d - 1), land.at[d - 1])
        own = rows(source, getattr(me, axis), size)
        for lead in range(target.shape[0]):

            @pl.loop(0, size // 16)
            def _(r):
                at = pl.ds(pl.multiple_of(r * 16, 16), 16)
                total = own[lead, at, :].astype(F32)
                for d in range(3):
                    total = total + land[d, lead, at, :].astype(F32)
                target[lead, at, :] = total.astype(BF16)

    def plain(k):
        grad, bufs = grads[k], scratch[8 * k : 8 * k + 8]
        in_a, a_land, total, z_land = bufs[2], bufs[4], bufs[5], bufs[6]
        send, relay, collect = ring_stages(
            k, 0, me.move(b=ring(me.b, 1)), me.move(b=ring(me.b, -1)),
            lambda step: rows(grad, ring(me.b, step), 64), bufs[:4], half_of,
        )

        def third():
            collect()
            direct_send(k, 6, "a", 16, in_a, a_land)

        def fourth():
            direct_sum(k, 6, "a", 16, in_a, a_land, total)
            wire.push((k, 9), total.at[1 - me.zh], z_land.at[z], across)
            wire.push((k, 10), total.at[1 - me.zh], z_land.at[z], z_high)
            wire.push((k, 11), total.at[me.zh], z_land.at[z], z_low)
            z_land[z] = total[me.zh]

        def fifth():
            for slot, spot in ((9, across), (10, z_high), (11, z_low)):
                wire.take((k, slot), z_land.at[spot.zh * 2 + spot.zl])
            total = z_land[0].astype(F32)
            for i in range(1, 4):
                total = total + z_land[i].astype(F32)
            pieces[k][0] = total.astype(BF16)

        return [send, relay, third, fourth, fifth]

    def first_z(k):
        grad, bufs = grads[k], scratch[8 * k : 8 * k + 8]
        in_a, b_land, b_sum, a_land, a_sum = bufs[2], bufs[4], bufs[5], bufs[6], bufs[7]
        width = grad.shape[2] // 2

        def columns(ref, zl):
            return ref.at[:, :, pl.ds(pl.multiple_of(zl * width, width), width)]

        def block(step):
            far = lax.rem(z + step + 4, 4)
            return columns(grad.at[pl.ds(far // 2, 1)], lax.rem(far, 2))

        send, relay, collect = ring_stages(
            k, 0, z_spot(1), z_spot(-1), block, bufs[:4],
            lambda view, i: view.at[:, pl.ds(128 * i, 128)],
        )

        def third():
            collect()
            direct_send(k, 6, "b", 64, in_a, b_land)

        def fourth():
            direct_sum(k, 6, "b", 64, in_a, b_land, b_sum)
            direct_send(k, 9, "a", 16, b_sum, a_land)

        def fifth():
            direct_sum(k, 9, "a", 16, b_sum, a_land, a_sum)
            place = columns(pieces[k], me.zl)
            place[...] = a_sum[...]
            wire.push((k, 12), a_sum, place, z_low)

        def sixth():
            wire.take((k, 12), columns(pieces[k], 1 - me.zl))

        return [send, relay, third, fourth, fifth, sixth]

    lists = [first_z(k) if k in z_first else plain(k) for k in range(len(grads))]
    return lists, wire


def replicate_stages(me, pieces, outs, send, recv, load_sem):
    wire = Wire(send, recv, me.sibling())
    loads = {}

    def cut(k, row, rows, half=None):
        width = outs[k].shape[1] // 2
        at = pl.ds(pl.multiple_of(row, 16), rows)
        if half is None:
            return outs[k].at[at]
        return outs[k].at[at, pl.ds(half * width, width)]

    b_next, b_prev = me.move(b=ring(me.b, 1)), me.move(b=ring(me.b, -1))

    def a_row(step):
        return (me.b * 4 + ring(me.a, step)) * 16

    def b_row(step):
        return ring(me.b, step) * 64

    def a_send(k):
        place = cut(k, a_row(0), 16)
        for d in (1, 3, 2):
            wire.push((k, d - 1), pieces[k].at[0], place, me.move(a=ring(me.a, d)))
        loads[k] = pltpu.make_async_copy(pieces[k].at[0], place, load_sem.at[k])
        loads[k].start()

    def b_send(k):
        for d in (1, 3, 2):
            wire.take((k, d - 1), cut(k, a_row(-d), 16))
        loads[k].wait()
        mine = cut(k, b_row(0), 64)
        wire.push((k, 4), mine, mine, b_next)
        wire.push((k, 5), mine, mine, b_prev)

    def b_relay(k):
        wire.take((k, 4), cut(k, b_row(-1), 64))
        wire.push((k, 6), cut(k, b_row(-1), 64, 0), cut(k, b_row(-1), 64, 0), b_next)
        wire.take((k, 5), cut(k, b_row(1), 64))
        wire.push((k, 7), cut(k, b_row(1), 64, 1), cut(k, b_row(1), 64, 1), b_prev)

    def b_collect(k):
        wire.take((k, 6), cut(k, b_row(2), 64, 0))
        wire.take((k, 7), cut(k, b_row(2), 64, 1))

    stages = (a_send, b_send, b_relay, b_collect)
    lists = [[functools.partial(stage, k) for stage in stages] for k in range(len(pieces))]
    return lists, wire


class Plan:
    def __init__(self, **lists):
        self.lists = {name: list(stages) for name, stages in lists.items()}

    def run(self, names):
        for name in names:
            self.lists[name].pop(0)()

    def check(self):
        assert not any(self.lists.values())


def gain_turns(me, gains, gains_out, gain_slots, gain_send, gain_recv):
    first = me.core == 0
    x, y = jnp.where(first, me.a, me.b), jnp.where(first, me.b, me.a)
    z = me.zh * 2 + me.zl
    wire = Wire(gain_send, gain_recv, me.sibling())

    def pick(d, on_x):
        use_a = first if on_x else jnp.logical_not(first)
        return me.move(
            a=jnp.where(use_a, ring(me.a, d), me.a), b=jnp.where(use_a, me.b, ring(me.b, d))
        )

    def z_spot(d):
        far = lax.rem(z + d, 4)
        return me.move(zl=lax.rem(far, 2), zh=far // 2)

    def push(stage, position, spots):
        for d, spot in enumerate(spots):
            slot = gain_slots.at[stage, position]
            wire.push((stage, d), slot, slot, spot)

    def take(stage, position, size):
        for d in range(size - 1):
            wire.take((stage, d), gain_slots.at[stage, lax.rem(position + size - 1 - d, size)])

    def total(stage):
        return (gain_slots[stage, 0] + gain_slots[stage, 1]) + (gain_slots[stage, 2] + gain_slots[stage, 3])

    def turn0():
        gain_slots[0, me.core] = gains[...]
        push(0, me.core, [me.sibling()])

    def turn1():
        take(0, me.core, 2)
        gain_slots[1, x] = gain_slots[0, 0] + gain_slots[0, 1]
        push(1, x, [pick(d, True) for d in (1, 2, 3)])

    def turn2():
        take(1, x, 4)
        gain_slots[2, y] = total(1)
        push(2, y, [pick(d, False) for d in (1, 2, 3)])

    def turn3():
        take(2, y, 4)
        gain_slots[3, z] = total(2)
        push(3, z, [z_spot(d) for d in (1, 2, 3)])

    def turn4():
        take(3, z, 4)
        gains_out[...] = total(3)

    return [turn0, turn1, turn2, turn3, turn4], wire.close


def unrope(s, low, grads, raw, inner, outer, gain, column, gain_part):
    cosine, sine = rope_rows(inner, outer, low)
    value = raw[s, :, column : column + 128]
    scale = norm_scale(value)
    hat = value * scale
    hat_cot = grads * cosine - pltpu.roll(grads, 64, 1) * sine
    gain_part[...] += jnp.sum((hat_cot * hat).reshape(16, 8, 128), axis=0)
    scaled = hat_cot * gain[...]
    return (scale * (scaled - hat * mean_last(scaled * hat))).astype(BF16)


WIDTHS = (3072, 3072, 3072, 2048, 2048, 2048)
Z_FIRST = (2, 3, 4)
BETWEEN = {
    "cots": "ddgguoou",
    "tiles": "dg",
    "own tile": "",
    "rows 2": "",
    "rows 4": "",
    "rows 6": "",
    "rows 0": "guodug",
    "proj": "qdkkoukdquugoddkqugok",
    "weights": "d",
    "input": "qkkousdsqgoksqqqdsogqkgoqsuoqk",
}


def backward_body(*refs):
    (
        pair, x, attn_gain, query_gain, key_gain, inner, outer, rows, raw, kv, mixed_t, log_total, parts,
        mlp_in, down_cot, branch_cot, gate_cot, up_cot, hidden, attn_out, middle_cot, mlp_gain_part, wq, wk, wv,
    ), refs = refs[:25], refs[25:]
    (input_cot, gains_out), outs, refs = refs[:2], refs[2:8], refs[8:]
    (
        cots_in, dkv, queries, cots, deltas, query_pos, key_pos, probs_all, score_cots, acc, held, stacked, message,
        attn_in, proj, head_gains, gains, gain_slots,
        cot_send, cot_recv, p_send, p_recv, m_send, m_recv, w_send, w_recv, out_send, out_recv, out_load, w_load,
        gain_send, gain_recv,
    ), refs = refs[:32], refs[32:]
    pieces, grads, refs = refs[:6], list(refs[6:11]), refs[11:]
    grads.append(grads[2].at[:, :, pl.ds(0, WIDTHS[5])])
    me = here()
    head = group_head(me)
    twin = me.sibling()
    others = [me.move(b=ring(me.b, d)) for d in (1, 2, 3)]
    greet([twin, me.across(), me.move(zh=1 - me.zh)] + group_neighbours(me))
    cot_wire = Wire(cot_send, cot_recv, twin)
    p_wire = Wire(p_send, p_recv, twin)
    m_wire = Wire(m_send, m_recv, twin)
    w_wire = Wire(w_send, w_recv, twin)

    def of_head(ref, h):
        return ref.at[:, pl.ds(pl.multiple_of(h * 256, 256), 256)]

    for k in range(1, 8):
        peer = peer_of(head, k)
        cot_wire.push(k - 1, of_head(parts, peer), cots_in.at[head], group_spot(me, peer))
    lefts = (mlp_in, None, down_cot, branch_cot, attn_in, None)
    rights = (
        gate_cot, up_cot, hidden, attn_out, proj.at[:, pl.ds(0, 2048)], proj.at[:, pl.ds(2048, 2048)]
    )
    held_lefts, twin_rights, refs = refs[:8], refs[8:14], refs[14:]
    pairs = []
    for i, share in enumerate((0, 0, 1, 2, 3, 3)):
        pairs.append(
            PairGrad(
                me, lefts[i], rights[i], held_lefts[2 * share : 2 * share + 2], twin_rights[i], grads[i], w_wire, 3 * i
            )
        )
    sums, sum_wire = reduce_stages(me, grads, pieces, refs, Z_FIRST)
    copies, out_wire = replicate_stages(me, pieces, outs, out_send, out_recv, out_load)
    small, gain_finish = gain_turns(me, gains, gains_out, gain_slots, gain_send, gain_recv)
    plan = Plan(s=small, **{
        name: [pairs[i].multiply] + sums[i] + copies[i] for i, name in enumerate("gudoqk")
    })
    for i in (2, 0, 1, 3):
        pairs[i].send()
    query_positions(pair, me, query_pos)
    cots_in[head] = parts[:, pl.ds(pl.multiple_of(head * 256, 256), 256)]
    head_gains[...] = jnp.zeros_like(head_gains)
    inputs = x[...].astype(F32)
    scale = norm_scale(inputs)
    normed = inputs * scale
    attn_in[...] = (normed * attn_gain[...]).astype(BF16)
    plan.run(BETWEEN["cots"])
    for k in range(7):
        cot_wire.take(k, cots_in.at[peer_of(head, 7 - k)])
    start_grad(rows, mixed_t, cots_in, queries, cots, deltas, acc)
    for d in (2, 1, 3, 0):
        j = ring(me.b, d)
        if d == 0:
            plan.run(BETWEEN["tiles"])
        for part in range(2):
            grad_tile(
                me, j, part, pair, kv, query_pos, queries, cots, deltas, log_total, key_pos,
                probs_all, score_cots, acc, dkv,
            )
        if d:
            for k in range(8):
                peer = peer_of(head, k)
                p_wire.push((k, d - 1), dkv.at[j, peer], held.at[d - 1, peer], others[d - 1])
    for chunk in range(8):
        columns = pl.ds(chunk * CHUNK, CHUNK)
        stacked[columns, :] = (acc[:, columns] * SCORE_SCALE).T
    plan.run(BETWEEN["own tile"])

    def places(h):
        return (
            (pl.ds(0, 256), pl.ds(pl.multiple_of(h * 256, 256), 256)),
            (pl.ds(256, 128), pl.ds(pl.multiple_of(2048 + h * 128, 128), 128)),
            (pl.ds(384, 128), pl.ds(pl.multiple_of(3072 + h * 128, 128), 128)),
        )

    for k in (1, 2, 3, 4, 5, 6, 7, 0):
        s = peer_of(head, k)
        low = low_block(pair, me, me.b, s)
        for d in range(3):
            p_wire.take((k, d), held.at[d, s])
        for h in range(2):
            turned = jnp.concatenate(
                [
                    stacked[pl.ds(pl.multiple_of(part * 1024 + s * 128 + h * 64, 64), 64), :]
                    for part in range(2)
                ],
                axis=0,
            )
            message[s, :, h * 128 : h * 128 + 128] = unrope(
                s, low, turned, raw, inner, outer, query_gain, h * 128, head_gains.at[0]
            )
        total = (
            dkv[me.b, s].astype(F32)
            + held[0, s].astype(F32)
            + held[1, s].astype(F32)
            + held[2, s].astype(F32)
        )
        message[s, :, 256:384] = unrope(
            s, low, total[:, :128], raw, inner, outer, key_gain, 256, head_gains.at[1]
        )
        message[s, :, 384:] = total[:, 128:].astype(BF16)
        if k:
            for i, (source, target) in enumerate(places(head)):
                m_wire.push((k - 1, i), message.at[s, :, source], proj.at[:, target], group_spot(me, s))
        if k % 2 == 0:
            plan.run(BETWEEN[f"rows {k}"])
    for source, target in places(head):
        proj[:, target] = message[head, :, source]
    for k in range(7):
        for i, (_, target) in enumerate(places(peer_of(head, 7 - k))):
            m_wire.take((k, i), proj.at[:, target])
    for i in (4, 5):
        pairs[i].send()
    for k in range(3):
        sum_wire.settle(k)
    plan.run(BETWEEN["proj"])

    loads = []
    value_rows = (score_cots, probs_all)
    for i in range(4):
        at = pl.ds(256 * i, 256)
        target = grads[i // 2].at[i % 2]
        loads.append((wq.at[at], target.at[:, pl.ds(0, 2048)]))
        loads.append((wk.at[at], target.at[:, pl.ds(2048, 1024)]))
        loads.append((wv.at[at], value_rows[i // 2].at[pl.ds(i % 2 * 256, 256)]))
    loads = [pltpu.make_async_copy(*pair_, w_load.at[i]) for i, pair_ in enumerate(loads)]
    for load in loads:
        load.start()
    plan.run(BETWEEN["weights"])
    for load in loads:
        load.wait()
    attn_in_cot = jnp.concatenate(
        [
            dot_nt(proj[:, :3072], grads[i // 2][i % 2])
            + dot_nt(proj[:, 3072:], value_rows[i // 2][i % 2 * 256 : i % 2 * 256 + 256, :])
            for i in range(4)
        ],
        axis=1,
    )
    scaled = attn_in_cot * attn_gain[...]
    input_cot[...] = middle_cot[...] + scale * (scaled - normed * mean_last(scaled * normed))
    gains[...] = jnp.zeros_like(gains)
    gains[0:1, :] = jnp.sum(attn_in_cot * normed, axis=0, keepdims=True)
    gains[1:2, :] = mlp_gain_part[...]
    for i in range(2):
        gains[2 + i : 3 + i, 0:128] = jnp.sum(head_gains[i], axis=0, keepdims=True)
    plan.run(BETWEEN["input"])
    plan.check()
    gain_finish()
    for wire in (cot_wire, p_wire, m_wire, w_wire, sum_wire, out_wire):
        wire.close()


def attention_backward(pair, x, gains, tables, kept, attended_cot, lefts, rights, middle_cot, mlp_gain_part, weights):
    heads = (8, 128, 256)
    count = len(WIDTHS)
    outs = pl.pallas_call(
        backward_body,
        out_shape=[jax.ShapeDtypeStruct((128, 1024), F32), jax.ShapeDtypeStruct((4, 1024), F32)]
        + [jax.ShapeDtypeStruct((256, width), BF16) for width in WIDTHS],
        in_specs=[SMEM] + [VMEM] * 21 + [HBM] * 3,
        out_specs=[VMEM] * 2 + [HBM] * count,
        scratch_shapes=[
            pltpu.VMEM(heads, BF16),
            pltpu.VMEM((4,) + heads, BF16),
            pltpu.VMEM((2048, 128), BF16),
            pltpu.VMEM((2048, 128), BF16),
            pltpu.VMEM((8, 2048), F32),
            pltpu.VMEM((8, 2048), jnp.int32),
            pltpu.VMEM((TILE, CHUNK), jnp.int32),
            pltpu.VMEM((TILE, 1024), BF16),
            pltpu.VMEM((TILE, 1024), BF16),
            pltpu.VMEM((128, 2048), F32),
            pltpu.VMEM((3,) + heads, BF16),
            pltpu.VMEM((2048, 128), F32),
            pltpu.VMEM((8, 128, 512), BF16),
            pltpu.VMEM((128, 1024), BF16),
            pltpu.VMEM((128, 4096), BF16),
            pltpu.VMEM((2, 8, 128), F32),
            pltpu.VMEM((4, 1024), F32),
            pltpu.VMEM((4, 4, 4, 1024), F32),
            dma(7), dma(7), dma(8, 3), dma(8, 3), dma(7, 3), dma(7, 3), dma(18), dma(18),
            dma(count, 8), dma(count, 8), dma(count), dma(12), dma(4, 3), dma(4, 3),
        ]
        + [pltpu.VMEM((1, 16, width), BF16) for width in WIDTHS]
        + [pltpu.VMEM((2, 256, width), BF16) for width in WIDTHS[:5]]
        + [pltpu.VMEM((2, 128, 256), BF16), pltpu.VMEM((512, 256), BF16)] * 4
        + [pltpu.VMEM((128, width), BF16) for width in WIDTHS]
        + reduce_scratch(WIDTHS, Z_FIRST),
        compiler_params=comm_params(2, 62 * 1024 * 1024),
        name="attention_backward",
    )(pair, x, *gains, *tables, *kept, attended_cot, *lefts, *rights, middle_cot, mlp_gain_part, *weights)
    return outs[0], outs[1], outs[2:]


FF_TILE = 512


def feed_body(
    x, attn_out, down_cot, gain, w_out, w_gate, w_up, w_down,
    result, mlp_in, gate_cot, up_cot, hidden, branch_cot, middle_cot, attended_cot, gain_part,
    middle, total, cot_total,
):
    step = pl.program_id(0)

    @pl.when(step == 0)
    def _():
        value = x[...].astype(F32) + dot_nt(attn_out[...], w_out[...])
        middle[...] = value
        total[...] = value
        mlp_in[...] = (value * norm_scale(value) * gain[...]).astype(BF16)
        cot_total[...] = jnp.zeros_like(cot_total)

    gate = dot_nn(mlp_in[...], w_gate[...])
    up = dot_nn(mlp_in[...], w_up[...])
    sigmoid = jax.nn.sigmoid(gate)
    silu = gate * sigmoid
    hidden_tile = (silu * up).astype(BF16)
    hidden[...] = hidden_tile
    total[...] += dot_nt(hidden_tile, w_down[...])
    hidden_cot = dot_nn(down_cot[...], w_down[...])
    gate_tile = (hidden_cot * up * sigmoid * (1.0 + gate * (1.0 - sigmoid))).astype(BF16)
    up_tile = (hidden_cot * silu).astype(BF16)
    gate_cot[...] = gate_tile
    up_cot[...] = up_tile
    cot_total[...] += dot_nt(gate_tile, w_gate[...]) + dot_nt(up_tile, w_up[...])

    @pl.when(step == pl.num_programs(0) - 1)
    def _():
        result[...] = total[...].astype(BF16)
        value = middle[...]
        scale = norm_scale(value)
        normed = value * scale
        mlp_in_cot = cot_total[...]
        gain_part[...] = jnp.sum(mlp_in_cot * normed, axis=0, keepdims=True)
        scaled = mlp_in_cot * gain[...]
        cot = down_cot[...].astype(F32) + scale * (scaled - normed * mean_last(scaled * normed))
        middle_cot[...] = cot
        branch_cot[...] = cot.astype(BF16)
        attended_cot[...] = dot_nn(cot.astype(BF16), w_out[...]).astype(BF16)


def feed_forward(x, attn_out, down_cot, gain, w_out, w_gate, w_up, w_down):
    steps = w_gate.shape[1] // FF_TILE
    wide = jax.ShapeDtypeStruct((128, w_gate.shape[1]), BF16)
    narrow = jax.ShapeDtypeStruct((128, 1024), BF16)
    whole = lambda shape: pl.BlockSpec(shape, lambda t: (0, 0))
    weight = pl.BlockSpec((1024, FF_TILE), lambda t: (0, t))
    tile = pl.BlockSpec((128, FF_TILE), lambda t: (0, t))
    return pl.pallas_call(
        feed_body,
        grid=(steps,),
        out_shape=[
            narrow, narrow, wide, wide, wide, narrow,
            jax.ShapeDtypeStruct((128, 1024), F32),
            jax.ShapeDtypeStruct((128, 2048), BF16),
            jax.ShapeDtypeStruct((1, 1024), F32),
        ],
        in_specs=[
            whole((128, 1024)), whole((128, 2048)), whole((128, 1024)), whole((1, 1024)), whole((1024, 2048)),
            weight, weight, weight,
        ],
        out_specs=[
            whole((128, 1024)), whole((128, 1024)), tile, tile, tile, whole((128, 1024)),
            whole((128, 1024)), whole((128, 2048)), whole((1, 1024)),
        ],
        scratch_shapes=[pltpu.VMEM((128, 1024), F32)] * 3,
        compiler_params=pltpu.CompilerParams(vmem_limit_bytes=VMEM_LIMIT),
        name="feed_forward",
    )(x, attn_out, down_cot, gain, w_out, w_gate, w_up, w_down)


def shards(
    tokens,
    query_weight,
    key_weight,
    value_weight,
    out_weight,
    gate_weight,
    up_weight,
    down_weight,
    attn_gain,
    mlp_gain,
    query_gain,
    key_gain,
    pair_order,
    out_grad,
):
    tables = rope_tables()
    attn_row, query_row, key_row = attn_gain[None], query_gain[None], key_gain[None]
    (attn_out, *kept), full = attention_forward(
        pair_order,
        tokens[0],
        (attn_row, query_row, key_row),
        tables,
        [out_weight, gate_weight, up_weight, query_weight, key_weight, value_weight, down_weight],
    )
    full_out, full_gate, full_up, *full_qkv, full_down = full

    down_cot = out_grad[0]
    result, mlp_in, gate_cot, up_cot, hidden, branch_cot, middle_cot, attended_cot, mlp_gain_part = feed_forward(
        tokens[0], attn_out, down_cot, mlp_gain[None], full_out, full_gate, full_up, full_down
    )
    input_cot, gains, grads = attention_backward(
        pair_order,
        tokens[0],
        (attn_row, query_row, key_row),
        tables,
        kept,
        attended_cot,
        (mlp_in, down_cot, branch_cot),
        (gate_cot, up_cot, hidden, attn_out),
        middle_cot,
        mlp_gain_part,
        full_qkv,
    )
    gate, up, down, out, query, key_value = (grad.astype(F32) for grad in grads)
    return (
        result[None],
        input_cot[None],
        query,
        key_value[:, :1024],
        key_value[:, 1024:],
        out,
        gate,
        up,
        down,
        gains[0],
        gains[1],
        gains[2, :128],
        gains[3, :128],
    )


def solution(mesh):
    rows, split, whole = P("fsdp", None), P("fsdp", "ctx", None), P()
    return jax.shard_map(
        shards,
        mesh=mesh,
        in_specs=(split,) + (rows,) * 7 + (whole,) * 4 + (rows, split),
        out_specs=(split, split) + (rows,) * 7 + (whole,) * 4,
        check_vma=False,
    )
```

```python
import functools

import jax
import jax.numpy as jnp
import numpy as np
from jax import lax
from jax.experimental import pallas as pl
from jax.experimental.pallas import tpu as pltpu
from jax.sharding import PartitionSpec as P

EPSILON = 1e-06
ROPE_BASE = 1000000.0
MESH = pl.DeviceIdType.MESH
HBM = pl.BlockSpec(memory_space=pltpu.HBM)
VMEM = pl.BlockSpec(memory_space=pltpu.VMEM)
SMEM = pl.BlockSpec(memory_space=pltpu.SMEM)
LOG2E = 1.4426950408889634
VMEM_LIMIT = 56 * 1024 * 1024
BF16 = jnp.bfloat16
F32 = jnp.float32


class Spot:
    def __init__(self, a, b, zl, zh, core):
        self.a, self.b, self.zl, self.zh, self.core = a, b, zl, zh, core

    def move(self, a=None, b=None, zl=None, zh=None):
        return Spot(
            self.a if a is None else a,
            self.b if b is None else b,
            self.zl if zl is None else zl,
            self.zh if zh is None else zh,
            self.core,
        )

    def id(self):
        first = self.core == 0
        x = jnp.where(first, self.a, self.b)
        y = jnp.where(first, self.b, self.a)
        return (self.zl * 16 + y * 4 + x, self.zh * 2 + self.core)

    def sibling(self):
        return Spot(self.b, self.a, self.zl, self.zh, 1 - self.core)

    def across(self):
        return self.move(zl=1 - self.zl, zh=1 - self.zh)


def here():
    ctx = lax.axis_index("ctx")
    fsdp = lax.axis_index("fsdp")
    x = lax.rem(ctx, 4)
    y = lax.rem(ctx // 4, 4)
    core = lax.rem(fsdp, 2)
    first = core == 0
    return Spot(jnp.where(first, x, y), jnp.where(first, y, x), ctx // 16, fsdp // 2, core)


def ring(position, step):
    return lax.rem(position + step + 4, 4)


def greet(spots):
    barrier = pltpu.get_barrier_semaphore()
    for spot in spots:
        pl.semaphore_signal(barrier, inc=1, device_id=spot.id(), device_id_type=MESH)
    pl.semaphore_wait(barrier, len(spots))


def remote(src, dst, send_sem, recv_sem, spot):
    return pltpu.make_async_remote_copy(
        src_ref=src,
        dst_ref=dst,
        send_sem=send_sem,
        recv_sem=recv_sem,
        device_id=spot.id(),
        device_id_type=MESH,
    )


def comm_params(collective_id, limit=VMEM_LIMIT):
    return pltpu.CompilerParams(
        collective_id=collective_id, has_side_effects=True, vmem_limit_bytes=limit
    )


class Wire:
    def __init__(self, send, recv, spot):
        self.send, self.recv, self.spot, self.sent = send, recv, spot, []

    def push(self, slot, src, dst, spot):
        copy = remote(src, dst, self.send.at[slot], self.recv.at[slot], spot)
        copy.start()
        self.sent.append((slot, copy))

    def take(self, slot, dst):
        remote(dst, dst, self.send.at[slot], self.recv.at[slot], self.spot).wait_recv()

    def settle(self, k):
        for slot, copy in self.sent:
            if slot[0] == k:
                copy.wait_send()
        self.sent = [(slot, copy) for slot, copy in self.sent if slot[0] != k]

    def close(self):
        for _, copy in self.sent:
            copy.wait_send()


def pipeline(stages, count):
    def turn(t):
        for depth, stage in enumerate(stages):
            if 0 <= t - depth < count:
                stage(t - depth)

    return [functools.partial(turn, t) for t in range(count + len(stages) - 1)]


GATHER_SLOTS = 14
FF_TILE = 512
FF_STEPS = 6


def gather_scratch(weights):
    count = len(weights)
    return [pltpu.VMEM(w.shape, w.dtype) for w in weights] + [
        pltpu.SemaphoreType.DMA((count, GATHER_SLOTS)),
        pltpu.SemaphoreType.DMA((count, GATHER_SLOTS)),
        pltpu.SemaphoreType.DMA((2, count)),
    ]


def gather_turns(me, ins, outs, scratch):
    count = len(ins)
    held, (send, recv, local_sem) = scratch[:count], scratch[count:]
    mine = me.zh * 2 + me.core
    other = (1 - me.zh) * 2 + me.core
    twin_mine = me.zh * 2 + 1 - me.core
    twin_other = (1 - me.zh) * 2 + 1 - me.core
    twin, across = me.sibling(), me.across()
    a_next, a_prev = me.move(a=ring(me.a, 1)), me.move(a=ring(me.a, -1))
    b_next, b_prev = me.move(b=ring(me.b, 1)), me.move(b=ring(me.b, -1))
    wire = Wire(send, recv, twin)

    def cut(m, rows, half):
        width = ins[m].shape[1] // 2
        if half is None:
            return outs[m].at[other, rows]
        return outs[m].at[other, rows, pl.ds(half * width, width)]

    def piece(m, a, half=None):
        return cut(m, pl.ds(pl.multiple_of((me.b * 4 + a) * 16, 16), 16), half)

    def block(m, b, half=None):
        return cut(m, pl.ds(pl.multiple_of(b * 64, 64), 64), half)

    def push(m, slot, src, dst, spot):
        wire.push((m, slot), src, dst, spot)

    def take(m, slot, dst):
        wire.take((m, slot), dst)

    loads = [pltpu.make_async_copy(ins[m], held[m], local_sem.at[0, m]) for m in range(count)]
    stores = [pltpu.make_async_copy(held[m], outs[m].at[mine], local_sem.at[1, m]) for m in range(count)]

    last = count - 1

    def start():
        for m in range(last):
            rows = pl.ds(pl.multiple_of((me.b * 4 + me.a) * 16, 16), 16)
            push(m, 0, ins[m].at[rows], outs[m].at[mine, rows], across)
        for t in range(FF_STEPS):
            columns = pl.ds(FF_TILE * t, FF_TILE)
            push(last, t, ins[last].at[:, columns], outs[last].at[mine, :, columns], across)
        for load in loads:
            load.start()

    def spread_own():
        for m in range(count):
            loads[m].wait()
            stores[m].start()
            push(m, 2 * FF_STEPS if m == last else 9, ins[m], outs[m].at[mine], twin)

    def stage_z(m):
        take(m, 0, piece(m, me.a))
        push(m, 1, piece(m, me.a), piece(m, me.a), a_next)
        push(m, 2, piece(m, me.a), piece(m, me.a), a_prev)

    def stage_a(m):
        left, right = ring(me.a, -1), ring(me.a, 1)
        take(m, 1, piece(m, left))
        push(m, 3, piece(m, left, 0), piece(m, left, 0), a_next)
        take(m, 2, piece(m, right))
        push(m, 4, piece(m, right, 1), piece(m, right, 1), a_prev)

    def stage_b(m):
        far = ring(me.a, 2)
        take(m, 3, piece(m, far, 0))
        take(m, 4, piece(m, far, 1))
        push(m, 5, block(m, me.b), block(m, me.b), b_next)
        push(m, 6, block(m, me.b), block(m, me.b), b_prev)
        push(m, 10, block(m, me.b), block(m, me.b), twin)

    def stage_c(m):
        left, right = ring(me.b, -1), ring(me.b, 1)
        take(m, 5, block(m, left))
        push(m, 7, block(m, left, 0), block(m, left, 0), b_next)
        push(m, 11, block(m, left), block(m, left), twin)
        take(m, 6, block(m, right))
        push(m, 8, block(m, right, 1), block(m, right, 1), b_prev)
        push(m, 12, block(m, right), block(m, right), twin)

    def stage_d(m):
        far = ring(me.b, 2)
        take(m, 7, block(m, far, 0))
        take(m, 8, block(m, far, 1))
        push(m, 13, block(m, far), block(m, far), twin)

    def pass_tile(t):
        tile = outs[last].at[other, :, pl.ds(FF_TILE * t, FF_TILE)]
        take(last, t, tile)
        push(last, FF_STEPS + t, tile, tile, twin)

    def finish_tile(t):
        take(last, FF_STEPS + t, outs[last].at[twin_other, :, pl.ds(FF_TILE * t, FF_TILE)])

    def finish(m):
        take(m, 2 * FF_STEPS if m == last else 9, outs[m].at[twin_mine])
        stores[m].wait()
        if m < last:
            for slot, step in ((10, 0), (11, -1), (12, 1), (13, 2)):
                rows = pl.ds(pl.multiple_of(ring(me.a, step) * 64, 64), 64)
                take(m, slot, outs[m].at[twin_other, rows])

    turns = pipeline((stage_z, stage_a, stage_b, stage_c, stage_d), last)
    return start, spread_own, turns, pass_tile, finish_tile, finish, wire


def group_spot(me, head):
    return me.move(a=lax.rem(head, 4), zl=head // 4)


def group_head(me):
    return me.a + 4 * me.zl


def peer_of(head, k):
    return lax.rem(head + k, 8)


def group_neighbours(me):
    head = group_head(me)
    return [group_spot(me, peer_of(head, k)) for k in range(1, 8)] + [
        me.move(b=ring(me.b, d)) for d in (1, 2, 3)
    ]


def dma(*shape):
    return pltpu.SemaphoreType.DMA(shape)


TILE = 512
CHUNK = 256
SCORE_SCALE = 128.0**-0.5


def dot_nt(left, right):
    return lax.dot_general(left, right, (((1,), (1,)), ((), ())), preferred_element_type=F32)


def dot_nn(left, right):
    return lax.dot_general(left, right, (((1,), (0,)), ((), ())), preferred_element_type=F32)


def stack_heads(read, target):
    for s in range(8):
        rows = read(s)
        for part in range(2):
            for head in range(2):
                at = part * 1024 + s * 128 + head * 64
                target[at : at + 64, :] = rows[part * 64 : part * 64 + 64, head * 128 : head * 128 + 128]


def unstack_heads(stacked, s, out):
    for part in range(2):
        for head in range(2):
            at = part * 1024 + s * 128 + head * 64
            out[s, part * 64 : part * 64 + 64, head * 128 : head * 128 + 128] = stacked[at : at + 64, :]


def low_block(pair, me, j, s):
    a = lax.rem(s, 4)
    first = me.core == 0
    return pair[0, (s // 4) * 16 + jnp.where(first, j * 4 + a, a * 4 + j)]


def key_positions(pair, me, j, part, target):
    line = lax.broadcasted_iota(jnp.int32, (64, CHUNK), 0)
    for s in range(8):
        low = low_block(pair, me, j, s)
        block = low if part == 0 else 63 - low
        target[s * 64 : s * 64 + 64, :] = line + block * 64


def query_positions(pair, me, target):
    line = lax.rem(lax.broadcasted_iota(jnp.int32, (8, 128), 1), 64)
    for s in range(8):
        low = low_block(pair, me, me.b, s)
        target[:, s * 128 : s * 128 + 128] = line + low * 64
        target[:, 1024 + s * 128 : 1152 + s * 128] = line + (63 - low) * 64


def rope_tables():
    frequency = ROPE_BASE ** (-np.arange(0, 128, 2, dtype=np.float64) / 128)
    frequency = np.concatenate([frequency, frequency])
    sign = np.where(np.arange(128) < 64, -1.0, 1.0)
    inner = np.arange(64, dtype=np.float64)[:, None] * frequency
    outer = inner * 64.0
    make = lambda angles: jnp.asarray(np.stack([np.cos(angles), np.sin(angles) * sign]), F32)
    return make(inner), make(outer)


def rope_rows(inner, outer, low):
    cosines, sines = [], []
    for block in (low, 63 - low):
        cos_b, sin_b = outer[0, pl.ds(block, 1), :], outer[1, pl.ds(block, 1), :]
        cosines.append(cos_b * inner[0] - sin_b * inner[1])
        sines.append(sin_b * inner[0] + cos_b * inner[1])
    return jnp.concatenate(cosines, axis=0), jnp.concatenate(sines, axis=0)


def mean_last(value):
    return jnp.mean(value, axis=-1, keepdims=True)


def norm_scale(value):
    return lax.rsqrt(mean_last(value * value) + EPSILON)


def tile_rows(kv, j, part, start):
    return kv[j, :, part * 64 : part * 64 + 64, start : start + 128].reshape(TILE, 128)


def tile_probs(scores, masked, key_pos, query_pos, columns, shift=None):
    logits = scores * (LOG2E * SCORE_SCALE)
    if shift is not None:
        logits = logits - shift
    probs = jnp.exp2(logits)
    if masked:
        probs = jnp.where(key_pos[...] <= query_pos[0:1, columns], probs, 0.0)
    return probs


def mix_tile(me, j, part, pair, kv, query_pos, queries, key_pos, acc, total):
    key_positions(pair, me, j, part, key_pos)
    keys = tile_rows(kv, j, part, 0)
    values_t = tile_rows(kv, j, part, 128).T
    for chunk in range(4 * part, 8):
        columns = pl.ds(chunk * CHUNK, CHUNK)
        masked = part == 1 or chunk < 4
        probs = tile_probs(dot_nt(keys, queries[columns, :]), masked, key_pos, query_pos, columns)
        total[:, columns] += jnp.sum(probs.reshape(TILE // 8, 8, CHUNK), axis=0)
        acc[:, columns] += dot_nn(values_t, probs.astype(BF16))


def finish_mix(out, mixed_t, log_total, stacked, total):
    for chunk in range(8):
        columns = pl.ds(chunk * CHUNK, CHUNK)
        full = jnp.sum(total[:, columns], axis=0, keepdims=True)
        log_total[:, columns] = jnp.broadcast_to(jnp.log2(full), (8, CHUNK))
        mixed = mixed_t[:, columns] / full
        mixed_t[:, columns] = mixed
        stacked[columns, :] = mixed.T.astype(BF16)
    for s in range(8):
        unstack_heads(stacked, s, out)


def grad_tile(
    me, j, part, pair, kv, query_pos, queries, cots, deltas, log_total, key_pos, probs_all, score_cots, acc, dkv
):
    key_positions(pair, me, j, part, key_pos)
    keys = tile_rows(kv, j, part, 0)
    values = tile_rows(kv, j, part, 128)
    keys_t = keys.T
    key_cot, value_cot = 0.0, 0.0
    for first in range(part, 2):
        for chunk in range(4 * first, 4 * first + 4):
            columns = pl.ds(chunk * CHUNK, CHUNK)
            local = pl.ds((chunk - 4 * first) * CHUNK, CHUNK)
            masked = part == first
            scores = dot_nt(keys, queries[columns, :])
            prob_cot = dot_nt(values, cots[columns, :])
            probs = tile_probs(scores, masked, key_pos, query_pos, columns, log_total[0:1, columns])
            score_cot = (probs * (prob_cot - deltas[0:1, columns])).astype(BF16)
            probs_all[:, local] = probs.astype(BF16)
            score_cots[:, local] = score_cot
            acc[:, columns] += dot_nn(keys_t, score_cot)
        rows = pl.ds(1024 * first, 1024)
        key_cot = key_cot + dot_nn(score_cots[...], queries[rows, :])
        value_cot = value_cot + dot_nn(probs_all[...], cots[rows, :])
    key_cot = key_cot * SCORE_SCALE
    at = part * 64
    dkv[j, :, at : at + 64, 0:128] = key_cot.astype(BF16).reshape(8, 64, 128)
    dkv[j, :, at : at + 64, 128:256] = value_cot.astype(BF16).reshape(8, 64, 128)


def start_grad(rows, mixed_t, cots_in, queries, cots, deltas, acc):
    stack_heads(lambda s: rows[s, :, :256], queries)
    stack_heads(lambda s: cots_in[s], cots)
    for chunk in range(8):
        columns = pl.ds(chunk * CHUNK, CHUNK)
        product = cots[columns, :].astype(F32).T * mixed_t[:, columns]
        deltas[:, columns] = jnp.broadcast_to(jnp.sum(product, axis=0, keepdims=True), (8, CHUNK))
    acc[...] = jnp.zeros_like(acc)


class FeedForward:
    def __init__(self, x, attn_out, down_cot, gain, outs, full, scratch):
        self.x, self.attn_out, self.down_cot, self.gain = x, attn_out, down_cot, gain
        self.outs, self.full = outs, full
        self.w_out, self.tiles, self.middle, self.total, self.cot_total, self.sems = scratch

    def out_copy(self):
        return pltpu.make_async_copy(self.full[0], self.w_out, self.sems.at[6])

    def tile_copies(self, t):
        columns = pl.ds(FF_TILE * t, FF_TILE)
        return [
            pltpu.make_async_copy(
                self.full[m].at[:, :, columns], self.tiles.at[t % 2, i], self.sems.at[t % 2 * 3 + i]
            )
            for i, m in enumerate((1, 2, 6))
        ]

    def load_out(self):
        self.out_copy().start()

    def load_tile(self, t):
        for copy in self.tile_copies(t):
            copy.start()

    def begin(self):
        self.out_copy().wait()
        value = self.x[...].astype(F32) + dot_nt(self.attn_out[...], self.w_out[...].reshape(1024, 2048))
        self.middle[...] = value
        self.total[...] = value
        self.outs[1][...] = (value * norm_scale(value) * self.gain[...]).astype(BF16)
        self.cot_total[...] = jnp.zeros_like(self.cot_total)

    def tile(self, t):
        mlp_in, gate_cot, up_cot, hidden = self.outs[1:5]
        for copy in self.tile_copies(t):
            copy.wait()
        w_gate, w_up, w_down = (self.tiles[t % 2, i].reshape(1024, FF_TILE) for i in range(3))
        gate = dot_nn(mlp_in[...], w_gate)
        up = dot_nn(mlp_in[...], w_up)
        sigmoid = jax.nn.sigmoid(gate)
        silu = gate * sigmoid
        hidden_tile = (silu * up).astype(BF16)
        hidden_cot = dot_nn(self.down_cot[...], w_down)
        gate_tile = (hidden_cot * up * sigmoid * (1.0 + gate * (1.0 - sigmoid))).astype(BF16)
        up_tile = (hidden_cot * silu).astype(BF16)
        columns = pl.ds(FF_TILE * t, FF_TILE)
        gate_cot[:, columns] = gate_tile
        up_cot[:, columns] = up_tile
        hidden[:, columns] = hidden_tile
        self.total[...] += dot_nt(hidden_tile, w_down)
        self.cot_total[...] += dot_nt(gate_tile, w_gate) + dot_nt(up_tile, w_up)

    def end(self):
        result, _, _, _, _, branch_cot, middle_cot, attended_cot, gain_part = self.outs
        result[...] = self.total[...].astype(BF16)
        value = self.middle[...]
        scale = norm_scale(value)
        normed = value * scale
        mlp_in_cot = self.cot_total[...]
        gain_part[...] = jnp.sum(mlp_in_cot * normed, axis=0, keepdims=True)
        scaled = mlp_in_cot * self.gain[...]
        cot = self.down_cot[...].astype(F32) + scale * (scaled - normed * mean_last(scaled * normed))
        middle_cot[...] = cot
        branch_cot[...] = cot.astype(BF16)
        attended_cot[...] = dot_nn(cot.astype(BF16), self.w_out[...].reshape(1024, 2048)).astype(BF16)


def head_columns(head):
    return (
        (pl.ds(pl.multiple_of(head * 256, 256), 256), pl.ds(0, 256)),
        (pl.ds(pl.multiple_of(head * 128, 128), 128), pl.ds(256, 128)),
        (pl.ds(pl.multiple_of(head * 128, 128), 128), pl.ds(384, 128)),
    )


def project_rows(s, low, xs, heads_w, inner, outer, query_gain, key_gain, raw, rows):
    product = dot_nn(xs[s], heads_w[...].reshape(1024, 512))
    cosine, sine = rope_rows(inner, outer, low)
    raw[s] = product[:, :384]
    for i, gain in enumerate((query_gain, query_gain, key_gain)):
        value = product[:, i * 128 : i * 128 + 128]
        value = value * norm_scale(value) * gain[...]
        value = value * cosine + pltpu.roll(value, 64, 1) * sine
        rows[s, :, i * 128 : i * 128 + 128] = value.astype(BF16)
    rows[s, :, 384:] = product[:, 384:].astype(BF16)


GATHER_AT = {
    "row 7": 2, "tile 00": 1, "tile 01": 1, "tile 11": 1, "tile 31": 1, "tile 21": 1,
    "feed 0": 1, "feed 2": 1, "feed 4": 1,
}


def forward_body(
    pair, x, attn_gain, query_gain, key_gain, inner, outer, down_cot, mlp_gain, *refs
):
    shards, refs = refs[:7], refs[7:]
    (attn_out, rows, raw, kv, mixed_t, log_total), refs = refs[:6], refs[6:]
    feed_outs, refs = refs[:9], refs[9:]
    full, refs = refs[:7], refs[7:]
    feed_scratch, refs = refs[:6], refs[6:]
    (
        xs, heads_w, queries, stacked, query_pos, key_pos, total, mixed,
        x_send, x_recv, w_send, w_recv, w_load, kv_send, kv_recv, back_send, back_recv,
    ), scratch = refs[:17], refs[17:]
    me = here()
    head = group_head(me)
    twin, across = me.sibling(), me.across()
    across_twin = across.sibling()
    others = [me.move(b=ring(me.b, d)) for d in (1, 2, 3)]
    along = [me.move(a=ring(me.a, d)) for d in (1, 2, 3)]
    z_low = me.move(zl=1 - me.zl)
    greet([twin, across, across_twin] + group_neighbours(me))
    start, spread_own, turns, pass_tile, finish_tile, finish, gather_wire = gather_turns(
        me, shards, full, scratch
    )
    turns = list(turns)

    def step(place):
        for _ in range(GATHER_AT.get(place, 0)):
            turns.pop(0)()

    x_wire = Wire(x_send, x_recv, twin)
    w_wire = Wire(w_send, w_recv, twin)
    kv_wire = Wire(kv_send, kv_recv, twin)
    back_wire = Wire(back_send, back_recv, twin)
    mine = me.zh * 2 + me.core
    qkv_shards = shards[3:6]
    loads = []
    for i, (source, target) in enumerate(head_columns(head)):
        load = pltpu.make_async_copy(qkv_shards[i].at[:, source], heads_w.at[mine, :, target], w_load.at[i])
        load.start()
        loads.append(load)
    for t, spot in enumerate((across, across_twin, twin)):
        for i, (source, target) in enumerate(head_columns(group_head(spot))):
            w_wire.push((t, i), qkv_shards[i].at[:, source], heads_w.at[mine, :, target], spot)
    inputs = x[...].astype(F32)
    xs[head] = (inputs * norm_scale(inputs) * attn_gain[...]).astype(BF16)
    x_wire.push(3, xs.at[head], xs.at[head], z_low)
    for d in (1, 3, 2):
        x_wire.push(d - 1, xs.at[head], xs.at[head], along[d - 1])
    start()
    query_positions(pair, me, query_pos)
    mixed_t[...] = jnp.zeros_like(mixed_t)
    total[...] = jnp.zeros_like(total)
    low_head = me.a + 4 * (1 - me.zl)
    x_wire.take(3, xs.at[low_head])
    for d in (1, 3, 2):
        x_wire.push(3 + d, xs.at[low_head], xs.at[low_head], along[d - 1])
    spread_own()
    for load in loads:
        load.wait()
    for t, f in enumerate(
        ((1 - me.zh) * 2 + me.core, (1 - me.zh) * 2 + 1 - me.core, me.zh * 2 + 1 - me.core)
    ):
        for i, (_, target) in enumerate(head_columns(head)):
            w_wire.take((t, i), heads_w.at[f, :, target])
    arrivals = [(None, head), (None, low_head)]
    for zl, first in ((me.zl, 0), (1 - me.zl, 4)):
        for d in (1, 3, 2):
            arrivals.append((first + d - 1, ring(me.a, -d) + 4 * zl))
    for k, (slot, s) in enumerate(arrivals):
        if slot is not None:
            x_wire.take(slot, xs.at[s])
        project_rows(
            s, low_block(pair, me, me.b, s), xs, heads_w, inner, outer, query_gain, key_gain, raw, rows
        )
        for d in range(3):
            kv_wire.push((k, d), rows.at[s, :, pl.ds(256, 256)], kv.at[me.b, s], others[d])
        kv[me.b, s] = rows[s, :, 256:]
        step(f"row {k}")
    stack_heads(lambda s: rows[s, :, :256], queries)
    for d in (0, 1, 3, 2):
        j = ring(me.b, -d)
        if d:
            for k, (_, s) in enumerate(arrivals):
                kv_wire.take((k, d - 1), kv.at[j, s])
        for part in range(2):
            mix_tile(me, j, part, pair, kv, query_pos, queries, key_pos, mixed_t, total)
            step(f"tile {d}{part}")
    finish_mix(mixed, mixed_t, log_total, stacked, total)

    def place(origin):
        return attn_out.at[:, pl.ds(pl.multiple_of(origin * 256, 256), 256)]

    for k in range(1, 8):
        peer = peer_of(head, k)
        back_wire.push(k - 1, mixed.at[peer], place(head), group_spot(me, peer))
    attn_out[:, pl.ds(pl.multiple_of(head * 256, 256), 256)] = mixed[head]
    step("back")
    feed = FeedForward(x, attn_out, down_cot, mlp_gain, feed_outs, full, feed_scratch)
    finish(0)
    feed.load_out()
    finish(1)
    finish(2)
    finish(6)
    pass_tile(0)
    pass_tile(1)
    finish_tile(0)
    feed.load_tile(0)
    for k in range(7):
        back_wire.take(k, place(peer_of(head, 7 - k)))
    feed.begin()
    for t in range(FF_STEPS):
        if t + 2 < FF_STEPS:
            pass_tile(t + 2)
        if t + 1 < FF_STEPS:
            finish_tile(t + 1)
            feed.load_tile(t + 1)
        feed.tile(t)
        step(f"feed {t}")
    feed.end()
    step("end")
    assert not turns
    for m in (3, 4, 5):
        finish(m)
    for wire in (x_wire, w_wire, kv_wire, back_wire, gather_wire):
        wire.close()


def attention_forward(pair, x, gains, tables, down_cot, mlp_gain, weights):
    narrow = jax.ShapeDtypeStruct((128, 1024), BF16)
    wide = jax.ShapeDtypeStruct((128, FF_STEPS * FF_TILE), BF16)
    outs = pl.pallas_call(
        forward_body,
        out_shape=[
            jax.ShapeDtypeStruct((128, 2048), BF16),
            jax.ShapeDtypeStruct((8, 128, 512), BF16),
            jax.ShapeDtypeStruct((8, 128, 384), F32),
            jax.ShapeDtypeStruct((4, 8, 128, 256), BF16),
            jax.ShapeDtypeStruct((128, 2048), F32),
            jax.ShapeDtypeStruct((8, 2048), F32),
            narrow, narrow, wide, wide, wide, narrow,
            jax.ShapeDtypeStruct((128, 1024), F32),
            jax.ShapeDtypeStruct((128, 2048), BF16),
            jax.ShapeDtypeStruct((1, 1024), F32),
        ]
        + [jax.ShapeDtypeStruct((4,) + w.shape, w.dtype) for w in weights],
        in_specs=[SMEM] + [VMEM] * 8 + [HBM] * 7,
        out_specs=[VMEM] * 15 + [HBM] * 7,
        scratch_shapes=[
            pltpu.VMEM((4, 256, 2048), BF16),
            pltpu.VMEM((2, 3, 4, 256, FF_TILE), BF16),
            pltpu.VMEM((128, 1024), F32),
            pltpu.VMEM((128, 1024), F32),
            pltpu.VMEM((128, 1024), F32),
            dma(7),
            pltpu.VMEM((8, 128, 1024), BF16),
            pltpu.VMEM((4, 256, 512), BF16),
            pltpu.VMEM((2048, 128), BF16),
            pltpu.VMEM((2048, 128), BF16),
            pltpu.VMEM((8, 2048), jnp.int32),
            pltpu.VMEM((TILE, CHUNK), jnp.int32),
            pltpu.VMEM((8, 2048), F32),
            pltpu.VMEM((8, 128, 256), BF16),
            dma(7), dma(7), dma(3, 3), dma(3, 3), dma(3), dma(8, 3), dma(8, 3), dma(7), dma(7),
        ]
        + gather_scratch(weights),
        compiler_params=comm_params(1),
        name="attention_forward",
    )(pair, x, *gains, *tables, down_cot, mlp_gain, *weights)
    return outs[:6], outs[6:15], [whole_rows(out) for out in outs[15:]]


def whole_rows(out):
    return out.reshape(4 * out.shape[1], out.shape[2])


PAIR_TILE = 512


def half_of(ref, half):
    width = ref.shape[-1] // 2
    return ref.at[:, :, pl.ds(half * width, width)]


def add_into(target, *sources):
    for zh in range(target.shape[0]):

        @pl.loop(0, target.shape[1] // 16)
        def _(r):
            at = pl.ds(pl.multiple_of(r * 16, 16), 16)
            total = target[zh, at, :].astype(F32)
            for source in sources:
                total = total + source[zh, at, :].astype(F32)
            target[zh, at, :] = total.astype(BF16)


class PairGrad:
    def __init__(self, me, left, right, left_scratch, twin_right, grad, wire, slot):
        self.me, self.left, self.right, self.wire, self.slot = me, left, right, wire, slot
        self.landing, self.left_t = left_scratch
        self.twin_right, self.grad = twin_right, grad

    def send(self):
        me = self.me
        twin = me.sibling()
        self.wire.push(self.slot + 2, self.right, self.twin_right, twin)
        for zh in range(0 if self.left is None else 2):
            columns = pl.ds(pl.multiple_of((zh * 2 + 1 - me.core) * 256, 256), 256)
            self.wire.push(self.slot + zh, self.left.at[:, columns], self.landing.at[zh], twin)

    def multiply(self):
        me = self.me
        for zh in range(0 if self.left is None else 2):
            columns = pl.ds(pl.multiple_of((zh * 2 + me.core) * 256, 256), 256)
            self.left_t[zh * 256 : zh * 256 + 256, 0:128] = self.left[:, columns].T
            self.wire.take(self.slot + zh, self.landing.at[zh])
            self.left_t[zh * 256 : zh * 256 + 256, 128:256] = self.landing[zh].T
        self.wire.take(self.slot + 2, self.twin_right)

        @pl.loop(0, self.twin_right.shape[1] // PAIR_TILE)
        def _(t):
            columns = pl.ds(pl.multiple_of(t * PAIR_TILE, PAIR_TILE), PAIR_TILE)
            right = jnp.concatenate([self.right[:, columns], self.twin_right[:, columns]], axis=0)
            product = dot_nn(self.left_t[...], right).astype(BF16)
            self.grad[:, :, columns] = product.reshape(2, 256, PAIR_TILE)


REDUCE_SLOTS = 13


def reduce_scratch(widths, z_first):
    scratch = []
    for k, width in enumerate(widths):
        half = width // 2
        if k in z_first:
            shapes = [
                (1, 128, half), (1, 128, half), (1, 256, half), (1, 256, half),
                (3, 1, 64, half), (1, 64, half), (3, 1, 16, half), (1, 16, half),
            ]
        else:
            shapes = [
                (2, 64, half), (2, 64, half), (2, 64, width), (2, 64, width),
                (3, 2, 16, width), (2, 16, width), (4, 16, width), (1, 16, width),
            ]
        scratch += [pltpu.VMEM(shape, BF16) for shape in shapes]
    count = len(widths)
    return scratch + [dma(count, REDUCE_SLOTS), dma(count, REDUCE_SLOTS)]


def reduce_stages(me, grads, pieces, scratch, z_first):
    wire = Wire(scratch[-2], scratch[-1], me.sibling())
    z = me.zh * 2 + me.zl
    z_low, across, z_high = me.move(zl=1 - me.zl), me.across(), me.move(zh=1 - me.zh)

    def z_spot(step):
        far = lax.rem(z + step + 4, 4)
        return me.move(zl=lax.rem(far, 2), zh=far // 2)

    def rows(ref, i, size):
        return ref.at[:, pl.ds(pl.multiple_of(i * size, size), size)]

    def ring_stages(k, slot, ahead, behind, block, bufs, half):
        far_a, far_b, in_a, in_b = bufs

        def send():
            wire.push((k, slot), half(block(2), 0), far_a, ahead)
            wire.push((k, slot + 1), half(block(2), 1), far_b, behind)
            wire.push((k, slot + 2), half(block(1), 1), half(in_a, 1), ahead)
            wire.push((k, slot + 3), half(block(-1), 0), half(in_b, 0), behind)

        def relay():
            wire.take((k, slot), far_a)
            add_into(far_a, half(block(1), 0))
            wire.push((k, slot + 4), far_a, half(in_a, 0), ahead)
            wire.take((k, slot + 1), far_b)
            add_into(far_b, half(block(-1), 1))
            wire.push((k, slot + 5), far_b, half(in_b, 1), behind)

        def collect():
            wire.take((k, slot + 2), half(in_a, 1))
            wire.take((k, slot + 3), half(in_b, 0))
            wire.take((k, slot + 4), half(in_a, 0))
            wire.take((k, slot + 5), half(in_b, 1))
            add_into(in_a, in_b, block(0))

        return send, relay, collect

    def direct_send(k, slot, axis, size, source, land):
        position = getattr(me, axis)
        for d in (1, 3, 2):
            spot = me.move(**{axis: ring(position, d)})
            wire.push((k, slot + d - 1), rows(source, ring(position, d), size), land.at[d - 1], spot)

    def direct_sum(k, slot, axis, size, source, land, target):
        for d in (1, 3, 2):
            wire.take((k, slot + d - 1), land.at[d - 1])
        own = rows(source, getattr(me, axis), size)
        for lead in range(target.shape[0]):

            @pl.loop(0, size // 16)
            def _(r):
                at = pl.ds(pl.multiple_of(r * 16, 16), 16)
                total = own[lead, at, :].astype(F32)
                for d in range(3):
                    total = total + land[d, lead, at, :].astype(F32)
                target[lead, at, :] = total.astype(BF16)

    def plain(k):
        grad, bufs = grads[k], scratch[8 * k : 8 * k + 8]
        in_a, a_land, total, z_land = bufs[2], bufs[4], bufs[5], bufs[6]
        send, relay, collect = ring_stages(
            k, 0, me.move(b=ring(me.b, 1)), me.move(b=ring(me.b, -1)),
            lambda step: rows(grad, ring(me.b, step), 64), bufs[:4], half_of,
        )

        def third():
            collect()
            direct_send(k, 6, "a", 16, in_a, a_land)

        def fourth():
            direct_sum(k, 6, "a", 16, in_a, a_land, total)
            wire.push((k, 9), total.at[1 - me.zh], z_land.at[z], across)
            wire.push((k, 10), total.at[1 - me.zh], z_land.at[z], z_high)
            wire.push((k, 11), total.at[me.zh], z_land.at[z], z_low)
            z_land[z] = total[me.zh]

        def fifth():
            for slot, spot in ((9, across), (10, z_high), (11, z_low)):
                wire.take((k, slot), z_land.at[spot.zh * 2 + spot.zl])
            total = z_land[0].astype(F32)
            for i in range(1, 4):
                total = total + z_land[i].astype(F32)
            pieces[k][0] = total.astype(BF16)

        return [send, relay, third, fourth, fifth]

    def first_z(k):
        grad, bufs = grads[k], scratch[8 * k : 8 * k + 8]
        in_a, b_land, b_sum, a_land, a_sum = bufs[2], bufs[4], bufs[5], bufs[6], bufs[7]
        width = grad.shape[2] // 2

        def columns(ref, zl):
            return ref.at[:, :, pl.ds(pl.multiple_of(zl * width, width), width)]

        def block(step):
            far = lax.rem(z + step + 4, 4)
            return columns(grad.at[pl.ds(far // 2, 1)], lax.rem(far, 2))

        send, relay, collect = ring_stages(
            k, 0, z_spot(1), z_spot(-1), block, bufs[:4],
            lambda view, i: view.at[:, pl.ds(128 * i, 128)],
        )

        def third():
            collect()
            direct_send(k, 6, "b", 64, in_a, b_land)

        def fourth():
            direct_sum(k, 6, "b", 64, in_a, b_land, b_sum)
            direct_send(k, 9, "a", 16, b_sum, a_land)

        def fifth():
            direct_sum(k, 9, "a", 16, b_sum, a_land, a_sum)
            place = columns(pieces[k], me.zl)
            place[...] = a_sum[...]
            wire.push((k, 12), a_sum, place, z_low)

        def sixth():
            wire.take((k, 12), columns(pieces[k], 1 - me.zl))

        return [send, relay, third, fourth, fifth, sixth]

    lists = [first_z(k) if k in z_first else plain(k) for k in range(len(grads))]
    return lists, wire


def replicate_stages(me, pieces, outs, send, recv, load_sem):
    wire = Wire(send, recv, me.sibling())
    loads = {}

    def cut(k, row, rows, half=None):
        width = outs[k].shape[1] // 2
        at = pl.ds(pl.multiple_of(row, 16), rows)
        if half is None:
            return outs[k].at[at]
        return outs[k].at[at, pl.ds(half * width, width)]

    b_next, b_prev = me.move(b=ring(me.b, 1)), me.move(b=ring(me.b, -1))

    def a_row(step):
        return (me.b * 4 + ring(me.a, step)) * 16

    def b_row(step):
        return ring(me.b, step) * 64

    def a_send(k):
        place = cut(k, a_row(0), 16)
        for d in (1, 3, 2):
            wire.push((k, d - 1), pieces[k].at[0], place, me.move(a=ring(me.a, d)))
        loads[k] = pltpu.make_async_copy(pieces[k].at[0], place, load_sem.at[k])
        loads[k].start()

    def b_send(k):
        for d in (1, 3, 2):
            wire.take((k, d - 1), cut(k, a_row(-d), 16))
        loads[k].wait()
        mine = cut(k, b_row(0), 64)
        wire.push((k, 4), mine, mine, b_next)
        wire.push((k, 5), mine, mine, b_prev)

    def b_relay(k):
        wire.take((k, 4), cut(k, b_row(-1), 64))
        wire.push((k, 6), cut(k, b_row(-1), 64, 0), cut(k, b_row(-1), 64, 0), b_next)
        wire.take((k, 5), cut(k, b_row(1), 64))
        wire.push((k, 7), cut(k, b_row(1), 64, 1), cut(k, b_row(1), 64, 1), b_prev)

    def b_collect(k):
        wire.take((k, 6), cut(k, b_row(2), 64, 0))
        wire.take((k, 7), cut(k, b_row(2), 64, 1))

    stages = (a_send, b_send, b_relay, b_collect)
    lists = [[functools.partial(stage, k) for stage in stages] for k in range(len(pieces))]
    return lists, wire


class Plan:
    def __init__(self, **lists):
        self.lists = {name: list(stages) for name, stages in lists.items()}

    def run(self, names):
        for name in names:
            self.lists[name].pop(0)()

    def check(self):
        assert not any(self.lists.values())


def gain_turns(me, gains, gains_out, gain_slots, gain_send, gain_recv):
    first = me.core == 0
    x, y = jnp.where(first, me.a, me.b), jnp.where(first, me.b, me.a)
    z = me.zh * 2 + me.zl
    wire = Wire(gain_send, gain_recv, me.sibling())

    def pick(d, on_x):
        use_a = first if on_x else jnp.logical_not(first)
        return me.move(
            a=jnp.where(use_a, ring(me.a, d), me.a), b=jnp.where(use_a, me.b, ring(me.b, d))
        )

    def z_spot(d):
        far = lax.rem(z + d, 4)
        return me.move(zl=lax.rem(far, 2), zh=far // 2)

    def push(stage, position, spots):
        for d, spot in enumerate(spots):
            slot = gain_slots.at[stage, position]
            wire.push((stage, d), slot, slot, spot)

    def take(stage, position, size):
        for d in range(size - 1):
            wire.take((stage, d), gain_slots.at[stage, lax.rem(position + size - 1 - d, size)])

    def total(stage):
        return (gain_slots[stage, 0] + gain_slots[stage, 1]) + (gain_slots[stage, 2] + gain_slots[stage, 3])

    def turn0():
        gain_slots[0, me.core] = gains[...]
        push(0, me.core, [me.sibling()])

    def turn1():
        take(0, me.core, 2)
        gain_slots[1, x] = gain_slots[0, 0] + gain_slots[0, 1]
        push(1, x, [pick(d, True) for d in (1, 2, 3)])

    def turn2():
        take(1, x, 4)
        gain_slots[2, y] = total(1)
        push(2, y, [pick(d, False) for d in (1, 2, 3)])

    def turn3():
        take(2, y, 4)
        gain_slots[3, z] = total(2)
        push(3, z, [z_spot(d) for d in (1, 2, 3)])

    def turn4():
        take(3, z, 4)
        gains_out[...] = total(3)

    return [turn0, turn1, turn2, turn3, turn4], wire.close


def unrope(s, low, grads, raw, inner, outer, gain, column, gain_part):
    cosine, sine = rope_rows(inner, outer, low)
    value = raw[s, :, column : column + 128]
    scale = norm_scale(value)
    hat = value * scale
    hat_cot = grads * cosine - pltpu.roll(grads, 64, 1) * sine
    gain_part[...] += jnp.sum((hat_cot * hat).reshape(16, 8, 128), axis=0)
    scaled = hat_cot * gain[...]
    return (scale * (scaled - hat * mean_last(scaled * hat))).astype(BF16)


WIDTHS = (3072, 3072, 3072, 2048, 2048, 2048)
Z_FIRST = (2, 3, 4)
BETWEEN = {
    "cots": "ddgguoou",
    "tiles": "dg",
    "own tile": "",
    "rows 2": "",
    "rows 4": "",
    "rows 6": "",
    "rows 0": "guodug",
    "proj": "qdkkoukdquugoddkqugok",
    "weights": "d",
    "input": "qkkousdsqgoksqqqdsogqkgoqsuoqk",
}


def backward_body(*refs):
    (
        pair, x, attn_gain, query_gain, key_gain, inner, outer, rows, raw, kv, mixed_t, log_total, parts,
        mlp_in, down_cot, branch_cot, gate_cot, up_cot, hidden, attn_out, middle_cot, mlp_gain_part, wq, wk, wv,
    ), refs = refs[:25], refs[25:]
    (input_cot, gains_out), outs, refs = refs[:2], refs[2:8], refs[8:]
    (
        cots_in, dkv, queries, cots, deltas, query_pos, key_pos, probs_all, score_cots, acc, held, stacked, message,
        attn_in, proj, head_gains, gains, gain_slots,
        cot_send, cot_recv, p_send, p_recv, m_send, m_recv, w_send, w_recv, out_send, out_recv, out_load, w_load,
        gain_send, gain_recv,
    ), refs = refs[:32], refs[32:]
    pieces, grads, refs = refs[:6], list(refs[6:11]), refs[11:]
    grads.append(grads[2].at[:, :, pl.ds(0, WIDTHS[5])])
    me = here()
    head = group_head(me)
    twin = me.sibling()
    others = [me.move(b=ring(me.b, d)) for d in (1, 2, 3)]
    greet([twin, me.across(), me.move(zh=1 - me.zh)] + group_neighbours(me))
    cot_wire = Wire(cot_send, cot_recv, twin)
    p_wire = Wire(p_send, p_recv, twin)
    m_wire = Wire(m_send, m_recv, twin)
    w_wire = Wire(w_send, w_recv, twin)

    def of_head(ref, h):
        return ref.at[:, pl.ds(pl.multiple_of(h * 256, 256), 256)]

    for k in range(1, 8):
        peer = peer_of(head, k)
        cot_wire.push(k - 1, of_head(parts, peer), cots_in.at[head], group_spot(me, peer))
    lefts = (mlp_in, None, down_cot, branch_cot, attn_in, None)
    rights = (
        gate_cot, up_cot, hidden, attn_out, proj.at[:, pl.ds(0, 2048)], proj.at[:, pl.ds(2048, 2048)]
    )
    held_lefts, twin_rights, refs = refs[:8], refs[8:14], refs[14:]
    pairs = []
    for i, share in enumerate((0, 0, 1, 2, 3, 3)):
        pairs.append(
            PairGrad(
                me, lefts[i], rights[i], held_lefts[2 * share : 2 * share + 2], twin_rights[i], grads[i], w_wire, 3 * i
            )
        )
    sums, sum_wire = reduce_stages(me, grads, pieces, refs, Z_FIRST)
    copies, out_wire = replicate_stages(me, pieces, outs, out_send, out_recv, out_load)
    small, gain_finish = gain_turns(me, gains, gains_out, gain_slots, gain_send, gain_recv)
    plan = Plan(s=small, **{
        name: [pairs[i].multiply] + sums[i] + copies[i] for i, name in enumerate("gudoqk")
    })
    for i in (2, 0, 1, 3):
        pairs[i].send()
    query_positions(pair, me, query_pos)
    cots_in[head] = parts[:, pl.ds(pl.multiple_of(head * 256, 256), 256)]
    head_gains[...] = jnp.zeros_like(head_gains)
    inputs = x[...].astype(F32)
    scale = norm_scale(inputs)
    normed = inputs * scale
    attn_in[...] = (normed * attn_gain[...]).astype(BF16)
    plan.run(BETWEEN["cots"])
    for k in range(7):
        cot_wire.take(k, cots_in.at[peer_of(head, 7 - k)])
    start_grad(rows, mixed_t, cots_in, queries, cots, deltas, acc)
    for d in (2, 1, 3, 0):
        j = ring(me.b, d)
        if d == 0:
            plan.run(BETWEEN["tiles"])
        for part in range(2):
            grad_tile(
                me, j, part, pair, kv, query_pos, queries, cots, deltas, log_total, key_pos,
                probs_all, score_cots, acc, dkv,
            )
        if d:
            for k in range(8):
                peer = peer_of(head, k)
                p_wire.push((k, d - 1), dkv.at[j, peer], held.at[d - 1, peer], others[d - 1])
    for chunk in range(8):
        columns = pl.ds(chunk * CHUNK, CHUNK)
        stacked[columns, :] = (acc[:, columns] * SCORE_SCALE).T
    plan.run(BETWEEN["own tile"])

    def places(h):
        return (
            (pl.ds(0, 256), pl.ds(pl.multiple_of(h * 256, 256), 256)),
            (pl.ds(256, 128), pl.ds(pl.multiple_of(2048 + h * 128, 128), 128)),
            (pl.ds(384, 128), pl.ds(pl.multiple_of(3072 + h * 128, 128), 128)),
        )

    for k in (1, 2, 3, 4, 5, 6, 7, 0):
        s = peer_of(head, k)
        low = low_block(pair, me, me.b, s)
        for d in range(3):
            p_wire.take((k, d), held.at[d, s])
        for h in range(2):
            turned = jnp.concatenate(
                [
                    stacked[pl.ds(pl.multiple_of(part * 1024 + s * 128 + h * 64, 64), 64), :]
                    for part in range(2)
                ],
                axis=0,
            )
            message[s, :, h * 128 : h * 128 + 128] = unrope(
                s, low, turned, raw, inner, outer, query_gain, h * 128, head_gains.at[0]
            )
        total = (
            dkv[me.b, s].astype(F32)
            + held[0, s].astype(F32)
            + held[1, s].astype(F32)
            + held[2, s].astype(F32)
        )
        message[s, :, 256:384] = unrope(
            s, low, total[:, :128], raw, inner, outer, key_gain, 256, head_gains.at[1]
        )
        message[s, :, 384:] = total[:, 128:].astype(BF16)
        if k:
            for i, (source, target) in enumerate(places(head)):
                m_wire.push((k - 1, i), message.at[s, :, source], proj.at[:, target], group_spot(me, s))
        if k % 2 == 0:
            plan.run(BETWEEN[f"rows {k}"])
    for source, target in places(head):
        proj[:, target] = message[head, :, source]
    for k in range(7):
        for i, (_, target) in enumerate(places(peer_of(head, 7 - k))):
            m_wire.take((k, i), proj.at[:, target])
    for i in (4, 5):
        pairs[i].send()
    for k in range(3):
        sum_wire.settle(k)
    plan.run(BETWEEN["proj"])

    loads = []
    value_rows = (score_cots, probs_all)
    for i in range(4):
        at = pl.ds(256 * i, 256)
        target = grads[i // 2].at[i % 2]
        loads.append((wq.at[at], target.at[:, pl.ds(0, 2048)]))
        loads.append((wk.at[at], target.at[:, pl.ds(2048, 1024)]))
        loads.append((wv.at[at], value_rows[i // 2].at[pl.ds(i % 2 * 256, 256)]))
    loads = [pltpu.make_async_copy(*pair_, w_load.at[i]) for i, pair_ in enumerate(loads)]
    for load in loads:
        load.start()
    plan.run(BETWEEN["weights"])
    for load in loads:
        load.wait()
    attn_in_cot = jnp.concatenate(
        [
            dot_nt(proj[:, :3072], grads[i // 2][i % 2])
            + dot_nt(proj[:, 3072:], value_rows[i // 2][i % 2 * 256 : i % 2 * 256 + 256, :])
            for i in range(4)
        ],
        axis=1,
    )
    scaled = attn_in_cot * attn_gain[...]
    input_cot[...] = middle_cot[...] + scale * (scaled - normed * mean_last(scaled * normed))
    gains[...] = jnp.zeros_like(gains)
    gains[0:1, :] = jnp.sum(attn_in_cot * normed, axis=0, keepdims=True)
    gains[1:2, :] = mlp_gain_part[...]
    for i in range(2):
        gains[2 + i : 3 + i, 0:128] = jnp.sum(head_gains[i], axis=0, keepdims=True)
    plan.run(BETWEEN["input"])
    plan.check()
    gain_finish()
    for wire in (cot_wire, p_wire, m_wire, w_wire, sum_wire, out_wire):
        wire.close()


def attention_backward(pair, x, gains, tables, kept, attended_cot, lefts, rights, middle_cot, mlp_gain_part, weights):
    heads = (8, 128, 256)
    count = len(WIDTHS)
    outs = pl.pallas_call(
        backward_body,
        out_shape=[jax.ShapeDtypeStruct((128, 1024), F32), jax.ShapeDtypeStruct((4, 1024), F32)]
        + [jax.ShapeDtypeStruct((256, width), BF16) for width in WIDTHS],
        in_specs=[SMEM] + [VMEM] * 21 + [HBM] * 3,
        out_specs=[VMEM] * 2 + [HBM] * count,
        scratch_shapes=[
            pltpu.VMEM(heads, BF16),
            pltpu.VMEM((4,) + heads, BF16),
            pltpu.VMEM((2048, 128), BF16),
            pltpu.VMEM((2048, 128), BF16),
            pltpu.VMEM((8, 2048), F32),
            pltpu.VMEM((8, 2048), jnp.int32),
            pltpu.VMEM((TILE, CHUNK), jnp.int32),
            pltpu.VMEM((TILE, 1024), BF16),
            pltpu.VMEM((TILE, 1024), BF16),
            pltpu.VMEM((128, 2048), F32),
            pltpu.VMEM((3,) + heads, BF16),
            pltpu.VMEM((2048, 128), F32),
            pltpu.VMEM((8, 128, 512), BF16),
            pltpu.VMEM((128, 1024), BF16),
            pltpu.VMEM((128, 4096), BF16),
            pltpu.VMEM((2, 8, 128), F32),
            pltpu.VMEM((4, 1024), F32),
            pltpu.VMEM((4, 4, 4, 1024), F32),
            dma(7), dma(7), dma(8, 3), dma(8, 3), dma(7, 3), dma(7, 3), dma(18), dma(18),
            dma(count, 8), dma(count, 8), dma(count), dma(12), dma(4, 3), dma(4, 3),
        ]
        + [pltpu.VMEM((1, 16, width), BF16) for width in WIDTHS]
        + [pltpu.VMEM((2, 256, width), BF16) for width in WIDTHS[:5]]
        + [pltpu.VMEM((2, 128, 256), BF16), pltpu.VMEM((512, 256), BF16)] * 4
        + [pltpu.VMEM((128, width), BF16) for width in WIDTHS]
        + reduce_scratch(WIDTHS, Z_FIRST),
        compiler_params=comm_params(2, 62 * 1024 * 1024),
        name="attention_backward",
    )(pair, x, *gains, *tables, *kept, attended_cot, *lefts, *rights, middle_cot, mlp_gain_part, *weights)
    return outs[0], outs[1], outs[2:]


def shards(
    tokens,
    query_weight,
    key_weight,
    value_weight,
    out_weight,
    gate_weight,
    up_weight,
    down_weight,
    attn_gain,
    mlp_gain,
    query_gain,
    key_gain,
    pair_order,
    out_grad,
):
    tables = rope_tables()
    attn_row, query_row, key_row = attn_gain[None], query_gain[None], key_gain[None]
    down_cot = out_grad[0]
    (attn_out, *kept), feed, full = attention_forward(
        pair_order,
        tokens[0],
        (attn_row, query_row, key_row),
        tables,
        down_cot,
        mlp_gain[None],
        [out_weight, gate_weight, up_weight, query_weight, key_weight, value_weight, down_weight],
    )
    result, mlp_in, gate_cot, up_cot, hidden, branch_cot, middle_cot, attended_cot, mlp_gain_part = feed
    full_qkv = full[3:6]
    input_cot, gains, grads = attention_backward(
        pair_order,
        tokens[0],
        (attn_row, query_row, key_row),
        tables,
        kept,
        attended_cot,
        (mlp_in, down_cot, branch_cot),
        (gate_cot, up_cot, hidden, attn_out),
        middle_cot,
        mlp_gain_part,
        full_qkv,
    )
    gate, up, down, out, query, key_value = (grad.astype(F32) for grad in grads)
    return (
        result[None],
        input_cot[None],
        query,
        key_value[:, :1024],
        key_value[:, 1024:],
        out,
        gate,
        up,
        down,
        gains[0],
        gains[1],
        gains[2, :128],
        gains[3, :128],
    )


def solution(mesh):
    rows, split, whole = P("fsdp", None), P("fsdp", "ctx", None), P()
    return jax.shard_map(
        shards,
        mesh=mesh,
        in_specs=(split,) + (rows,) * 7 + (whole,) * 4 + (rows, split),
        out_specs=(split, split) + (rows,) * 7 + (whole,) * 4,
        check_vma=False,
    )
```

```python
import functools

import jax
import jax.numpy as jnp
import numpy as np
from jax import lax
from jax.experimental import pallas as pl
from jax.experimental.pallas import tpu as pltpu
from jax.sharding import PartitionSpec as P

EPSILON = 1e-06
ROPE_BASE = 1000000.0
MESH = pl.DeviceIdType.MESH
HBM = pl.BlockSpec(memory_space=pltpu.HBM)
VMEM = pl.BlockSpec(memory_space=pltpu.VMEM)
SMEM = pl.BlockSpec(memory_space=pltpu.SMEM)
LOG2E = 1.4426950408889634
VMEM_LIMIT = 56 * 1024 * 1024
BF16 = jnp.bfloat16
F32 = jnp.float32


class Spot:
    def __init__(self, a, b, zl, zh, core):
        self.a, self.b, self.zl, self.zh, self.core = a, b, zl, zh, core

    def move(self, a=None, b=None, zl=None, zh=None):
        return Spot(
            self.a if a is None else a,
            self.b if b is None else b,
            self.zl if zl is None else zl,
            self.zh if zh is None else zh,
            self.core,
        )

    def id(self):
        first = self.core == 0
        x = jnp.where(first, self.a, self.b)
        y = jnp.where(first, self.b, self.a)
        return (self.zl * 16 + y * 4 + x, self.zh * 2 + self.core)

    def sibling(self):
        return Spot(self.b, self.a, self.zl, self.zh, 1 - self.core)

    def across(self):
        return self.move(zl=1 - self.zl, zh=1 - self.zh)


def here():
    ctx = lax.axis_index("ctx")
    fsdp = lax.axis_index("fsdp")
    x = lax.rem(ctx, 4)
    y = lax.rem(ctx // 4, 4)
    core = lax.rem(fsdp, 2)
    first = core == 0
    return Spot(jnp.where(first, x, y), jnp.where(first, y, x), ctx // 16, fsdp // 2, core)


def ring(position, step):
    return lax.rem(position + step + 4, 4)


def greet(spots):
    barrier = pltpu.get_barrier_semaphore()
    for spot in spots:
        pl.semaphore_signal(barrier, inc=1, device_id=spot.id(), device_id_type=MESH)
    pl.semaphore_wait(barrier, len(spots))


def remote(src, dst, send_sem, recv_sem, spot):
    return pltpu.make_async_remote_copy(
        src_ref=src,
        dst_ref=dst,
        send_sem=send_sem,
        recv_sem=recv_sem,
        device_id=spot.id(),
        device_id_type=MESH,
    )


def comm_params(collective_id, limit=VMEM_LIMIT):
    return pltpu.CompilerParams(
        collective_id=collective_id, has_side_effects=True, vmem_limit_bytes=limit
    )


class Wire:
    def __init__(self, send, recv, spot):
        self.send, self.recv, self.spot, self.sent = send, recv, spot, []

    def push(self, slot, src, dst, spot):
        copy = remote(src, dst, self.send.at[slot], self.recv.at[slot], spot)
        copy.start()
        self.sent.append((slot, copy))

    def take(self, slot, dst):
        remote(dst, dst, self.send.at[slot], self.recv.at[slot], self.spot).wait_recv()

    def settle(self, k):
        for slot, copy in self.sent:
            if slot[0] == k:
                copy.wait_send()
        self.sent = [(slot, copy) for slot, copy in self.sent if slot[0] != k]

    def close(self):
        for _, copy in self.sent:
            copy.wait_send()


def pipeline(stages, count):
    def turn(t):
        for depth, stage in enumerate(stages):
            if 0 <= t - depth < count:
                stage(t - depth)

    return [functools.partial(turn, t) for t in range(count + len(stages) - 1)]


GATHER_SLOTS = 14
FF_TILE = 512
FF_STEPS = 6


def gather_scratch(weights):
    count = len(weights)
    return [pltpu.VMEM(w.shape, w.dtype) for w in weights] + [
        pltpu.SemaphoreType.DMA((count, GATHER_SLOTS)),
        pltpu.SemaphoreType.DMA((count, GATHER_SLOTS)),
        pltpu.SemaphoreType.DMA((2, count)),
    ]


def gather_turns(me, ins, outs, scratch):
    count = len(ins)
    held, (send, recv, local_sem) = scratch[:count], scratch[count:]
    mine = me.zh * 2 + me.core
    other = (1 - me.zh) * 2 + me.core
    twin_mine = me.zh * 2 + 1 - me.core
    twin_other = (1 - me.zh) * 2 + 1 - me.core
    twin, across = me.sibling(), me.across()
    a_next, a_prev = me.move(a=ring(me.a, 1)), me.move(a=ring(me.a, -1))
    b_next, b_prev = me.move(b=ring(me.b, 1)), me.move(b=ring(me.b, -1))
    wire = Wire(send, recv, twin)

    def cut(m, rows, half):
        width = ins[m].shape[1] // 2
        if half is None:
            return outs[m].at[other, rows]
        return outs[m].at[other, rows, pl.ds(half * width, width)]

    def piece(m, a, half=None):
        return cut(m, pl.ds(pl.multiple_of((me.b * 4 + a) * 16, 16), 16), half)

    def block(m, b, half=None):
        return cut(m, pl.ds(pl.multiple_of(b * 64, 64), 64), half)

    def push(m, slot, src, dst, spot):
        wire.push((m, slot), src, dst, spot)

    def take(m, slot, dst):
        wire.take((m, slot), dst)

    loads = [pltpu.make_async_copy(ins[m], held[m], local_sem.at[0, m]) for m in range(count)]
    stores = [pltpu.make_async_copy(held[m], outs[m].at[mine], local_sem.at[1, m]) for m in range(count)]

    last = count - 1

    def start():
        for m in range(last):
            rows = pl.ds(pl.multiple_of((me.b * 4 + me.a) * 16, 16), 16)
            push(m, 0, ins[m].at[rows], outs[m].at[mine, rows], across)
        for t in range(FF_STEPS):
            columns = pl.ds(FF_TILE * t, FF_TILE)
            push(last, t, ins[last].at[:, columns], outs[last].at[mine, :, columns], across)
        for load in loads:
            load.start()

    def spread_own():
        for m in range(count):
            loads[m].wait()
            stores[m].start()
            push(m, 2 * FF_STEPS if m == last else 9, ins[m], outs[m].at[mine], twin)

    def stage_z(m):
        take(m, 0, piece(m, me.a))
        push(m, 1, piece(m, me.a), piece(m, me.a), a_next)
        push(m, 2, piece(m, me.a), piece(m, me.a), a_prev)

    def stage_a(m):
        left, right = ring(me.a, -1), ring(me.a, 1)
        take(m, 1, piece(m, left))
        push(m, 3, piece(m, left, 0), piece(m, left, 0), a_next)
        take(m, 2, piece(m, right))
        push(m, 4, piece(m, right, 1), piece(m, right, 1), a_prev)

    def stage_b(m):
        far = ring(me.a, 2)
        take(m, 3, piece(m, far, 0))
        take(m, 4, piece(m, far, 1))
        push(m, 5, block(m, me.b), block(m, me.b), b_next)
        push(m, 6, block(m, me.b), block(m, me.b), b_prev)
        push(m, 10, block(m, me.b), block(m, me.b), twin)

    def stage_c(m):
        left, right = ring(me.b, -1), ring(me.b, 1)
        take(m, 5, block(m, left))
        push(m, 7, block(m, left, 0), block(m, left, 0), b_next)
        push(m, 11, block(m, left), block(m, left), twin)
        take(m, 6, block(m, right))
        push(m, 8, block(m, right, 1), block(m, right, 1), b_prev)
        push(m, 12, block(m, right), block(m, right), twin)

    def stage_d(m):
        far = ring(me.b, 2)
        take(m, 7, block(m, far, 0))
        take(m, 8, block(m, far, 1))
        push(m, 13, block(m, far), block(m, far), twin)

    def pass_tile(t):
        tile = outs[last].at[other, :, pl.ds(FF_TILE * t, FF_TILE)]
        take(last, t, tile)
        push(last, FF_STEPS + t, tile, tile, twin)

    def finish_tile(t):
        take(last, FF_STEPS + t, outs[last].at[twin_other, :, pl.ds(FF_TILE * t, FF_TILE)])

    def finish(m):
        take(m, 2 * FF_STEPS if m == last else 9, outs[m].at[twin_mine])
        stores[m].wait()
        if m < last:
            for slot, step in ((10, 0), (11, -1), (12, 1), (13, 2)):
                rows = pl.ds(pl.multiple_of(ring(me.a, step) * 64, 64), 64)
                take(m, slot, outs[m].at[twin_other, rows])

    turns = pipeline((stage_z, stage_a, stage_b, stage_c, stage_d), last)
    return start, spread_own, turns, pass_tile, finish_tile, finish, wire


def group_spot(me, head):
    return me.move(a=lax.rem(head, 4), zl=head // 4)


def group_head(me):
    return me.a + 4 * me.zl


def peer_of(head, k):
    return lax.rem(head + k, 8)


def group_neighbours(me):
    head = group_head(me)
    return [group_spot(me, peer_of(head, k)) for k in range(1, 8)] + [
        me.move(b=ring(me.b, d)) for d in (1, 2, 3)
    ]


def dma(*shape):
    return pltpu.SemaphoreType.DMA(shape)


TILE = 512
CHUNK = 256
SCORE_SCALE = 128.0**-0.5


def dot_nt(left, right):
    return lax.dot_general(left, right, (((1,), (1,)), ((), ())), preferred_element_type=F32)


def dot_nn(left, right):
    return lax.dot_general(left, right, (((1,), (0,)), ((), ())), preferred_element_type=F32)


def stack_heads(read, target):
    for s in range(8):
        rows = read(s)
        for part in range(2):
            for head in range(2):
                at = part * 1024 + s * 128 + head * 64
                target[at : at + 64, :] = rows[part * 64 : part * 64 + 64, head * 128 : head * 128 + 128]


def unstack_heads(stacked, s, out):
    for part in range(2):
        for head in range(2):
            at = part * 1024 + s * 128 + head * 64
            out[s, part * 64 : part * 64 + 64, head * 128 : head * 128 + 128] = stacked[at : at + 64, :]


def low_block(pair, me, j, s):
    a = lax.rem(s, 4)
    first = me.core == 0
    return pair[0, (s // 4) * 16 + jnp.where(first, j * 4 + a, a * 4 + j)]


def key_positions(pair, me, j, part, target):
    line = lax.broadcasted_iota(jnp.int32, (64, CHUNK), 0)
    for s in range(8):
        low = low_block(pair, me, j, s)
        block = low if part == 0 else 63 - low
        target[s * 64 : s * 64 + 64, :] = line + block * 64


def query_positions(pair, me, target):
    line = lax.rem(lax.broadcasted_iota(jnp.int32, (8, 128), 1), 64)
    for s in range(8):
        low = low_block(pair, me, me.b, s)
        target[:, s * 128 : s * 128 + 128] = line + low * 64
        target[:, 1024 + s * 128 : 1152 + s * 128] = line + (63 - low) * 64


def rope_tables():
    frequency = ROPE_BASE ** (-np.arange(0, 128, 2, dtype=np.float64) / 128)
    frequency = np.concatenate([frequency, frequency])
    sign = np.where(np.arange(128) < 64, -1.0, 1.0)
    inner = np.arange(64, dtype=np.float64)[:, None] * frequency
    outer = inner * 64.0
    make = lambda angles: jnp.asarray(np.stack([np.cos(angles), np.sin(angles) * sign]), F32)
    return make(inner), make(outer)


def rope_rows(inner, outer, low):
    cosines, sines = [], []
    for block in (low, 63 - low):
        cos_b, sin_b = outer[0, pl.ds(block, 1), :], outer[1, pl.ds(block, 1), :]
        cosines.append(cos_b * inner[0] - sin_b * inner[1])
        sines.append(sin_b * inner[0] + cos_b * inner[1])
    return jnp.concatenate(cosines, axis=0), jnp.concatenate(sines, axis=0)


def mean_last(value):
    return jnp.mean(value, axis=-1, keepdims=True)


def norm_scale(value):
    return lax.rsqrt(mean_last(value * value) + EPSILON)


def tile_rows(kv, j, part, start):
    return kv[j, :, part * 64 : part * 64 + 64, start : start + 128].reshape(TILE, 128)


def tile_probs(scores, masked, key_pos, query_pos, columns, shift=None):
    logits = scores * (LOG2E * SCORE_SCALE)
    if shift is not None:
        logits = logits - shift
    probs = jnp.exp2(logits)
    if masked:
        probs = jnp.where(key_pos[...] <= query_pos[0:1, columns], probs, 0.0)
    return probs


def mix_tile(me, j, part, pair, kv, query_pos, queries, key_pos, acc, total):
    key_positions(pair, me, j, part, key_pos)
    keys = tile_rows(kv, j, part, 0)
    values_t = tile_rows(kv, j, part, 128).T
    for chunk in range(4 * part, 8):
        columns = pl.ds(chunk * CHUNK, CHUNK)
        masked = part == 1 or chunk < 4
        probs = tile_probs(dot_nt(keys, queries[columns, :]), masked, key_pos, query_pos, columns)
        total[:, columns] += jnp.sum(probs.reshape(TILE // 8, 8, CHUNK), axis=0)
        acc[:, columns] += dot_nn(values_t, probs.astype(BF16))


def finish_mix(out, mixed_t, log_total, stacked, total):
    for chunk in range(8):
        columns = pl.ds(chunk * CHUNK, CHUNK)
        full = jnp.sum(total[:, columns], axis=0, keepdims=True)
        log_total[:, columns] = jnp.broadcast_to(jnp.log2(full), (8, CHUNK))
        mixed = mixed_t[:, columns] / full
        mixed_t[:, columns] = mixed
        stacked[columns, :] = mixed.T.astype(BF16)
    for s in range(8):
        unstack_heads(stacked, s, out)


def grad_tile(
    me, j, part, pair, kv, query_pos, queries, cots, deltas, log_total, key_pos, probs_all, score_cots, acc, dkv
):
    key_positions(pair, me, j, part, key_pos)
    keys = tile_rows(kv, j, part, 0)
    values = tile_rows(kv, j, part, 128)
    keys_t = keys.T
    key_cot, value_cot = 0.0, 0.0
    for first in range(part, 2):
        for chunk in range(4 * first, 4 * first + 4):
            columns = pl.ds(chunk * CHUNK, CHUNK)
            local = pl.ds((chunk - 4 * first) * CHUNK, CHUNK)
            masked = part == first
            scores = dot_nt(keys, queries[columns, :])
            prob_cot = dot_nt(values, cots[columns, :])
            probs = tile_probs(scores, masked, key_pos, query_pos, columns, log_total[0:1, columns])
            score_cot = (probs * (prob_cot - deltas[0:1, columns])).astype(BF16)
            probs_all[:, local] = probs.astype(BF16)
            score_cots[:, local] = score_cot
            acc[:, columns] += dot_nn(keys_t, score_cot)
        rows = pl.ds(1024 * first, 1024)
        key_cot = key_cot + dot_nn(score_cots[...], queries[rows, :])
        value_cot = value_cot + dot_nn(probs_all[...], cots[rows, :])
    key_cot = key_cot * SCORE_SCALE
    at = part * 64
    dkv[j, :, at : at + 64, 0:128] = key_cot.astype(BF16).reshape(8, 64, 128)
    dkv[j, :, at : at + 64, 128:256] = value_cot.astype(BF16).reshape(8, 64, 128)


def start_grad(rows, mixed_t, cots_in, queries, cots, deltas, acc):
    stack_heads(lambda s: rows[s, :, :256], queries)
    stack_heads(lambda s: cots_in[s], cots)
    for chunk in range(8):
        columns = pl.ds(chunk * CHUNK, CHUNK)
        product = cots[columns, :].astype(F32).T * mixed_t[:, columns]
        deltas[:, columns] = jnp.broadcast_to(jnp.sum(product, axis=0, keepdims=True), (8, CHUNK))
    acc[...] = jnp.zeros_like(acc)


class FeedForward:
    def __init__(self, x, attn_out, down_cot, gain, outs, full, scratch):
        self.x, self.attn_out, self.down_cot, self.gain = x, attn_out, down_cot, gain
        self.outs, self.full = outs, full
        self.w_out, self.tiles, self.middle, self.total, self.cot_total, self.sems = scratch

    def out_copy(self):
        return pltpu.make_async_copy(self.full[0], self.w_out, self.sems.at[6])

    def tile_copies(self, t):
        columns = pl.ds(FF_TILE * t, FF_TILE)
        return [
            pltpu.make_async_copy(
                self.full[m].at[:, :, columns], self.tiles.at[t % 2, i], self.sems.at[t % 2 * 3 + i]
            )
            for i, m in enumerate((1, 2, 6))
        ]

    def load_out(self):
        self.out_copy().start()

    def load_tile(self, t):
        for copy in self.tile_copies(t):
            copy.start()

    def begin(self):
        self.out_copy().wait()
        value = self.x[...].astype(F32) + dot_nt(self.attn_out[...], self.w_out[...].reshape(1024, 2048))
        self.middle[...] = value
        self.total[...] = value
        self.outs[1][...] = (value * norm_scale(value) * self.gain[...]).astype(BF16)
        self.cot_total[...] = jnp.zeros_like(self.cot_total)

    def tile(self, t):
        mlp_in, gate_cot, up_cot, hidden = self.outs[1:5]
        for copy in self.tile_copies(t):
            copy.wait()
        w_gate, w_up, w_down = (self.tiles[t % 2, i].reshape(1024, FF_TILE) for i in range(3))
        gate = dot_nn(mlp_in[...], w_gate)
        up = dot_nn(mlp_in[...], w_up)
        sigmoid = jax.nn.sigmoid(gate)
        silu = gate * sigmoid
        hidden_tile = (silu * up).astype(BF16)
        hidden_cot = dot_nn(self.down_cot[...], w_down)
        gate_tile = (hidden_cot * up * sigmoid * (1.0 + gate * (1.0 - sigmoid))).astype(BF16)
        up_tile = (hidden_cot * silu).astype(BF16)
        columns = pl.ds(FF_TILE * t, FF_TILE)
        gate_cot[:, columns] = gate_tile
        up_cot[:, columns] = up_tile
        hidden[:, columns] = hidden_tile
        self.total[...] += dot_nt(hidden_tile, w_down)
        self.cot_total[...] += dot_nt(gate_tile, w_gate) + dot_nt(up_tile, w_up)

    def end(self):
        result, _, _, _, _, branch_cot, middle_cot, attended_cot, gain_part = self.outs
        result[...] = self.total[...].astype(BF16)
        value = self.middle[...]
        scale = norm_scale(value)
        normed = value * scale
        mlp_in_cot = self.cot_total[...]
        gain_part[...] = jnp.sum(mlp_in_cot * normed, axis=0, keepdims=True)
        scaled = mlp_in_cot * self.gain[...]
        cot = self.down_cot[...].astype(F32) + scale * (scaled - normed * mean_last(scaled * normed))
        middle_cot[...] = cot
        branch_cot[...] = cot.astype(BF16)
        attended_cot[...] = dot_nn(cot.astype(BF16), self.w_out[...].reshape(1024, 2048)).astype(BF16)


def head_columns(head):
    return (
        (pl.ds(pl.multiple_of(head * 256, 256), 256), pl.ds(0, 256)),
        (pl.ds(pl.multiple_of(head * 128, 128), 128), pl.ds(256, 128)),
        (pl.ds(pl.multiple_of(head * 128, 128), 128), pl.ds(384, 128)),
    )


def project_rows(s, low, xs, heads_w, inner, outer, query_gain, key_gain, raw, rows):
    product = dot_nn(xs[s], heads_w[...].reshape(1024, 512))
    cosine, sine = rope_rows(inner, outer, low)
    raw[s] = product[:, :384]
    for i, gain in enumerate((query_gain, query_gain, key_gain)):
        value = product[:, i * 128 : i * 128 + 128]
        value = value * norm_scale(value) * gain[...]
        value = value * cosine + pltpu.roll(value, 64, 1) * sine
        rows[s, :, i * 128 : i * 128 + 128] = value.astype(BF16)
    rows[s, :, 384:] = product[:, 384:].astype(BF16)


GATHER_AT = {
    "row 7": 2, "tile 00": 1, "tile 01": 1, "tile 11": 1, "tile 31": 1, "tile 21": 1,
    "feed 0": 1, "feed 2": 1, "feed 4": 1,
}


def forward_body(
    pair, x, attn_gain, query_gain, key_gain, inner, outer, down_cot, mlp_gain, *refs
):
    shards, refs = refs[:7], refs[7:]
    (attn_out, rows, raw, kv, mixed_t, log_total), refs = refs[:6], refs[6:]
    feed_outs, refs = refs[:9], refs[9:]
    full, refs = refs[:7], refs[7:]
    feed_scratch, refs = refs[:6], refs[6:]
    (
        xs, heads_w, queries, stacked, query_pos, key_pos, total, mixed,
        x_send, x_recv, w_send, w_recv, w_load, kv_send, kv_recv, back_send, back_recv,
    ), scratch = refs[:17], refs[17:]
    me = here()
    head = group_head(me)
    twin, across = me.sibling(), me.across()
    across_twin = across.sibling()
    others = [me.move(b=ring(me.b, d)) for d in (1, 2, 3)]
    along = [me.move(a=ring(me.a, d)) for d in (1, 2, 3)]
    z_low = me.move(zl=1 - me.zl)
    greet([twin, across, across_twin] + group_neighbours(me))
    start, spread_own, turns, pass_tile, finish_tile, finish, gather_wire = gather_turns(
        me, shards, full, scratch
    )
    turns = list(turns)

    def step(place):
        for _ in range(GATHER_AT.get(place, 0)):
            turns.pop(0)()

    x_wire = Wire(x_send, x_recv, twin)
    w_wire = Wire(w_send, w_recv, twin)
    kv_wire = Wire(kv_send, kv_recv, twin)
    back_wire = Wire(back_send, back_recv, twin)
    mine = me.zh * 2 + me.core
    qkv_shards = shards[3:6]
    loads = []
    for i, (source, target) in enumerate(head_columns(head)):
        load = pltpu.make_async_copy(qkv_shards[i].at[:, source], heads_w.at[mine, :, target], w_load.at[i])
        load.start()
        loads.append(load)
    for t, spot in enumerate((across, across_twin, twin)):
        for i, (source, target) in enumerate(head_columns(group_head(spot))):
            w_wire.push((t, i), qkv_shards[i].at[:, source], heads_w.at[mine, :, target], spot)
    inputs = x[...].astype(F32)
    xs[head] = (inputs * norm_scale(inputs) * attn_gain[...]).astype(BF16)
    x_wire.push(3, xs.at[head], xs.at[head], z_low)
    for d in (1, 3, 2):
        x_wire.push(d - 1, xs.at[head], xs.at[head], along[d - 1])
    start()
    query_positions(pair, me, query_pos)
    mixed_t[...] = jnp.zeros_like(mixed_t)
    total[...] = jnp.zeros_like(total)
    low_head = me.a + 4 * (1 - me.zl)
    x_wire.take(3, xs.at[low_head])
    for d in (1, 3, 2):
        x_wire.push(3 + d, xs.at[low_head], xs.at[low_head], along[d - 1])
    spread_own()
    for load in loads:
        load.wait()
    for t, f in enumerate(
        ((1 - me.zh) * 2 + me.core, (1 - me.zh) * 2 + 1 - me.core, me.zh * 2 + 1 - me.core)
    ):
        for i, (_, target) in enumerate(head_columns(head)):
            w_wire.take((t, i), heads_w.at[f, :, target])
    arrivals = [(None, head), (None, low_head)]
    for zl, first in ((me.zl, 0), (1 - me.zl, 4)):
        for d in (1, 3, 2):
            arrivals.append((first + d - 1, ring(me.a, -d) + 4 * zl))
    for k, (slot, s) in enumerate(arrivals):
        if slot is not None:
            x_wire.take(slot, xs.at[s])
        project_rows(
            s, low_block(pair, me, me.b, s), xs, heads_w, inner, outer, query_gain, key_gain, raw, rows
        )
        for d in range(3):
            kv_wire.push((k, d), rows.at[s, :, pl.ds(256, 256)], kv.at[me.b, s], others[d])
        kv[me.b, s] = rows[s, :, 256:]
        step(f"row {k}")
    stack_heads(lambda s: rows[s, :, :256], queries)
    for d in (0, 1, 3, 2):
        j = ring(me.b, -d)
        if d:
            for k, (_, s) in enumerate(arrivals):
                kv_wire.take((k, d - 1), kv.at[j, s])
        for part in range(2):
            mix_tile(me, j, part, pair, kv, query_pos, queries, key_pos, mixed_t, total)
            step(f"tile {d}{part}")
    finish_mix(mixed, mixed_t, log_total, stacked, total)

    def place(origin):
        return attn_out.at[:, pl.ds(pl.multiple_of(origin * 256, 256), 256)]

    for k in range(1, 8):
        peer = peer_of(head, k)
        back_wire.push(k - 1, mixed.at[peer], place(head), group_spot(me, peer))
    attn_out[:, pl.ds(pl.multiple_of(head * 256, 256), 256)] = mixed[head]
    step("back")
    feed = FeedForward(x, attn_out, down_cot, mlp_gain, feed_outs, full, feed_scratch)
    finish(0)
    feed.load_out()
    finish(1)
    finish(2)
    finish(6)
    pass_tile(0)
    pass_tile(1)
    finish_tile(0)
    feed.load_tile(0)
    for k in range(7):
        back_wire.take(k, place(peer_of(head, 7 - k)))
    feed.begin()
    for t in range(FF_STEPS):
        if t + 2 < FF_STEPS:
            pass_tile(t + 2)
        if t + 1 < FF_STEPS:
            finish_tile(t + 1)
            feed.load_tile(t + 1)
        feed.tile(t)
        step(f"feed {t}")
    feed.end()
    step("end")
    assert not turns
    for m in (3, 4, 5):
        finish(m)
    for wire in (x_wire, w_wire, kv_wire, back_wire, gather_wire):
        wire.close()


def attention_forward(pair, x, gains, tables, down_cot, mlp_gain, weights):
    narrow = jax.ShapeDtypeStruct((128, 1024), BF16)
    wide = jax.ShapeDtypeStruct((128, FF_STEPS * FF_TILE), BF16)
    outs = pl.pallas_call(
        forward_body,
        out_shape=[
            jax.ShapeDtypeStruct((128, 2048), BF16),
            jax.ShapeDtypeStruct((8, 128, 512), BF16),
            jax.ShapeDtypeStruct((8, 128, 384), F32),
            jax.ShapeDtypeStruct((4, 8, 128, 256), BF16),
            jax.ShapeDtypeStruct((128, 2048), F32),
            jax.ShapeDtypeStruct((8, 2048), F32),
            narrow, narrow, wide, wide, wide, narrow,
            jax.ShapeDtypeStruct((128, 1024), F32),
            jax.ShapeDtypeStruct((128, 2048), BF16),
            jax.ShapeDtypeStruct((1, 1024), F32),
        ]
        + [jax.ShapeDtypeStruct((4,) + w.shape, w.dtype) for w in weights],
        in_specs=[SMEM] + [VMEM] * 8 + [HBM] * 7,
        out_specs=[VMEM] * 15 + [HBM] * 7,
        scratch_shapes=[
            pltpu.VMEM((4, 256, 2048), BF16),
            pltpu.VMEM((2, 3, 4, 256, FF_TILE), BF16),
            pltpu.VMEM((128, 1024), F32),
            pltpu.VMEM((128, 1024), F32),
            pltpu.VMEM((128, 1024), F32),
            dma(7),
            pltpu.VMEM((8, 128, 1024), BF16),
            pltpu.VMEM((4, 256, 512), BF16),
            pltpu.VMEM((2048, 128), BF16),
            pltpu.VMEM((2048, 128), BF16),
            pltpu.VMEM((8, 2048), jnp.int32),
            pltpu.VMEM((TILE, CHUNK), jnp.int32),
            pltpu.VMEM((8, 2048), F32),
            pltpu.VMEM((8, 128, 256), BF16),
            dma(7), dma(7), dma(3, 3), dma(3, 3), dma(3), dma(8, 3), dma(8, 3), dma(7), dma(7),
        ]
        + gather_scratch(weights),
        compiler_params=comm_params(1),
        name="attention_forward",
    )(pair, x, *gains, *tables, down_cot, mlp_gain, *weights)
    return outs[:6], outs[6:15], [whole_rows(out) for out in outs[15:]]


def whole_rows(out):
    return out.reshape(4 * out.shape[1], out.shape[2])


PAIR_TILE = 512


def half_of(ref, half):
    width = ref.shape[-1] // 2
    return ref.at[:, :, pl.ds(half * width, width)]


def add_into(target, *sources):
    for zh in range(target.shape[0]):

        @pl.loop(0, target.shape[1] // 16)
        def _(r):
            at = pl.ds(pl.multiple_of(r * 16, 16), 16)
            total = target[zh, at, :].astype(F32)
            for source in sources:
                total = total + source[zh, at, :].astype(F32)
            target[zh, at, :] = total.astype(BF16)


class PairGrad:
    def __init__(self, me, left, right, left_scratch, twin_right, grad, wire, slot):
        self.me, self.left, self.right, self.wire, self.slot = me, left, right, wire, slot
        self.landing, self.left_t = left_scratch
        self.twin_right, self.grad = twin_right, grad

    def send(self):
        me = self.me
        twin = me.sibling()
        self.wire.push(self.slot + 2, self.right, self.twin_right, twin)
        for zh in range(0 if self.left is None else 2):
            columns = pl.ds(pl.multiple_of((zh * 2 + 1 - me.core) * 256, 256), 256)
            self.wire.push(self.slot + zh, self.left.at[:, columns], self.landing.at[zh], twin)

    def multiply(self):
        me = self.me
        for zh in range(0 if self.left is None else 2):
            columns = pl.ds(pl.multiple_of((zh * 2 + me.core) * 256, 256), 256)
            self.left_t[zh * 256 : zh * 256 + 256, 0:128] = self.left[:, columns].T
            self.wire.take(self.slot + zh, self.landing.at[zh])
            self.left_t[zh * 256 : zh * 256 + 256, 128:256] = self.landing[zh].T
        self.wire.take(self.slot + 2, self.twin_right)

        @pl.loop(0, self.twin_right.shape[1] // PAIR_TILE)
        def _(t):
            columns = pl.ds(pl.multiple_of(t * PAIR_TILE, PAIR_TILE), PAIR_TILE)
            right = jnp.concatenate([self.right[:, columns], self.twin_right[:, columns]], axis=0)
            product = dot_nn(self.left_t[...], right).astype(BF16)
            self.grad[:, :, columns] = product.reshape(2, 256, PAIR_TILE)


REDUCE_SLOTS = 13


def reduce_scratch(widths, z_first):
    scratch = []
    for k, width in enumerate(widths):
        half = width // 2
        if k in z_first:
            shapes = [
                (1, 128, half), (1, 128, half), (1, 256, half), (1, 256, half),
                (3, 1, 64, half), (1, 64, half), (3, 1, 16, half), (1, 16, half),
            ]
        else:
            shapes = [
                (2, 64, half), (2, 64, half), (2, 64, width), (2, 64, width),
                (3, 2, 16, width), (2, 16, width), (4, 16, width), (1, 16, width),
            ]
        scratch += [pltpu.VMEM(shape, BF16) for shape in shapes]
    count = len(widths)
    return scratch + [dma(count, REDUCE_SLOTS), dma(count, REDUCE_SLOTS)]


def reduce_stages(me, grads, pieces, scratch, z_first):
    wire = Wire(scratch[-2], scratch[-1], me.sibling())
    z = me.zh * 2 + me.zl
    z_low, across, z_high = me.move(zl=1 - me.zl), me.across(), me.move(zh=1 - me.zh)

    def z_spot(step):
        far = lax.rem(z + step + 4, 4)
        return me.move(zl=lax.rem(far, 2), zh=far // 2)

    def rows(ref, i, size):
        return ref.at[:, pl.ds(pl.multiple_of(i * size, size), size)]

    def ring_stages(k, slot, ahead, behind, block, bufs, half):
        far_a, far_b, in_a, in_b = bufs

        def send():
            wire.push((k, slot), half(block(2), 0), far_a, ahead)
            wire.push((k, slot + 1), half(block(2), 1), far_b, behind)
            wire.push((k, slot + 2), half(block(1), 1), half(in_a, 1), ahead)
            wire.push((k, slot + 3), half(block(-1), 0), half(in_b, 0), behind)

        def relay():
            wire.take((k, slot), far_a)
            add_into(far_a, half(block(1), 0))
            wire.push((k, slot + 4), far_a, half(in_a, 0), ahead)
            wire.take((k, slot + 1), far_b)
            add_into(far_b, half(block(-1), 1))
            wire.push((k, slot + 5), far_b, half(in_b, 1), behind)

        def collect():
            wire.take((k, slot + 2), half(in_a, 1))
            wire.take((k, slot + 3), half(in_b, 0))
            wire.take((k, slot + 4), half(in_a, 0))
            wire.take((k, slot + 5), half(in_b, 1))
            add_into(in_a, in_b, block(0))

        return send, relay, collect

    def direct_send(k, slot, axis, size, source, land):
        position = getattr(me, axis)
        for d in (1, 3, 2):
            spot = me.move(**{axis: ring(position, d)})
            wire.push((k, slot + d - 1), rows(source, ring(position, d), size), land.at[d - 1], spot)

    def direct_sum(k, slot, axis, size, source, land, target):
        for d in (1, 3, 2):
            wire.take((k, slot + d - 1), land.at[d - 1])
        own = rows(source, getattr(me, axis), size)
        for lead in range(target.shape[0]):

            @pl.loop(0, size // 16)
            def _(r):
                at = pl.ds(pl.multiple_of(r * 16, 16), 16)
                total = own[lead, at, :].astype(F32)
                for d in range(3):
                    total = total + land[d, lead, at, :].astype(F32)
                target[lead, at, :] = total.astype(BF16)

    def plain(k):
        grad, bufs = grads[k], scratch[8 * k : 8 * k + 8]
        in_a, a_land, total, z_land = bufs[2], bufs[4], bufs[5], bufs[6]
        send, relay, collect = ring_stages(
            k, 0, me.move(b=ring(me.b, 1)), me.move(b=ring(me.b, -1)),
            lambda step: rows(grad, ring(me.b, step), 64), bufs[:4], half_of,
        )

        def third():
            collect()
            direct_send(k, 6, "a", 16, in_a, a_land)

        def fourth():
            direct_sum(k, 6, "a", 16, in_a, a_land, total)
            wire.push((k, 9), total.at[1 - me.zh], z_land.at[z], across)
            wire.push((k, 10), total.at[1 - me.zh], z_land.at[z], z_high)
            wire.push((k, 11), total.at[me.zh], z_land.at[z], z_low)
            z_land[z] = total[me.zh]

        def fifth():
            for slot, spot in ((9, across), (10, z_high), (11, z_low)):
                wire.take((k, slot), z_land.at[spot.zh * 2 + spot.zl])
            total = z_land[0].astype(F32)
            for i in range(1, 4):
                total = total + z_land[i].astype(F32)
            pieces[k][0] = total.astype(BF16)

        return [send, relay, third, fourth, fifth]

    def first_z(k):
        grad, bufs = grads[k], scratch[8 * k : 8 * k + 8]
        in_a, b_land, b_sum, a_land, a_sum = bufs[2], bufs[4], bufs[5], bufs[6], bufs[7]
        width = grad.shape[2] // 2

        def columns(ref, zl):
            return ref.at[:, :, pl.ds(pl.multiple_of(zl * width, width), width)]

        def block(step):
            far = lax.rem(z + step + 4, 4)
            return columns(grad.at[pl.ds(far // 2, 1)], lax.rem(far, 2))

        send, relay, collect = ring_stages(
            k, 0, z_spot(1), z_spot(-1), block, bufs[:4],
            lambda view, i: view.at[:, pl.ds(128 * i, 128)],
        )

        def third():
            collect()
            direct_send(k, 6, "b", 64, in_a, b_land)

        def fourth():
            direct_sum(k, 6, "b", 64, in_a, b_land, b_sum)
            direct_send(k, 9, "a", 16, b_sum, a_land)

        def fifth():
            direct_sum(k, 9, "a", 16, b_sum, a_land, a_sum)
            place = columns(pieces[k], me.zl)
            place[...] = a_sum[...]
            wire.push((k, 12), a_sum, place, z_low)

        def sixth():
            wire.take((k, 12), columns(pieces[k], 1 - me.zl))

        return [send, relay, third, fourth, fifth, sixth]

    lists = [first_z(k) if k in z_first else plain(k) for k in range(len(grads))]
    return lists, wire


def replicate_stages(me, pieces, outs, send, recv, load_sem):
    wire = Wire(send, recv, me.sibling())
    loads = {}

    def cut(k, row, rows, half=None):
        width = outs[k].shape[1] // 2
        at = pl.ds(pl.multiple_of(row, 16), rows)
        if half is None:
            return outs[k].at[at]
        return outs[k].at[at, pl.ds(half * width, width)]

    b_next, b_prev = me.move(b=ring(me.b, 1)), me.move(b=ring(me.b, -1))

    def a_row(step):
        return (me.b * 4 + ring(me.a, step)) * 16

    def b_row(step):
        return ring(me.b, step) * 64

    def a_send(k):
        place = cut(k, a_row(0), 16)
        for d in (1, 3, 2):
            wire.push((k, d - 1), pieces[k].at[0], place, me.move(a=ring(me.a, d)))
        loads[k] = pltpu.make_async_copy(pieces[k].at[0], place, load_sem.at[k])
        loads[k].start()

    def b_send(k):
        for d in (1, 3, 2):
            wire.take((k, d - 1), cut(k, a_row(-d), 16))
        loads[k].wait()
        mine = cut(k, b_row(0), 64)
        wire.push((k, 4), mine, mine, b_next)
        wire.push((k, 5), mine, mine, b_prev)

    def b_relay(k):
        wire.take((k, 4), cut(k, b_row(-1), 64))
        wire.push((k, 6), cut(k, b_row(-1), 64, 0), cut(k, b_row(-1), 64, 0), b_next)
        wire.take((k, 5), cut(k, b_row(1), 64))
        wire.push((k, 7), cut(k, b_row(1), 64, 1), cut(k, b_row(1), 64, 1), b_prev)

    def b_collect(k):
        wire.take((k, 6), cut(k, b_row(2), 64, 0))
        wire.take((k, 7), cut(k, b_row(2), 64, 1))

    stages = (a_send, b_send, b_relay, b_collect)
    lists = [[functools.partial(stage, k) for stage in stages] for k in range(len(pieces))]
    return lists, wire


class Plan:
    def __init__(self, **lists):
        self.lists = {name: list(stages) for name, stages in lists.items()}

    def run(self, names):
        for name in names:
            self.lists[name].pop(0)()

    def check(self):
        assert not any(self.lists.values())


def gain_turns(me, gains, gains_out, gain_slots, gain_send, gain_recv):
    first = me.core == 0
    x, y = jnp.where(first, me.a, me.b), jnp.where(first, me.b, me.a)
    z = me.zh * 2 + me.zl
    wire = Wire(gain_send, gain_recv, me.sibling())

    def pick(d, on_x):
        use_a = first if on_x else jnp.logical_not(first)
        return me.move(
            a=jnp.where(use_a, ring(me.a, d), me.a), b=jnp.where(use_a, me.b, ring(me.b, d))
        )

    def z_spot(d):
        far = lax.rem(z + d, 4)
        return me.move(zl=lax.rem(far, 2), zh=far // 2)

    def push(stage, position, spots):
        for d, spot in enumerate(spots):
            slot = gain_slots.at[stage, position]
            wire.push((stage, d), slot, slot, spot)

    def take(stage, position, size):
        for d in range(size - 1):
            wire.take((stage, d), gain_slots.at[stage, lax.rem(position + size - 1 - d, size)])

    def total(stage):
        return (gain_slots[stage, 0] + gain_slots[stage, 1]) + (gain_slots[stage, 2] + gain_slots[stage, 3])

    def turn0():
        gain_slots[0, me.core] = gains[...]
        push(0, me.core, [me.sibling()])

    def turn1():
        take(0, me.core, 2)
        gain_slots[1, x] = gain_slots[0, 0] + gain_slots[0, 1]
        push(1, x, [pick(d, True) for d in (1, 2, 3)])

    def turn2():
        take(1, x, 4)
        gain_slots[2, y] = total(1)
        push(2, y, [pick(d, False) for d in (1, 2, 3)])

    def turn3():
        take(2, y, 4)
        gain_slots[3, z] = total(2)
        push(3, z, [z_spot(d) for d in (1, 2, 3)])

    def turn4():
        take(3, z, 4)
        gains_out[...] = total(3)

    return [turn0, turn1, turn2, turn3, turn4], wire.close


def unrope(s, low, grads, raw, inner, outer, gain, column, gain_part):
    cosine, sine = rope_rows(inner, outer, low)
    value = raw[s, :, column : column + 128]
    scale = norm_scale(value)
    hat = value * scale
    hat_cot = grads * cosine - pltpu.roll(grads, 64, 1) * sine
    gain_part[...] += jnp.sum((hat_cot * hat).reshape(16, 8, 128), axis=0)
    scaled = hat_cot * gain[...]
    return (scale * (scaled - hat * mean_last(scaled * hat))).astype(BF16)


WIDTHS = (3072, 3072, 3072, 2048, 2048, 2048)
Z_FIRST = (2, 3, 4)
BETWEEN = {
    "cots": "ddgguoou",
    "tiles": "dg",
    "own tile": "",
    "rows 2": "",
    "rows 4": "",
    "rows 6": "",
    "rows 0": "guodug",
    "proj": "qdkkoukdquugoddkqugok",
    "weights": "d",
    "input": "qkkousdsqgoksqqqdsogqkgoqsuoqk",
}


def backward_body(*refs):
    (
        pair, x, attn_gain, query_gain, key_gain, inner, outer, rows, raw, kv, mixed_t, log_total, parts,
        mlp_in, down_cot, branch_cot, gate_cot, up_cot, hidden, attn_out, middle_cot, mlp_gain_part, wq, wk, wv,
    ), refs = refs[:25], refs[25:]
    (input_cot, gains_out), outs, refs = refs[:2], refs[2:8], refs[8:]
    (
        cots_in, dkv, queries, cots, deltas, query_pos, key_pos, probs_all, score_cots, acc, held, stacked, message,
        attn_in, proj, head_gains, gains, gain_slots,
        cot_send, cot_recv, p_send, p_recv, m_send, m_recv, w_send, w_recv, out_send, out_recv, out_load, w_load,
        gain_send, gain_recv,
    ), refs = refs[:32], refs[32:]
    pieces, grads, refs = refs[:6], list(refs[6:11]), refs[11:]
    grads.append(grads[2].at[:, :, pl.ds(0, WIDTHS[5])])
    me = here()
    head = group_head(me)
    twin = me.sibling()
    others = [me.move(b=ring(me.b, d)) for d in (1, 2, 3)]
    greet([twin, me.across(), me.move(zh=1 - me.zh)] + group_neighbours(me))
    cot_wire = Wire(cot_send, cot_recv, twin)
    p_wire = Wire(p_send, p_recv, twin)
    m_wire = Wire(m_send, m_recv, twin)
    w_wire = Wire(w_send, w_recv, twin)

    def of_head(ref, h):
        return ref.at[:, pl.ds(pl.multiple_of(h * 256, 256), 256)]

    for k in range(1, 8):
        peer = peer_of(head, k)
        cot_wire.push(k - 1, of_head(parts, peer), cots_in.at[head], group_spot(me, peer))
    lefts = (mlp_in, None, down_cot, branch_cot, attn_in, None)
    rights = (
        gate_cot, up_cot, hidden, attn_out, proj.at[:, pl.ds(0, 2048)], proj.at[:, pl.ds(2048, 2048)]
    )
    held_lefts, twin_rights, refs = refs[:8], refs[8:14], refs[14:]
    pairs = []
    for i, share in enumerate((0, 0, 1, 2, 3, 3)):
        pairs.append(
            PairGrad(
                me, lefts[i], rights[i], held_lefts[2 * share : 2 * share + 2], twin_rights[i], grads[i], w_wire, 3 * i
            )
        )
    sums, sum_wire = reduce_stages(me, grads, pieces, refs, Z_FIRST)
    copies, out_wire = replicate_stages(me, pieces, outs, out_send, out_recv, out_load)
    small, gain_finish = gain_turns(me, gains, gains_out, gain_slots, gain_send, gain_recv)
    plan = Plan(s=small, **{
        name: [pairs[i].multiply] + sums[i] + copies[i] for i, name in enumerate("gudoqk")
    })
    for i in (2, 0, 1, 3):
        pairs[i].send()
    query_positions(pair, me, query_pos)
    cots_in[head] = parts[:, pl.ds(pl.multiple_of(head * 256, 256), 256)]
    head_gains[...] = jnp.zeros_like(head_gains)
    inputs = x[...].astype(F32)
    scale = norm_scale(inputs)
    normed = inputs * scale
    attn_in[...] = (normed * attn_gain[...]).astype(BF16)
    plan.run(BETWEEN["cots"])
    for k in range(7):
        cot_wire.take(k, cots_in.at[peer_of(head, 7 - k)])
    start_grad(rows, mixed_t, cots_in, queries, cots, deltas, acc)
    for d in (2, 1, 3, 0):
        j = ring(me.b, d)
        if d == 0:
            plan.run(BETWEEN["tiles"])
        for part in range(2):
            grad_tile(
                me, j, part, pair, kv, query_pos, queries, cots, deltas, log_total, key_pos,
                probs_all, score_cots, acc, dkv,
            )
        if d:
            for k in range(8):
                peer = peer_of(head, k)
                p_wire.push((k, d - 1), dkv.at[j, peer], held.at[d - 1, peer], others[d - 1])
    for chunk in range(8):
        columns = pl.ds(chunk * CHUNK, CHUNK)
        stacked[columns, :] = (acc[:, columns] * SCORE_SCALE).T
    plan.run(BETWEEN["own tile"])

    def places(h):
        return (
            (pl.ds(0, 256), pl.ds(pl.multiple_of(h * 256, 256), 256)),
            (pl.ds(256, 128), pl.ds(pl.multiple_of(2048 + h * 128, 128), 128)),
            (pl.ds(384, 128), pl.ds(pl.multiple_of(3072 + h * 128, 128), 128)),
        )

    for k in (1, 2, 3, 4, 5, 6, 7, 0):
        s = peer_of(head, k)
        low = low_block(pair, me, me.b, s)
        for d in range(3):
            p_wire.take((k, d), held.at[d, s])
        for h in range(2):
            turned = jnp.concatenate(
                [
                    stacked[pl.ds(pl.multiple_of(part * 1024 + s * 128 + h * 64, 64), 64), :]
                    for part in range(2)
                ],
                axis=0,
            )
            message[s, :, h * 128 : h * 128 + 128] = unrope(
                s, low, turned, raw, inner, outer, query_gain, h * 128, head_gains.at[0]
            )
        total = (
            dkv[me.b, s].astype(F32)
            + held[0, s].astype(F32)
            + held[1, s].astype(F32)
            + held[2, s].astype(F32)
        )
        message[s, :, 256:384] = unrope(
            s, low, total[:, :128], raw, inner, outer, key_gain, 256, head_gains.at[1]
        )
        message[s, :, 384:] = total[:, 128:].astype(BF16)
        if k:
            for i, (source, target) in enumerate(places(head)):
                m_wire.push((k - 1, i), message.at[s, :, source], proj.at[:, target], group_spot(me, s))
        if k % 2 == 0:
            plan.run(BETWEEN[f"rows {k}"])
    for source, target in places(head):
        proj[:, target] = message[head, :, source]
    for k in range(7):
        for i, (_, target) in enumerate(places(peer_of(head, 7 - k))):
            m_wire.take((k, i), proj.at[:, target])
    for i in (4, 5):
        pairs[i].send()
    for k in range(3):
        sum_wire.settle(k)
    plan.run(BETWEEN["proj"])

    loads = []
    value_rows = (score_cots, probs_all)
    for i in range(4):
        at = pl.ds(256 * i, 256)
        target = grads[i // 2].at[i % 2]
        loads.append((wq.at[at], target.at[:, pl.ds(0, 2048)]))
        loads.append((wk.at[at], target.at[:, pl.ds(2048, 1024)]))
        loads.append((wv.at[at], value_rows[i // 2].at[pl.ds(i % 2 * 256, 256)]))
    loads = [pltpu.make_async_copy(*pair_, w_load.at[i]) for i, pair_ in enumerate(loads)]
    for load in loads:
        load.start()
    plan.run(BETWEEN["weights"])
    for load in loads:
        load.wait()
    attn_in_cot = jnp.concatenate(
        [
            dot_nt(proj[:, :3072], grads[i // 2][i % 2])
            + dot_nt(proj[:, 3072:], value_rows[i // 2][i % 2 * 256 : i % 2 * 256 + 256, :])
            for i in range(4)
        ],
        axis=1,
    )
    scaled = attn_in_cot * attn_gain[...]
    input_cot[...] = middle_cot[...] + scale * (scaled - normed * mean_last(scaled * normed))
    gains[...] = jnp.zeros_like(gains)
    gains[0:1, :] = jnp.sum(attn_in_cot * normed, axis=0, keepdims=True)
    gains[1:2, :] = mlp_gain_part[...]
    for i in range(2):
        gains[2 + i : 3 + i, 0:128] = jnp.sum(head_gains[i], axis=0, keepdims=True)
    plan.run(BETWEEN["input"])
    plan.check()
    gain_finish()
    for wire in (cot_wire, p_wire, m_wire, w_wire, sum_wire, out_wire):
        wire.close()


def attention_backward(pair, x, gains, tables, kept, attended_cot, lefts, rights, middle_cot, mlp_gain_part, weights):
    heads = (8, 128, 256)
    count = len(WIDTHS)
    outs = pl.pallas_call(
        backward_body,
        out_shape=[jax.ShapeDtypeStruct((128, 1024), F32), jax.ShapeDtypeStruct((4, 1024), F32)]
        + [jax.ShapeDtypeStruct((256, width), BF16) for width in WIDTHS],
        in_specs=[SMEM] + [VMEM] * 21 + [HBM] * 3,
        out_specs=[VMEM] * 2 + [HBM] * count,
        scratch_shapes=[
            pltpu.VMEM(heads, BF16),
            pltpu.VMEM((4,) + heads, BF16),
            pltpu.VMEM((2048, 128), BF16),
            pltpu.VMEM((2048, 128), BF16),
            pltpu.VMEM((8, 2048), F32),
            pltpu.VMEM((8, 2048), jnp.int32),
            pltpu.VMEM((TILE, CHUNK), jnp.int32),
            pltpu.VMEM((TILE, 1024), BF16),
            pltpu.VMEM((TILE, 1024), BF16),
            pltpu.VMEM((128, 2048), F32),
            pltpu.VMEM((3,) + heads, BF16),
            pltpu.VMEM((2048, 128), F32),
            pltpu.VMEM((8, 128, 512), BF16),
            pltpu.VMEM((128, 1024), BF16),
            pltpu.VMEM((128, 4096), BF16),
            pltpu.VMEM((2, 8, 128), F32),
            pltpu.VMEM((4, 1024), F32),
            pltpu.VMEM((4, 4, 4, 1024), F32),
            dma(7), dma(7), dma(8, 3), dma(8, 3), dma(7, 3), dma(7, 3), dma(18), dma(18),
            dma(count, 8), dma(count, 8), dma(count), dma(12), dma(4, 3), dma(4, 3),
        ]
        + [pltpu.VMEM((1, 16, width), BF16) for width in WIDTHS]
        + [pltpu.VMEM((2, 256, width), BF16) for width in WIDTHS[:5]]
        + [pltpu.VMEM((2, 128, 256), BF16), pltpu.VMEM((512, 256), BF16)] * 4
        + [pltpu.VMEM((128, width), BF16) for width in WIDTHS]
        + reduce_scratch(WIDTHS, Z_FIRST),
        compiler_params=comm_params(2, 62 * 1024 * 1024),
        name="attention_backward",
    )(pair, x, *gains, *tables, *kept, attended_cot, *lefts, *rights, middle_cot, mlp_gain_part, *weights)
    return outs[0], outs[1], outs[2:]


WIDEN_STEPS = 8


def widen_body(
    result, input_cot, gate, up, down, out, query, key_value, gains,
    result_out, input_out, query_out, key_out, value_out, out_out, gate_out, up_out, down_out, g0, g1, g2, g3,
):
    result_out[0] = result[...]
    input_out[0] = input_cot[...]
    for source, target in ((query, query_out), (out, out_out), (gate, gate_out), (up, up_out), (down, down_out)):
        target[...] = source[...].astype(F32)
    key_out[...] = key_value[:, :1024].astype(F32)
    value_out[...] = key_value[:, 1024:].astype(F32)
    for i, target in enumerate((g0, g1, g2, g3)):
        target[...] = gains[i : i + 1, : target.shape[1]]


def widen_results(result, input_cot, grads, gains):
    def rows(array_shape):
        block = (array_shape[0] // WIDEN_STEPS,) + array_shape[1:]
        return pl.BlockSpec(block, lambda t: (t, 0))

    def split(array_shape):
        block = (1, array_shape[1] // WIDEN_STEPS, array_shape[2])
        return pl.BlockSpec(block, lambda t: (0, t, 0))

    def whole(array_shape):
        return pl.BlockSpec(array_shape, lambda t: (0, 0))

    tokens = (1, 128, 1024)
    widths = (2048, 1024, 1024, 2048, 3072, 3072, 3072)
    lengths = (1024, 1024, 128, 128)
    outs = pl.pallas_call(
        widen_body,
        grid=(WIDEN_STEPS,),
        out_shape=[jax.ShapeDtypeStruct(tokens, BF16), jax.ShapeDtypeStruct(tokens, F32)]
        + [jax.ShapeDtypeStruct((256, width), F32) for width in widths]
        + [jax.ShapeDtypeStruct((1, length), F32) for length in lengths],
        in_specs=[rows((128, 1024)), rows((128, 1024))]
        + [rows(grad.shape) for grad in grads]
        + [whole(gains.shape)],
        out_specs=[split(tokens), split(tokens)]
        + [rows((256, width)) for width in widths]
        + [whole((1, length)) for length in lengths],
        compiler_params=pltpu.CompilerParams(vmem_limit_bytes=VMEM_LIMIT),
        name="widen_results",
    )(result, input_cot, *grads, gains)
    return tuple(outs[:9]) + tuple(out[0] for out in outs[9:])


def shards(
    tokens,
    query_weight,
    key_weight,
    value_weight,
    out_weight,
    gate_weight,
    up_weight,
    down_weight,
    attn_gain,
    mlp_gain,
    query_gain,
    key_gain,
    pair_order,
    out_grad,
):
    tables = rope_tables()
    attn_row, query_row, key_row = attn_gain[None], query_gain[None], key_gain[None]
    down_cot = out_grad[0]
    (attn_out, *kept), feed, full = attention_forward(
        pair_order,
        tokens[0],
        (attn_row, query_row, key_row),
        tables,
        down_cot,
        mlp_gain[None],
        [out_weight, gate_weight, up_weight, query_weight, key_weight, value_weight, down_weight],
    )
    result, mlp_in, gate_cot, up_cot, hidden, branch_cot, middle_cot, attended_cot, mlp_gain_part = feed
    full_qkv = full[3:6]
    input_cot, gains, grads = attention_backward(
        pair_order,
        tokens[0],
        (attn_row, query_row, key_row),
        tables,
        kept,
        attended_cot,
        (mlp_in, down_cot, branch_cot),
        (gate_cot, up_cot, hidden, attn_out),
        middle_cot,
        mlp_gain_part,
        full_qkv,
    )
    return widen_results(result, input_cot, grads, gains)


def solution(mesh):
    rows, split, whole = P("fsdp", None), P("fsdp", "ctx", None), P()
    return jax.shard_map(
        shards,
        mesh=mesh,
        in_specs=(split,) + (rows,) * 7 + (whole,) * 4 + (rows, split),
        out_specs=(split, split) + (rows,) * 7 + (whole,) * 4,
        check_vma=False,
    )
```

```python
import functools

import jax
import jax.numpy as jnp
import numpy as np
from jax import lax
from jax.experimental import pallas as pl
from jax.experimental.pallas import tpu as pltpu
from jax.sharding import PartitionSpec as P

EPSILON = 1e-06
ROPE_BASE = 1000000.0
MESH = pl.DeviceIdType.MESH
HBM = pl.BlockSpec(memory_space=pltpu.HBM)
VMEM = pl.BlockSpec(memory_space=pltpu.VMEM)
SMEM = pl.BlockSpec(memory_space=pltpu.SMEM)
LOG2E = 1.4426950408889634
VMEM_LIMIT = 56 * 1024 * 1024
BF16 = jnp.bfloat16
F32 = jnp.float32


class Spot:
    def __init__(self, a, b, zl, zh, core):
        self.a, self.b, self.zl, self.zh, self.core = a, b, zl, zh, core

    def move(self, a=None, b=None, zl=None, zh=None):
        return Spot(
            self.a if a is None else a,
            self.b if b is None else b,
            self.zl if zl is None else zl,
            self.zh if zh is None else zh,
            self.core,
        )

    def id(self):
        first = self.core == 0
        x = jnp.where(first, self.a, self.b)
        y = jnp.where(first, self.b, self.a)
        return (self.zl * 16 + y * 4 + x, self.zh * 2 + self.core)

    def sibling(self):
        return Spot(self.b, self.a, self.zl, self.zh, 1 - self.core)

    def across(self):
        return self.move(zl=1 - self.zl, zh=1 - self.zh)


def here():
    ctx = lax.axis_index("ctx")
    fsdp = lax.axis_index("fsdp")
    x = lax.rem(ctx, 4)
    y = lax.rem(ctx // 4, 4)
    core = lax.rem(fsdp, 2)
    first = core == 0
    return Spot(jnp.where(first, x, y), jnp.where(first, y, x), ctx // 16, fsdp // 2, core)


def ring(position, step):
    return lax.rem(position + step + 4, 4)


def greet(spots):
    barrier = pltpu.get_barrier_semaphore()
    for spot in spots:
        pl.semaphore_signal(barrier, inc=1, device_id=spot.id(), device_id_type=MESH)
    pl.semaphore_wait(barrier, len(spots))


def remote(src, dst, send_sem, recv_sem, spot):
    return pltpu.make_async_remote_copy(
        src_ref=src,
        dst_ref=dst,
        send_sem=send_sem,
        recv_sem=recv_sem,
        device_id=spot.id(),
        device_id_type=MESH,
    )


def comm_params(collective_id, limit=VMEM_LIMIT):
    return pltpu.CompilerParams(
        collective_id=collective_id, has_side_effects=True, vmem_limit_bytes=limit
    )


class Wire:
    def __init__(self, send, recv, spot):
        self.send, self.recv, self.spot, self.sent = send, recv, spot, []

    def push(self, slot, src, dst, spot):
        copy = remote(src, dst, self.send.at[slot], self.recv.at[slot], spot)
        copy.start()
        self.sent.append((slot, copy))

    def take(self, slot, dst):
        remote(dst, dst, self.send.at[slot], self.recv.at[slot], self.spot).wait_recv()

    def settle(self, k):
        for slot, copy in self.sent:
            if slot[0] == k:
                copy.wait_send()
        self.sent = [(slot, copy) for slot, copy in self.sent if slot[0] != k]

    def close(self):
        for _, copy in self.sent:
            copy.wait_send()


def pipeline(stages, count):
    def turn(t):
        for depth, stage in enumerate(stages):
            if 0 <= t - depth < count:
                stage(t - depth)

    return [functools.partial(turn, t) for t in range(count + len(stages) - 1)]


GATHER_SLOTS = 14
FF_TILE = 512
FF_STEPS = 6


def gather_scratch(weights):
    count = len(weights)
    return [pltpu.VMEM(w.shape, w.dtype) for w in weights] + [
        pltpu.SemaphoreType.DMA((count, GATHER_SLOTS)),
        pltpu.SemaphoreType.DMA((count, GATHER_SLOTS)),
        pltpu.SemaphoreType.DMA((2, count)),
    ]


def gather_turns(me, ins, outs, scratch):
    count = len(ins)
    held, (send, recv, local_sem) = scratch[:count], scratch[count:]
    mine = me.zh * 2 + me.core
    other = (1 - me.zh) * 2 + me.core
    twin_mine = me.zh * 2 + 1 - me.core
    twin_other = (1 - me.zh) * 2 + 1 - me.core
    twin, across = me.sibling(), me.across()
    a_next, a_prev = me.move(a=ring(me.a, 1)), me.move(a=ring(me.a, -1))
    b_next, b_prev = me.move(b=ring(me.b, 1)), me.move(b=ring(me.b, -1))
    wire = Wire(send, recv, twin)

    def cut(m, rows, half):
        width = ins[m].shape[1] // 2
        if half is None:
            return outs[m].at[other, rows]
        return outs[m].at[other, rows, pl.ds(half * width, width)]

    def piece(m, a, half=None):
        return cut(m, pl.ds(pl.multiple_of((me.b * 4 + a) * 16, 16), 16), half)

    def block(m, b, half=None):
        return cut(m, pl.ds(pl.multiple_of(b * 64, 64), 64), half)

    def push(m, slot, src, dst, spot):
        wire.push((m, slot), src, dst, spot)

    def take(m, slot, dst):
        wire.take((m, slot), dst)

    loads = [pltpu.make_async_copy(ins[m], held[m], local_sem.at[0, m]) for m in range(count)]
    stores = [pltpu.make_async_copy(held[m], outs[m].at[mine], local_sem.at[1, m]) for m in range(count)]

    last = count - 1

    def start():
        for m in range(last):
            rows = pl.ds(pl.multiple_of((me.b * 4 + me.a) * 16, 16), 16)
            push(m, 0, ins[m].at[rows], outs[m].at[mine, rows], across)
        for t in range(FF_STEPS):
            columns = pl.ds(FF_TILE * t, FF_TILE)
            push(last, t, ins[last].at[:, columns], outs[last].at[mine, :, columns], across)
        for load in loads:
            load.start()

    def spread_own():
        for m in range(count):
            loads[m].wait()
            stores[m].start()
            push(m, 2 * FF_STEPS if m == last else 9, ins[m], outs[m].at[mine], twin)

    def stage_z(m):
        take(m, 0, piece(m, me.a))
        push(m, 1, piece(m, me.a), piece(m, me.a), a_next)
        push(m, 2, piece(m, me.a), piece(m, me.a), a_prev)

    def stage_a(m):
        left, right = ring(me.a, -1), ring(me.a, 1)
        take(m, 1, piece(m, left))
        push(m, 3, piece(m, left, 0), piece(m, left, 0), a_next)
        take(m, 2, piece(m, right))
        push(m, 4, piece(m, right, 1), piece(m, right, 1), a_prev)

    def stage_b(m):
        far = ring(me.a, 2)
        take(m, 3, piece(m, far, 0))
        take(m, 4, piece(m, far, 1))
        push(m, 5, block(m, me.b), block(m, me.b), b_next)
        push(m, 6, block(m, me.b), block(m, me.b), b_prev)
        push(m, 10, block(m, me.b), block(m, me.b), twin)

    def stage_c(m):
        left, right = ring(me.b, -1), ring(me.b, 1)
        take(m, 5, block(m, left))
        push(m, 7, block(m, left, 0), block(m, left, 0), b_next)
        push(m, 11, block(m, left), block(m, left), twin)
        take(m, 6, block(m, right))
        push(m, 8, block(m, right, 1), block(m, right, 1), b_prev)
        push(m, 12, block(m, right), block(m, right), twin)

    def stage_d(m):
        far = ring(me.b, 2)
        take(m, 7, block(m, far, 0))
        take(m, 8, block(m, far, 1))
        push(m, 13, block(m, far), block(m, far), twin)

    def pass_tile(t):
        tile = outs[last].at[other, :, pl.ds(FF_TILE * t, FF_TILE)]
        take(last, t, tile)
        push(last, FF_STEPS + t, tile, tile, twin)

    def finish_tile(t):
        take(last, FF_STEPS + t, outs[last].at[twin_other, :, pl.ds(FF_TILE * t, FF_TILE)])

    def finish(m):
        take(m, 2 * FF_STEPS if m == last else 9, outs[m].at[twin_mine])
        stores[m].wait()
        if m < last:
            for slot, step in ((10, 0), (11, -1), (12, 1), (13, 2)):
                rows = pl.ds(pl.multiple_of(ring(me.a, step) * 64, 64), 64)
                take(m, slot, outs[m].at[twin_other, rows])

    turns = pipeline((stage_z, stage_a, stage_b, stage_c, stage_d), last)
    return start, spread_own, turns, pass_tile, finish_tile, finish, wire


def group_spot(me, head):
    return me.move(a=lax.rem(head, 4), zl=head // 4)


def group_head(me):
    return me.a + 4 * me.zl


def peer_of(head, k):
    return lax.rem(head + k, 8)


def group_neighbours(me):
    head = group_head(me)
    return [group_spot(me, peer_of(head, k)) for k in range(1, 8)] + [
        me.move(b=ring(me.b, d)) for d in (1, 2, 3)
    ]


def dma(*shape):
    return pltpu.SemaphoreType.DMA(shape)


TILE = 512
CHUNK = 256
SCORE_SCALE = 128.0**-0.5


def dot_nt(left, right):
    return lax.dot_general(left, right, (((1,), (1,)), ((), ())), preferred_element_type=F32)


def dot_nn(left, right):
    return lax.dot_general(left, right, (((1,), (0,)), ((), ())), preferred_element_type=F32)


def stack_heads(read, target):
    for s in range(8):
        rows = read(s)
        for part in range(2):
            for head in range(2):
                at = part * 1024 + s * 128 + head * 64
                target[at : at + 64, :] = rows[part * 64 : part * 64 + 64, head * 128 : head * 128 + 128]


def unstack_heads(stacked, s, out):
    for part in range(2):
        for head in range(2):
            at = part * 1024 + s * 128 + head * 64
            out[s, part * 64 : part * 64 + 64, head * 128 : head * 128 + 128] = stacked[at : at + 64, :]


def low_block(pair, me, j, s):
    a = lax.rem(s, 4)
    first = me.core == 0
    return pair[0, (s // 4) * 16 + jnp.where(first, j * 4 + a, a * 4 + j)]


def key_positions(pair, me, j, part, target):
    line = lax.broadcasted_iota(jnp.int32, (64, CHUNK), 0)
    for s in range(8):
        low = low_block(pair, me, j, s)
        block = low if part == 0 else 63 - low
        target[s * 64 : s * 64 + 64, :] = line + block * 64


def query_positions(pair, me, target):
    line = lax.rem(lax.broadcasted_iota(jnp.int32, (8, 128), 1), 64)
    for s in range(8):
        low = low_block(pair, me, me.b, s)
        target[:, s * 128 : s * 128 + 128] = line + low * 64
        target[:, 1024 + s * 128 : 1152 + s * 128] = line + (63 - low) * 64


def rope_tables():
    frequency = ROPE_BASE ** (-np.arange(0, 128, 2, dtype=np.float64) / 128)
    frequency = np.concatenate([frequency, frequency])
    sign = np.where(np.arange(128) < 64, -1.0, 1.0)
    inner = np.arange(64, dtype=np.float64)[:, None] * frequency
    outer = inner * 64.0
    make = lambda angles: jnp.asarray(np.stack([np.cos(angles), np.sin(angles) * sign]), F32)
    return make(inner), make(outer)


def rope_rows(inner, outer, low):
    cosines, sines = [], []
    for block in (low, 63 - low):
        cos_b, sin_b = outer[0, pl.ds(block, 1), :], outer[1, pl.ds(block, 1), :]
        cosines.append(cos_b * inner[0] - sin_b * inner[1])
        sines.append(sin_b * inner[0] + cos_b * inner[1])
    return jnp.concatenate(cosines, axis=0), jnp.concatenate(sines, axis=0)


def mean_last(value):
    return jnp.mean(value, axis=-1, keepdims=True)


def norm_scale(value):
    return lax.rsqrt(mean_last(value * value) + EPSILON)


def tile_rows(kv, j, part, start):
    return kv[j, :, part * 64 : part * 64 + 64, start : start + 128].reshape(TILE, 128)


def tile_probs(scores, masked, key_pos, query_pos, columns, shift=None):
    logits = scores * (LOG2E * SCORE_SCALE)
    if shift is not None:
        logits = logits - shift
    probs = jnp.exp2(logits)
    if masked:
        probs = jnp.where(key_pos[...] <= query_pos[0:1, columns], probs, 0.0)
    return probs


def mix_tile(me, j, part, pair, kv, query_pos, queries, key_pos, acc, total):
    key_positions(pair, me, j, part, key_pos)
    keys = tile_rows(kv, j, part, 0)
    values_t = tile_rows(kv, j, part, 128).T
    for chunk in range(4 * part, 8):
        columns = pl.ds(chunk * CHUNK, CHUNK)
        masked = part == 1 or chunk < 4
        probs = tile_probs(dot_nt(keys, queries[columns, :]), masked, key_pos, query_pos, columns)
        total[:, columns] += jnp.sum(probs.reshape(TILE // 8, 8, CHUNK), axis=0)
        acc[:, columns] += dot_nn(values_t, probs.astype(BF16))


def finish_mix(out, mixed_t, log_total, stacked, total):
    for chunk in range(8):
        columns = pl.ds(chunk * CHUNK, CHUNK)
        full = jnp.sum(total[:, columns], axis=0, keepdims=True)
        log_total[:, columns] = jnp.broadcast_to(jnp.log2(full), (8, CHUNK))
        mixed = mixed_t[:, columns] / full
        mixed_t[:, columns] = mixed
        stacked[columns, :] = mixed.T.astype(BF16)
    for s in range(8):
        unstack_heads(stacked, s, out)


def grad_tile(
    me, j, part, pair, kv, query_pos, queries, cots, deltas, log_total, key_pos, probs_all, score_cots, acc, dkv
):
    key_positions(pair, me, j, part, key_pos)
    keys = tile_rows(kv, j, part, 0)
    values = tile_rows(kv, j, part, 128)
    keys_t = keys.T
    key_cot, value_cot = 0.0, 0.0
    for first in range(part, 2):
        for chunk in range(4 * first, 4 * first + 4):
            columns = pl.ds(chunk * CHUNK, CHUNK)
            local = pl.ds((chunk - 4 * first) * CHUNK, CHUNK)
            masked = part == first
            scores = dot_nt(keys, queries[columns, :])
            prob_cot = dot_nt(values, cots[columns, :])
            probs = tile_probs(scores, masked, key_pos, query_pos, columns, log_total[0:1, columns])
            score_cot = (probs * (prob_cot - deltas[0:1, columns])).astype(BF16)
            probs_all[:, local] = probs.astype(BF16)
            score_cots[:, local] = score_cot
            acc[:, columns] += dot_nn(keys_t, score_cot)
        rows = pl.ds(1024 * first, 1024)
        key_cot = key_cot + dot_nn(score_cots[...], queries[rows, :])
        value_cot = value_cot + dot_nn(probs_all[...], cots[rows, :])
    key_cot = key_cot * SCORE_SCALE
    at = part * 64
    dkv[j, :, at : at + 64, 0:128] = key_cot.astype(BF16).reshape(8, 64, 128)
    dkv[j, :, at : at + 64, 128:256] = value_cot.astype(BF16).reshape(8, 64, 128)


def start_grad(rows, mixed_t, cots_in, queries, cots, deltas, acc):
    stack_heads(lambda s: rows[s, :, :256], queries)
    stack_heads(lambda s: cots_in[s], cots)
    for chunk in range(8):
        columns = pl.ds(chunk * CHUNK, CHUNK)
        product = cots[columns, :].astype(F32).T * mixed_t[:, columns]
        deltas[:, columns] = jnp.broadcast_to(jnp.sum(product, axis=0, keepdims=True), (8, CHUNK))
    acc[...] = jnp.zeros_like(acc)


class FeedForward:
    def __init__(self, x, attn_out, down_cot, gain, outs, full, scratch):
        self.x, self.attn_out, self.down_cot, self.gain = x, attn_out, down_cot, gain
        self.outs, self.full = outs, full
        self.w_out, self.tiles, self.middle, self.total, self.cot_total, self.sems = scratch

    def out_copy(self):
        return pltpu.make_async_copy(self.full[0], self.w_out, self.sems.at[6])

    def tile_copies(self, t):
        columns = pl.ds(FF_TILE * t, FF_TILE)
        return [
            pltpu.make_async_copy(
                self.full[m].at[:, :, columns], self.tiles.at[t % 2, i], self.sems.at[t % 2 * 3 + i]
            )
            for i, m in enumerate((1, 2, 6))
        ]

    def load_out(self):
        self.out_copy().start()

    def load_tile(self, t):
        for copy in self.tile_copies(t):
            copy.start()

    def begin(self):
        self.out_copy().wait()
        value = self.x[...].astype(F32) + dot_nt(self.attn_out[...], self.w_out[...].reshape(1024, 2048))
        self.middle[...] = value
        self.total[...] = value
        self.outs[1][...] = (value * norm_scale(value) * self.gain[...]).astype(BF16)
        self.cot_total[...] = jnp.zeros_like(self.cot_total)

    def tile(self, t):
        mlp_in, gate_cot, up_cot, hidden = self.outs[1:5]
        for copy in self.tile_copies(t):
            copy.wait()
        w_gate, w_up, w_down = (self.tiles[t % 2, i].reshape(1024, FF_TILE) for i in range(3))
        gate = dot_nn(mlp_in[...], w_gate)
        up = dot_nn(mlp_in[...], w_up)
        sigmoid = jax.nn.sigmoid(gate)
        silu = gate * sigmoid
        hidden_tile = (silu * up).astype(BF16)
        hidden_cot = dot_nn(self.down_cot[...], w_down)
        gate_tile = (hidden_cot * up * sigmoid * (1.0 + gate * (1.0 - sigmoid))).astype(BF16)
        up_tile = (hidden_cot * silu).astype(BF16)
        columns = pl.ds(FF_TILE * t, FF_TILE)
        gate_cot[:, columns] = gate_tile
        up_cot[:, columns] = up_tile
        hidden[:, columns] = hidden_tile
        self.total[...] += dot_nt(hidden_tile, w_down)
        self.cot_total[...] += dot_nt(gate_tile, w_gate) + dot_nt(up_tile, w_up)

    def end(self):
        result, _, _, _, _, branch_cot, middle_cot, attended_cot, gain_part = self.outs
        result[...] = self.total[...].astype(BF16)
        value = self.middle[...]
        scale = norm_scale(value)
        normed = value * scale
        mlp_in_cot = self.cot_total[...]
        gain_part[...] = jnp.sum(mlp_in_cot * normed, axis=0, keepdims=True)
        scaled = mlp_in_cot * self.gain[...]
        cot = self.down_cot[...].astype(F32) + scale * (scaled - normed * mean_last(scaled * normed))
        middle_cot[...] = cot
        branch_cot[...] = cot.astype(BF16)
        attended_cot[...] = dot_nn(cot.astype(BF16), self.w_out[...].reshape(1024, 2048)).astype(BF16)


def head_columns(head):
    return (
        (pl.ds(pl.multiple_of(head * 256, 256), 256), pl.ds(0, 256)),
        (pl.ds(pl.multiple_of(head * 128, 128), 128), pl.ds(256, 128)),
        (pl.ds(pl.multiple_of(head * 128, 128), 128), pl.ds(384, 128)),
    )


def project_rows(s, low, xs, heads_w, inner, outer, query_gain, key_gain, raw, rows):
    product = dot_nn(xs[s], heads_w[...].reshape(1024, 512))
    cosine, sine = rope_rows(inner, outer, low)
    raw[s] = product[:, :384]
    for i, gain in enumerate((query_gain, query_gain, key_gain)):
        value = product[:, i * 128 : i * 128 + 128]
        value = value * norm_scale(value) * gain[...]
        value = value * cosine + pltpu.roll(value, 64, 1) * sine
        rows[s, :, i * 128 : i * 128 + 128] = value.astype(BF16)
    rows[s, :, 384:] = product[:, 384:].astype(BF16)


GATHER_AT = {
    "row 7": 2, "tile 00": 1, "tile 01": 1, "tile 11": 1, "tile 31": 1, "tile 21": 1,
    "feed 0": 1, "feed 2": 1, "feed 4": 1,
}


def forward_body(
    pair, x, attn_gain, query_gain, key_gain, inner, outer, down_cot, mlp_gain, *refs
):
    shards, refs = refs[:7], refs[7:]
    results, refs = refs[:15], refs[15:]
    full, refs = refs[:7], refs[7:]
    held, result_sem, refs = refs[:15], refs[15], refs[16:]
    attn_out, rows, raw, kv, mixed_t, log_total = held[:6]
    feed_outs = held[6:]
    stores = [
        pltpu.make_async_copy(source, target, result_sem.at[i])
        for i, (source, target) in enumerate(zip(held, results))
    ]
    feed_scratch, refs = refs[:6], refs[6:]
    (
        xs, heads_w, queries, stacked, query_pos, key_pos, total, mixed,
        x_send, x_recv, w_send, w_recv, w_load, kv_send, kv_recv, back_send, back_recv,
    ), scratch = refs[:17], refs[17:]
    me = here()
    head = group_head(me)
    twin, across = me.sibling(), me.across()
    across_twin = across.sibling()
    others = [me.move(b=ring(me.b, d)) for d in (1, 2, 3)]
    along = [me.move(a=ring(me.a, d)) for d in (1, 2, 3)]
    z_low = me.move(zl=1 - me.zl)
    greet([twin, across, across_twin] + group_neighbours(me))
    start, spread_own, turns, pass_tile, finish_tile, finish, gather_wire = gather_turns(
        me, shards, full, scratch
    )
    turns = list(turns)

    def step(place):
        for _ in range(GATHER_AT.get(place, 0)):
            turns.pop(0)()

    x_wire = Wire(x_send, x_recv, twin)
    w_wire = Wire(w_send, w_recv, twin)
    kv_wire = Wire(kv_send, kv_recv, twin)
    back_wire = Wire(back_send, back_recv, twin)
    mine = me.zh * 2 + me.core
    qkv_shards = shards[3:6]
    loads = []
    for i, (source, target) in enumerate(head_columns(head)):
        load = pltpu.make_async_copy(qkv_shards[i].at[:, source], heads_w.at[mine, :, target], w_load.at[i])
        load.start()
        loads.append(load)
    for t, spot in enumerate((across, across_twin, twin)):
        for i, (source, target) in enumerate(head_columns(group_head(spot))):
            w_wire.push((t, i), qkv_shards[i].at[:, source], heads_w.at[mine, :, target], spot)
    inputs = x[...].astype(F32)
    xs[head] = (inputs * norm_scale(inputs) * attn_gain[...]).astype(BF16)
    x_wire.push(3, xs.at[head], xs.at[head], z_low)
    for d in (1, 3, 2):
        x_wire.push(d - 1, xs.at[head], xs.at[head], along[d - 1])
    start()
    query_positions(pair, me, query_pos)
    mixed_t[...] = jnp.zeros_like(mixed_t)
    total[...] = jnp.zeros_like(total)
    low_head = me.a + 4 * (1 - me.zl)
    x_wire.take(3, xs.at[low_head])
    for d in (1, 3, 2):
        x_wire.push(3 + d, xs.at[low_head], xs.at[low_head], along[d - 1])
    spread_own()
    for load in loads:
        load.wait()
    for t, f in enumerate(
        ((1 - me.zh) * 2 + me.core, (1 - me.zh) * 2 + 1 - me.core, me.zh * 2 + 1 - me.core)
    ):
        for i, (_, target) in enumerate(head_columns(head)):
            w_wire.take((t, i), heads_w.at[f, :, target])
    arrivals = [(None, head), (None, low_head)]
    for zl, first in ((me.zl, 0), (1 - me.zl, 4)):
        for d in (1, 3, 2):
            arrivals.append((first + d - 1, ring(me.a, -d) + 4 * zl))
    for k, (slot, s) in enumerate(arrivals):
        if slot is not None:
            x_wire.take(slot, xs.at[s])
        project_rows(
            s, low_block(pair, me, me.b, s), xs, heads_w, inner, outer, query_gain, key_gain, raw, rows
        )
        for d in range(3):
            kv_wire.push((k, d), rows.at[s, :, pl.ds(256, 256)], kv.at[me.b, s], others[d])
        kv[me.b, s] = rows[s, :, 256:]
        step(f"row {k}")
    stack_heads(lambda s: rows[s, :, :256], queries)
    for d in (0, 1, 3, 2):
        j = ring(me.b, -d)
        if d:
            for k, (_, s) in enumerate(arrivals):
                kv_wire.take((k, d - 1), kv.at[j, s])
        for part in range(2):
            mix_tile(me, j, part, pair, kv, query_pos, queries, key_pos, mixed_t, total)
            step(f"tile {d}{part}")
    finish_mix(mixed, mixed_t, log_total, stacked, total)

    for i in range(1, 6):
        stores[i].start()

    def place(origin):
        return attn_out.at[:, pl.ds(pl.multiple_of(origin * 256, 256), 256)]

    for k in range(1, 8):
        peer = peer_of(head, k)
        back_wire.push(k - 1, mixed.at[peer], place(head), group_spot(me, peer))
    attn_out[:, pl.ds(pl.multiple_of(head * 256, 256), 256)] = mixed[head]
    step("back")
    feed = FeedForward(x, attn_out, down_cot, mlp_gain, feed_outs, full, feed_scratch)
    finish(0)
    feed.load_out()
    finish(1)
    finish(2)
    finish(6)
    pass_tile(0)
    pass_tile(1)
    finish_tile(0)
    feed.load_tile(0)
    for k in range(7):
        back_wire.take(k, place(peer_of(head, 7 - k)))
    stores[0].start()
    feed.begin()
    for t in range(FF_STEPS):
        if t + 2 < FF_STEPS:
            pass_tile(t + 2)
        if t + 1 < FF_STEPS:
            finish_tile(t + 1)
            feed.load_tile(t + 1)
        feed.tile(t)
        step(f"feed {t}")
    feed.end()
    for store in stores[6:]:
        store.start()
    step("end")
    assert not turns
    for m in (3, 4, 5):
        finish(m)
    for store in stores:
        store.wait()
    for wire in (x_wire, w_wire, kv_wire, back_wire, gather_wire):
        wire.close()


def attention_forward(pair, x, gains, tables, down_cot, mlp_gain, weights):
    narrow = jax.ShapeDtypeStruct((128, 1024), BF16)
    wide = jax.ShapeDtypeStruct((128, FF_STEPS * FF_TILE), BF16)
    results = [
        jax.ShapeDtypeStruct((128, 2048), BF16),
        jax.ShapeDtypeStruct((8, 128, 512), BF16),
        jax.ShapeDtypeStruct((8, 128, 384), F32),
        jax.ShapeDtypeStruct((4, 8, 128, 256), BF16),
        jax.ShapeDtypeStruct((128, 2048), F32),
        jax.ShapeDtypeStruct((8, 2048), F32),
        narrow, narrow, wide, wide, wide, narrow,
        jax.ShapeDtypeStruct((128, 1024), F32),
        jax.ShapeDtypeStruct((128, 2048), BF16),
        jax.ShapeDtypeStruct((1, 1024), F32),
    ]
    outs = pl.pallas_call(
        forward_body,
        out_shape=results
        + [jax.ShapeDtypeStruct((4,) + w.shape, w.dtype) for w in weights],
        in_specs=[SMEM] + [VMEM] * 8 + [HBM] * 7,
        out_specs=[HBM] * 22,
        scratch_shapes=[pltpu.VMEM(result.shape, result.dtype) for result in results]
        + [
            dma(len(results)),
            pltpu.VMEM((4, 256, 2048), BF16),
            pltpu.VMEM((2, 3, 4, 256, FF_TILE), BF16),
            pltpu.VMEM((128, 1024), F32),
            pltpu.VMEM((128, 1024), F32),
            pltpu.VMEM((128, 1024), F32),
            dma(7),
            pltpu.VMEM((8, 128, 1024), BF16),
            pltpu.VMEM((4, 256, 512), BF16),
            pltpu.VMEM((2048, 128), BF16),
            pltpu.VMEM((2048, 128), BF16),
            pltpu.VMEM((8, 2048), jnp.int32),
            pltpu.VMEM((TILE, CHUNK), jnp.int32),
            pltpu.VMEM((8, 2048), F32),
            pltpu.VMEM((8, 128, 256), BF16),
            dma(7), dma(7), dma(3, 3), dma(3, 3), dma(3), dma(8, 3), dma(8, 3), dma(7), dma(7),
        ]
        + gather_scratch(weights),
        compiler_params=comm_params(1),
        name="attention_forward",
    )(pair, x, *gains, *tables, down_cot, mlp_gain, *weights)
    return outs[:6], outs[6:15], [whole_rows(out) for out in outs[15:]]


def whole_rows(out):
    return out.reshape(4 * out.shape[1], out.shape[2])


PAIR_TILE = 512


def half_of(ref, half):
    width = ref.shape[-1] // 2
    return ref.at[:, :, pl.ds(half * width, width)]


def add_into(target, *sources):
    for zh in range(target.shape[0]):

        @pl.loop(0, target.shape[1] // 16)
        def _(r):
            at = pl.ds(pl.multiple_of(r * 16, 16), 16)
            total = target[zh, at, :].astype(F32)
            for source in sources:
                total = total + source[zh, at, :].astype(F32)
            target[zh, at, :] = total.astype(BF16)


class PairGrad:
    def __init__(self, me, left, right, left_scratch, twin_right, grad, wire, slot):
        self.me, self.left, self.right, self.wire, self.slot = me, left, right, wire, slot
        self.landing, self.left_t = left_scratch
        self.twin_right, self.grad = twin_right, grad

    def send(self):
        me = self.me
        twin = me.sibling()
        self.wire.push(self.slot + 2, self.right, self.twin_right, twin)
        for zh in range(0 if self.left is None else 2):
            columns = pl.ds(pl.multiple_of((zh * 2 + 1 - me.core) * 256, 256), 256)
            self.wire.push(self.slot + zh, self.left.at[:, columns], self.landing.at[zh], twin)

    def multiply(self):
        me = self.me
        for zh in range(0 if self.left is None else 2):
            columns = pl.ds(pl.multiple_of((zh * 2 + me.core) * 256, 256), 256)
            self.left_t[zh * 256 : zh * 256 + 256, 0:128] = self.left[:, columns].T
            self.wire.take(self.slot + zh, self.landing.at[zh])
            self.left_t[zh * 256 : zh * 256 + 256, 128:256] = self.landing[zh].T
        self.wire.take(self.slot + 2, self.twin_right)

        @pl.loop(0, self.twin_right.shape[1] // PAIR_TILE)
        def _(t):
            columns = pl.ds(pl.multiple_of(t * PAIR_TILE, PAIR_TILE), PAIR_TILE)
            right = jnp.concatenate([self.right[:, columns], self.twin_right[:, columns]], axis=0)
            product = dot_nn(self.left_t[...], right).astype(BF16)
            self.grad[:, :, columns] = product.reshape(2, 256, PAIR_TILE)


REDUCE_SLOTS = 13


def reduce_scratch(widths, z_first):
    scratch = []
    for k, width in enumerate(widths):
        half = width // 2
        if k in z_first:
            shapes = [
                (1, 128, half), (1, 128, half), (1, 256, half), (1, 256, half),
                (3, 1, 64, half), (1, 64, half), (3, 1, 16, half), (1, 16, half),
            ]
        else:
            shapes = [
                (2, 64, half), (2, 64, half), (2, 64, width), (2, 64, width),
                (3, 2, 16, width), (2, 16, width), (4, 16, width), (1, 16, width),
            ]
        scratch += [pltpu.VMEM(shape, BF16) for shape in shapes]
    count = len(widths)
    return scratch + [dma(count, REDUCE_SLOTS), dma(count, REDUCE_SLOTS)]


def reduce_stages(me, grads, pieces, scratch, z_first):
    wire = Wire(scratch[-2], scratch[-1], me.sibling())
    z = me.zh * 2 + me.zl
    z_low, across, z_high = me.move(zl=1 - me.zl), me.across(), me.move(zh=1 - me.zh)

    def z_spot(step):
        far = lax.rem(z + step + 4, 4)
        return me.move(zl=lax.rem(far, 2), zh=far // 2)

    def rows(ref, i, size):
        return ref.at[:, pl.ds(pl.multiple_of(i * size, size), size)]

    def ring_stages(k, slot, ahead, behind, block, bufs, half):
        far_a, far_b, in_a, in_b = bufs

        def send():
            wire.push((k, slot), half(block(2), 0), far_a, ahead)
            wire.push((k, slot + 1), half(block(2), 1), far_b, behind)
            wire.push((k, slot + 2), half(block(1), 1), half(in_a, 1), ahead)
            wire.push((k, slot + 3), half(block(-1), 0), half(in_b, 0), behind)

        def relay():
            wire.take((k, slot), far_a)
            add_into(far_a, half(block(1), 0))
            wire.push((k, slot + 4), far_a, half(in_a, 0), ahead)
            wire.take((k, slot + 1), far_b)
            add_into(far_b, half(block(-1), 1))
            wire.push((k, slot + 5), far_b, half(in_b, 1), behind)

        def collect():
            wire.take((k, slot + 2), half(in_a, 1))
            wire.take((k, slot + 3), half(in_b, 0))
            wire.take((k, slot + 4), half(in_a, 0))
            wire.take((k, slot + 5), half(in_b, 1))
            add_into(in_a, in_b, block(0))

        return send, relay, collect

    def direct_send(k, slot, axis, size, source, land):
        position = getattr(me, axis)
        for d in (1, 3, 2):
            spot = me.move(**{axis: ring(position, d)})
            wire.push((k, slot + d - 1), rows(source, ring(position, d), size), land.at[d - 1], spot)

    def direct_sum(k, slot, axis, size, source, land, target):
        for d in (1, 3, 2):
            wire.take((k, slot + d - 1), land.at[d - 1])
        own = rows(source, getattr(me, axis), size)
        for lead in range(target.shape[0]):

            @pl.loop(0, size // 16)
            def _(r):
                at = pl.ds(pl.multiple_of(r * 16, 16), 16)
                total = own[lead, at, :].astype(F32)
                for d in range(3):
                    total = total + land[d, lead, at, :].astype(F32)
                target[lead, at, :] = total.astype(BF16)

    def plain(k):
        grad, bufs = grads[k], scratch[8 * k : 8 * k + 8]
        in_a, a_land, total, z_land = bufs[2], bufs[4], bufs[5], bufs[6]
        send, relay, collect = ring_stages(
            k, 0, me.move(b=ring(me.b, 1)), me.move(b=ring(me.b, -1)),
            lambda step: rows(grad, ring(me.b, step), 64), bufs[:4], half_of,
        )

        def third():
            collect()
            direct_send(k, 6, "a", 16, in_a, a_land)

        def fourth():
            direct_sum(k, 6, "a", 16, in_a, a_land, total)
            wire.push((k, 9), total.at[1 - me.zh], z_land.at[z], across)
            wire.push((k, 10), total.at[1 - me.zh], z_land.at[z], z_high)
            wire.push((k, 11), total.at[me.zh], z_land.at[z], z_low)
            z_land[z] = total[me.zh]

        def fifth():
            for slot, spot in ((9, across), (10, z_high), (11, z_low)):
                wire.take((k, slot), z_land.at[spot.zh * 2 + spot.zl])
            total = z_land[0].astype(F32)
            for i in range(1, 4):
                total = total + z_land[i].astype(F32)
            pieces[k][0] = total.astype(BF16)

        return [send, relay, third, fourth, fifth]

    def first_z(k):
        grad, bufs = grads[k], scratch[8 * k : 8 * k + 8]
        in_a, b_land, b_sum, a_land, a_sum = bufs[2], bufs[4], bufs[5], bufs[6], bufs[7]
        width = grad.shape[2] // 2

        def columns(ref, zl):
            return ref.at[:, :, pl.ds(pl.multiple_of(zl * width, width), width)]

        def block(step):
            far = lax.rem(z + step + 4, 4)
            return columns(grad.at[pl.ds(far // 2, 1)], lax.rem(far, 2))

        send, relay, collect = ring_stages(
            k, 0, z_spot(1), z_spot(-1), block, bufs[:4],
            lambda view, i: view.at[:, pl.ds(128 * i, 128)],
        )

        def third():
            collect()
            direct_send(k, 6, "b", 64, in_a, b_land)

        def fourth():
            direct_sum(k, 6, "b", 64, in_a, b_land, b_sum)
            direct_send(k, 9, "a", 16, b_sum, a_land)

        def fifth():
            direct_sum(k, 9, "a", 16, b_sum, a_land, a_sum)
            place = columns(pieces[k], me.zl)
            place[...] = a_sum[...]
            wire.push((k, 12), a_sum, place, z_low)

        def sixth():
            wire.take((k, 12), columns(pieces[k], 1 - me.zl))

        return [send, relay, third, fourth, fifth, sixth]

    lists = [first_z(k) if k in z_first else plain(k) for k in range(len(grads))]
    return lists, wire


def replicate_stages(me, pieces, outs, send, recv, load_sem):
    wire = Wire(send, recv, me.sibling())
    loads = {}

    def cut(k, row, rows, half=None):
        width = outs[k].shape[1] // 2
        at = pl.ds(pl.multiple_of(row, 16), rows)
        if half is None:
            return outs[k].at[at]
        return outs[k].at[at, pl.ds(half * width, width)]

    b_next, b_prev = me.move(b=ring(me.b, 1)), me.move(b=ring(me.b, -1))

    def a_row(step):
        return (me.b * 4 + ring(me.a, step)) * 16

    def b_row(step):
        return ring(me.b, step) * 64

    def a_send(k):
        place = cut(k, a_row(0), 16)
        for d in (1, 3, 2):
            wire.push((k, d - 1), pieces[k].at[0], place, me.move(a=ring(me.a, d)))
        loads[k] = pltpu.make_async_copy(pieces[k].at[0], place, load_sem.at[k])
        loads[k].start()

    def b_send(k):
        for d in (1, 3, 2):
            wire.take((k, d - 1), cut(k, a_row(-d), 16))
        loads[k].wait()
        mine = cut(k, b_row(0), 64)
        wire.push((k, 4), mine, mine, b_next)
        wire.push((k, 5), mine, mine, b_prev)

    def b_relay(k):
        wire.take((k, 4), cut(k, b_row(-1), 64))
        wire.push((k, 6), cut(k, b_row(-1), 64, 0), cut(k, b_row(-1), 64, 0), b_next)
        wire.take((k, 5), cut(k, b_row(1), 64))
        wire.push((k, 7), cut(k, b_row(1), 64, 1), cut(k, b_row(1), 64, 1), b_prev)

    def b_collect(k):
        wire.take((k, 6), cut(k, b_row(2), 64, 0))
        wire.take((k, 7), cut(k, b_row(2), 64, 1))

    stages = (a_send, b_send, b_relay, b_collect)
    lists = [[functools.partial(stage, k) for stage in stages] for k in range(len(pieces))]
    return lists, wire


class Plan:
    def __init__(self, **lists):
        self.lists = {name: list(stages) for name, stages in lists.items()}

    def run(self, names):
        for name in names:
            self.lists[name].pop(0)()

    def check(self):
        assert not any(self.lists.values())


def gain_turns(me, gains, gains_out, gain_slots, gain_send, gain_recv):
    first = me.core == 0
    x, y = jnp.where(first, me.a, me.b), jnp.where(first, me.b, me.a)
    z = me.zh * 2 + me.zl
    wire = Wire(gain_send, gain_recv, me.sibling())

    def pick(d, on_x):
        use_a = first if on_x else jnp.logical_not(first)
        return me.move(
            a=jnp.where(use_a, ring(me.a, d), me.a), b=jnp.where(use_a, me.b, ring(me.b, d))
        )

    def z_spot(d):
        far = lax.rem(z + d, 4)
        return me.move(zl=lax.rem(far, 2), zh=far // 2)

    def push(stage, position, spots):
        for d, spot in enumerate(spots):
            slot = gain_slots.at[stage, position]
            wire.push((stage, d), slot, slot, spot)

    def take(stage, position, size):
        for d in range(size - 1):
            wire.take((stage, d), gain_slots.at[stage, lax.rem(position + size - 1 - d, size)])

    def total(stage):
        return (gain_slots[stage, 0] + gain_slots[stage, 1]) + (gain_slots[stage, 2] + gain_slots[stage, 3])

    def turn0():
        gain_slots[0, me.core] = gains[...]
        push(0, me.core, [me.sibling()])

    def turn1():
        take(0, me.core, 2)
        gain_slots[1, x] = gain_slots[0, 0] + gain_slots[0, 1]
        push(1, x, [pick(d, True) for d in (1, 2, 3)])

    def turn2():
        take(1, x, 4)
        gain_slots[2, y] = total(1)
        push(2, y, [pick(d, False) for d in (1, 2, 3)])

    def turn3():
        take(2, y, 4)
        gain_slots[3, z] = total(2)
        push(3, z, [z_spot(d) for d in (1, 2, 3)])

    def turn4():
        take(3, z, 4)
        gains_out[...] = total(3)

    return [turn0, turn1, turn2, turn3, turn4], wire.close


def unrope(s, low, grads, raw, inner, outer, gain, column, gain_part):
    cosine, sine = rope_rows(inner, outer, low)
    value = raw[s, :, column : column + 128]
    scale = norm_scale(value)
    hat = value * scale
    hat_cot = grads * cosine - pltpu.roll(grads, 64, 1) * sine
    gain_part[...] += jnp.sum((hat_cot * hat).reshape(16, 8, 128), axis=0)
    scaled = hat_cot * gain[...]
    return (scale * (scaled - hat * mean_last(scaled * hat))).astype(BF16)


WIDTHS = (3072, 3072, 3072, 2048, 2048, 2048)
Z_FIRST = (2, 3, 4)
BETWEEN = {
    "cots": "ddgguoou",
    "tiles": "dg",
    "own tile": "",
    "rows 2": "",
    "rows 4": "",
    "rows 6": "",
    "rows 0": "guodug",
    "proj": "qdkkoukdquugoddkqugok",
    "weights": "d",
    "input": "qkkousdsqgoksqqqdsogqkgoqsuoqk",
}


def backward_body(*refs):
    (
        pair, attn_gain, query_gain, key_gain, inner, outer, mlp_gain_part, wq, wk, wv,
    ), sources, refs = refs[:10], refs[10:25], refs[25:]
    (input_cot, gains_out), outs, refs = refs[:2], refs[2:8], refs[8:]
    (
        cots_in, dkv, queries, cots, deltas, query_pos, key_pos, probs_all, score_cots, acc, held, stacked, message,
        attn_in, proj, head_gains, gains, gain_slots,
        cot_send, cot_recv, p_send, p_recv, m_send, m_recv, w_send, w_recv, out_send, out_recv, out_load, w_load,
        gain_send, gain_recv,
    ), refs = refs[:32], refs[32:]
    held_inputs, input_sem, refs = refs[:15], refs[15], refs[16:]
    inputs_in = [
        pltpu.make_async_copy(source, target, input_sem.at[i])
        for i, (source, target) in enumerate(zip(sources, held_inputs))
    ]
    for load in inputs_in:
        load.start()
    (
        parts, down_cot, hidden, mlp_in, gate_cot, up_cot, branch_cot, attn_out, x,
        rows, mixed_t, log_total, kv, raw, middle_cot,
    ) = held_inputs
    pieces, grads, refs = refs[:6], list(refs[6:11]), refs[11:]
    grads.append(grads[2].at[:, :, pl.ds(0, WIDTHS[5])])
    me = here()
    head = group_head(me)
    twin = me.sibling()
    others = [me.move(b=ring(me.b, d)) for d in (1, 2, 3)]
    greet([twin, me.across(), me.move(zh=1 - me.zh)] + group_neighbours(me))
    cot_wire = Wire(cot_send, cot_recv, twin)
    p_wire = Wire(p_send, p_recv, twin)
    m_wire = Wire(m_send, m_recv, twin)
    w_wire = Wire(w_send, w_recv, twin)

    def of_head(ref, h):
        return ref.at[:, pl.ds(pl.multiple_of(h * 256, 256), 256)]

    for load in inputs_in[:9]:
        load.wait()
    for k in range(1, 8):
        peer = peer_of(head, k)
        cot_wire.push(k - 1, of_head(parts, peer), cots_in.at[head], group_spot(me, peer))
    lefts = (mlp_in, None, down_cot, branch_cot, attn_in, None)
    rights = (
        gate_cot, up_cot, hidden, attn_out, proj.at[:, pl.ds(0, 2048)], proj.at[:, pl.ds(2048, 2048)]
    )
    held_lefts, twin_rights, refs = refs[:8], refs[8:14], refs[14:]
    pairs = []
    for i, share in enumerate((0, 0, 1, 2, 3, 3)):
        pairs.append(
            PairGrad(
                me, lefts[i], rights[i], held_lefts[2 * share : 2 * share + 2], twin_rights[i], grads[i], w_wire, 3 * i
            )
        )
    sums, sum_wire = reduce_stages(me, grads, pieces, refs, Z_FIRST)
    copies, out_wire = replicate_stages(me, pieces, outs, out_send, out_recv, out_load)
    small, gain_finish = gain_turns(me, gains, gains_out, gain_slots, gain_send, gain_recv)
    plan = Plan(s=small, **{
        name: [pairs[i].multiply] + sums[i] + copies[i] for i, name in enumerate("gudoqk")
    })
    for i in (2, 0, 1, 3):
        pairs[i].send()
    query_positions(pair, me, query_pos)
    cots_in[head] = parts[:, pl.ds(pl.multiple_of(head * 256, 256), 256)]
    head_gains[...] = jnp.zeros_like(head_gains)
    inputs = x[...].astype(F32)
    scale = norm_scale(inputs)
    normed = inputs * scale
    attn_in[...] = (normed * attn_gain[...]).astype(BF16)
    plan.run(BETWEEN["cots"])
    for k in range(7):
        cot_wire.take(k, cots_in.at[peer_of(head, 7 - k)])
    for load in inputs_in[9:]:
        load.wait()
    start_grad(rows, mixed_t, cots_in, queries, cots, deltas, acc)
    for d in (2, 1, 3, 0):
        j = ring(me.b, d)
        if d == 0:
            plan.run(BETWEEN["tiles"])
        for part in range(2):
            grad_tile(
                me, j, part, pair, kv, query_pos, queries, cots, deltas, log_total, key_pos,
                probs_all, score_cots, acc, dkv,
            )
        if d:
            for k in range(8):
                peer = peer_of(head, k)
                p_wire.push((k, d - 1), dkv.at[j, peer], held.at[d - 1, peer], others[d - 1])
    for chunk in range(8):
        columns = pl.ds(chunk * CHUNK, CHUNK)
        stacked[columns, :] = (acc[:, columns] * SCORE_SCALE).T
    plan.run(BETWEEN["own tile"])

    def places(h):
        return (
            (pl.ds(0, 256), pl.ds(pl.multiple_of(h * 256, 256), 256)),
            (pl.ds(256, 128), pl.ds(pl.multiple_of(2048 + h * 128, 128), 128)),
            (pl.ds(384, 128), pl.ds(pl.multiple_of(3072 + h * 128, 128), 128)),
        )

    for k in (1, 2, 3, 4, 5, 6, 7, 0):
        s = peer_of(head, k)
        low = low_block(pair, me, me.b, s)
        for d in range(3):
            p_wire.take((k, d), held.at[d, s])
        for h in range(2):
            turned = jnp.concatenate(
                [
                    stacked[pl.ds(pl.multiple_of(part * 1024 + s * 128 + h * 64, 64), 64), :]
                    for part in range(2)
                ],
                axis=0,
            )
            message[s, :, h * 128 : h * 128 + 128] = unrope(
                s, low, turned, raw, inner, outer, query_gain, h * 128, head_gains.at[0]
            )
        total = (
            dkv[me.b, s].astype(F32)
            + held[0, s].astype(F32)
            + held[1, s].astype(F32)
            + held[2, s].astype(F32)
        )
        message[s, :, 256:384] = unrope(
            s, low, total[:, :128], raw, inner, outer, key_gain, 256, head_gains.at[1]
        )
        message[s, :, 384:] = total[:, 128:].astype(BF16)
        if k:
            for i, (source, target) in enumerate(places(head)):
                m_wire.push((k - 1, i), message.at[s, :, source], proj.at[:, target], group_spot(me, s))
        if k % 2 == 0:
            plan.run(BETWEEN[f"rows {k}"])
    for source, target in places(head):
        proj[:, target] = message[head, :, source]
    for k in range(7):
        for i, (_, target) in enumerate(places(peer_of(head, 7 - k))):
            m_wire.take((k, i), proj.at[:, target])
    for i in (4, 5):
        pairs[i].send()
    for k in range(3):
        sum_wire.settle(k)
    plan.run(BETWEEN["proj"])

    loads = []
    value_rows = (score_cots, probs_all)
    for i in range(4):
        at = pl.ds(256 * i, 256)
        target = grads[i // 2].at[i % 2]
        loads.append((wq.at[at], target.at[:, pl.ds(0, 2048)]))
        loads.append((wk.at[at], target.at[:, pl.ds(2048, 1024)]))
        loads.append((wv.at[at], value_rows[i // 2].at[pl.ds(i % 2 * 256, 256)]))
    loads = [pltpu.make_async_copy(*pair_, w_load.at[i]) for i, pair_ in enumerate(loads)]
    for load in loads:
        load.start()
    plan.run(BETWEEN["weights"])
    for load in loads:
        load.wait()
    attn_in_cot = jnp.concatenate(
        [
            dot_nt(proj[:, :3072], grads[i // 2][i % 2])
            + dot_nt(proj[:, 3072:], value_rows[i // 2][i % 2 * 256 : i % 2 * 256 + 256, :])
            for i in range(4)
        ],
        axis=1,
    )
    scaled = attn_in_cot * attn_gain[...]
    input_cot[...] = middle_cot[...] + scale * (scaled - normed * mean_last(scaled * normed))
    gains[...] = jnp.zeros_like(gains)
    gains[0:1, :] = jnp.sum(attn_in_cot * normed, axis=0, keepdims=True)
    gains[1:2, :] = mlp_gain_part[...]
    for i in range(2):
        gains[2 + i : 3 + i, 0:128] = jnp.sum(head_gains[i], axis=0, keepdims=True)
    plan.run(BETWEEN["input"])
    plan.check()
    gain_finish()
    for wire in (cot_wire, p_wire, m_wire, w_wire, sum_wire, out_wire):
        wire.close()


def attention_backward(pair, x, gains, tables, kept, attended_cot, lefts, rights, middle_cot, mlp_gain_part, weights):
    heads = (8, 128, 256)
    count = len(WIDTHS)
    attn_out = rights[3]
    attended, raw, kv, mixed_t, log_total = kept
    held = (
        attended_cot, lefts[1], rights[2], lefts[0], rights[0], rights[1], lefts[2], attn_out, x,
        attended, mixed_t, log_total, kv, raw, middle_cot,
    )
    outs = pl.pallas_call(
        backward_body,
        out_shape=[jax.ShapeDtypeStruct((128, 1024), F32), jax.ShapeDtypeStruct((4, 1024), F32)]
        + [jax.ShapeDtypeStruct((256, width), BF16) for width in WIDTHS],
        in_specs=[SMEM] + [VMEM] * 6 + [HBM] * 18,
        out_specs=[VMEM] * 2 + [HBM] * count,
        scratch_shapes=[
            pltpu.VMEM(heads, BF16),
            pltpu.VMEM((4,) + heads, BF16),
            pltpu.VMEM((2048, 128), BF16),
            pltpu.VMEM((2048, 128), BF16),
            pltpu.VMEM((8, 2048), F32),
            pltpu.VMEM((8, 2048), jnp.int32),
            pltpu.VMEM((TILE, CHUNK), jnp.int32),
            pltpu.VMEM((TILE, 1024), BF16),
            pltpu.VMEM((TILE, 1024), BF16),
            pltpu.VMEM((128, 2048), F32),
            pltpu.VMEM((3,) + heads, BF16),
            pltpu.VMEM((2048, 128), F32),
            pltpu.VMEM((8, 128, 512), BF16),
            pltpu.VMEM((128, 1024), BF16),
            pltpu.VMEM((128, 4096), BF16),
            pltpu.VMEM((2, 8, 128), F32),
            pltpu.VMEM((4, 1024), F32),
            pltpu.VMEM((4, 4, 4, 1024), F32),
            dma(7), dma(7), dma(8, 3), dma(8, 3), dma(7, 3), dma(7, 3), dma(18), dma(18),
            dma(count, 8), dma(count, 8), dma(count), dma(12), dma(4, 3), dma(4, 3),
        ]
        + [pltpu.VMEM(value.shape, value.dtype) for value in held]
        + [dma(len(held))]
        + [pltpu.VMEM((1, 16, width), BF16) for width in WIDTHS]
        + [pltpu.VMEM((2, 256, width), BF16) for width in WIDTHS[:5]]
        + [pltpu.VMEM((2, 128, 256), BF16), pltpu.VMEM((512, 256), BF16)] * 4
        + [pltpu.VMEM((128, width), BF16) for width in WIDTHS]
        + reduce_scratch(WIDTHS, Z_FIRST),
        compiler_params=comm_params(2, 62 * 1024 * 1024),
        name="attention_backward",
    )(pair, *gains, *tables, mlp_gain_part, *weights, *held)
    return outs[0], outs[1], outs[2:]


WIDEN_STEPS = 8


def widen_body(
    result, input_cot, gate, up, down, out, query, key_value, gains,
    result_out, input_out, query_out, key_out, value_out, out_out, gate_out, up_out, down_out, g0, g1, g2, g3,
):
    result_out[0] = result[...]
    input_out[0] = input_cot[...]
    for source, target in ((query, query_out), (out, out_out), (gate, gate_out), (up, up_out), (down, down_out)):
        target[...] = source[...].astype(F32)
    key_out[...] = key_value[:, :1024].astype(F32)
    value_out[...] = key_value[:, 1024:].astype(F32)
    for i, target in enumerate((g0, g1, g2, g3)):
        target[...] = gains[i : i + 1, : target.shape[1]]


def widen_results(result, input_cot, grads, gains):
    def rows(array_shape):
        block = (array_shape[0] // WIDEN_STEPS,) + array_shape[1:]
        return pl.BlockSpec(block, lambda t: (t, 0))

    def split(array_shape):
        block = (1, array_shape[1] // WIDEN_STEPS, array_shape[2])
        return pl.BlockSpec(block, lambda t: (0, t, 0))

    def whole(array_shape):
        return pl.BlockSpec(array_shape, lambda t: (0, 0))

    tokens = (1, 128, 1024)
    widths = (2048, 1024, 1024, 2048, 3072, 3072, 3072)
    lengths = (1024, 1024, 128, 128)
    outs = pl.pallas_call(
        widen_body,
        grid=(WIDEN_STEPS,),
        out_shape=[jax.ShapeDtypeStruct(tokens, BF16), jax.ShapeDtypeStruct(tokens, F32)]
        + [jax.ShapeDtypeStruct((256, width), F32) for width in widths]
        + [jax.ShapeDtypeStruct((1, length), F32) for length in lengths],
        in_specs=[rows((128, 1024)), rows((128, 1024))]
        + [rows(grad.shape) for grad in grads]
        + [whole(gains.shape)],
        out_specs=[split(tokens), split(tokens)]
        + [rows((256, width)) for width in widths]
        + [whole((1, length)) for length in lengths],
        compiler_params=pltpu.CompilerParams(vmem_limit_bytes=VMEM_LIMIT),
        name="widen_results",
    )(result, input_cot, *grads, gains)
    return tuple(outs[:9]) + tuple(out[0] for out in outs[9:])


def shards(
    tokens,
    query_weight,
    key_weight,
    value_weight,
    out_weight,
    gate_weight,
    up_weight,
    down_weight,
    attn_gain,
    mlp_gain,
    query_gain,
    key_gain,
    pair_order,
    out_grad,
):
    tables = rope_tables()
    attn_row, query_row, key_row = attn_gain[None], query_gain[None], key_gain[None]
    down_cot = out_grad[0]
    (attn_out, *kept), feed, full = attention_forward(
        pair_order,
        tokens[0],
        (attn_row, query_row, key_row),
        tables,
        down_cot,
        mlp_gain[None],
        [out_weight, gate_weight, up_weight, query_weight, key_weight, value_weight, down_weight],
    )
    result, mlp_in, gate_cot, up_cot, hidden, branch_cot, middle_cot, attended_cot, mlp_gain_part = feed
    full_qkv = full[3:6]
    input_cot, gains, grads = attention_backward(
        pair_order,
        tokens[0],
        (attn_row, query_row, key_row),
        tables,
        kept,
        attended_cot,
        (mlp_in, down_cot, branch_cot),
        (gate_cot, up_cot, hidden, attn_out),
        middle_cot,
        mlp_gain_part,
        full_qkv,
    )
    return widen_results(result, input_cot, grads, gains)


def solution(mesh):
    rows, split, whole = P("fsdp", None), P("fsdp", "ctx", None), P()
    return jax.shard_map(
        shards,
        mesh=mesh,
        in_specs=(split,) + (rows,) * 7 + (whole,) * 4 + (rows, split),
        out_specs=(split, split) + (rows,) * 7 + (whole,) * 4,
        check_vma=False,
    )
```

```python
import functools

import jax
import jax.numpy as jnp
import numpy as np
from jax import lax
from jax.experimental import pallas as pl
from jax.experimental.pallas import tpu as pltpu
from jax.sharding import PartitionSpec as P

EPSILON = 1e-06
ROPE_BASE = 1000000.0
MESH = pl.DeviceIdType.MESH
HBM = pl.BlockSpec(memory_space=pltpu.HBM)
VMEM = pl.BlockSpec(memory_space=pltpu.VMEM)
SMEM = pl.BlockSpec(memory_space=pltpu.SMEM)
LOG2E = 1.4426950408889634
VMEM_LIMIT = 56 * 1024 * 1024
BF16 = jnp.bfloat16
F32 = jnp.float32


class Spot:
    def __init__(self, a, b, zl, zh, core):
        self.a, self.b, self.zl, self.zh, self.core = a, b, zl, zh, core

    def move(self, a=None, b=None, zl=None, zh=None):
        return Spot(
            self.a if a is None else a,
            self.b if b is None else b,
            self.zl if zl is None else zl,
            self.zh if zh is None else zh,
            self.core,
        )

    def id(self):
        first = self.core == 0
        x = jnp.where(first, self.a, self.b)
        y = jnp.where(first, self.b, self.a)
        return (self.zl * 16 + y * 4 + x, self.zh * 2 + self.core)

    def sibling(self):
        return Spot(self.b, self.a, self.zl, self.zh, 1 - self.core)

    def across(self):
        return self.move(zl=1 - self.zl, zh=1 - self.zh)


def here():
    ctx = lax.axis_index("ctx")
    fsdp = lax.axis_index("fsdp")
    x = lax.rem(ctx, 4)
    y = lax.rem(ctx // 4, 4)
    core = lax.rem(fsdp, 2)
    first = core == 0
    return Spot(jnp.where(first, x, y), jnp.where(first, y, x), ctx // 16, fsdp // 2, core)


def ring(position, step):
    return lax.rem(position + step + 4, 4)


def greet(spots):
    barrier = pltpu.get_barrier_semaphore()
    for spot in spots:
        pl.semaphore_signal(barrier, inc=1, device_id=spot.id(), device_id_type=MESH)
    pl.semaphore_wait(barrier, len(spots))


def remote(src, dst, send_sem, recv_sem, spot):
    return pltpu.make_async_remote_copy(
        src_ref=src,
        dst_ref=dst,
        send_sem=send_sem,
        recv_sem=recv_sem,
        device_id=spot.id(),
        device_id_type=MESH,
    )


def comm_params(collective_id, limit=VMEM_LIMIT):
    return pltpu.CompilerParams(
        collective_id=collective_id, has_side_effects=True, vmem_limit_bytes=limit
    )


class Wire:
    def __init__(self, send, recv, spot):
        self.send, self.recv, self.spot, self.sent = send, recv, spot, []

    def push(self, slot, src, dst, spot):
        copy = remote(src, dst, self.send.at[slot], self.recv.at[slot], spot)
        copy.start()
        self.sent.append((slot, copy))

    def take(self, slot, dst):
        remote(dst, dst, self.send.at[slot], self.recv.at[slot], self.spot).wait_recv()

    def settle(self, k):
        for slot, copy in self.sent:
            if slot[0] == k:
                copy.wait_send()
        self.sent = [(slot, copy) for slot, copy in self.sent if slot[0] != k]

    def close(self):
        for _, copy in self.sent:
            copy.wait_send()


def pipeline(stages, count):
    def turn(t):
        for depth, stage in enumerate(stages):
            if 0 <= t - depth < count:
                stage(t - depth)

    return [functools.partial(turn, t) for t in range(count + len(stages) - 1)]


GATHER_SLOTS = 14
FF_TILE = 512
FF_STEPS = 6


def gather_scratch(weights):
    count = len(weights)
    return [pltpu.VMEM(w.shape, w.dtype) for w in weights] + [
        pltpu.SemaphoreType.DMA((count, GATHER_SLOTS)),
        pltpu.SemaphoreType.DMA((count, GATHER_SLOTS)),
        pltpu.SemaphoreType.DMA((2, count)),
    ]


def gather_turns(me, ins, outs, scratch):
    count = len(ins)
    held, (send, recv, local_sem) = scratch[:count], scratch[count:]
    mine = me.zh * 2 + me.core
    other = (1 - me.zh) * 2 + me.core
    twin_mine = me.zh * 2 + 1 - me.core
    twin_other = (1 - me.zh) * 2 + 1 - me.core
    twin, across = me.sibling(), me.across()
    a_next, a_prev = me.move(a=ring(me.a, 1)), me.move(a=ring(me.a, -1))
    b_next, b_prev = me.move(b=ring(me.b, 1)), me.move(b=ring(me.b, -1))
    wire = Wire(send, recv, twin)

    def cut(m, rows, half):
        width = ins[m].shape[1] // 2
        if half is None:
            return outs[m].at[other, rows]
        return outs[m].at[other, rows, pl.ds(half * width, width)]

    def piece(m, a, half=None):
        return cut(m, pl.ds(pl.multiple_of((me.b * 4 + a) * 16, 16), 16), half)

    def block(m, b, half=None):
        return cut(m, pl.ds(pl.multiple_of(b * 64, 64), 64), half)

    def push(m, slot, src, dst, spot):
        wire.push((m, slot), src, dst, spot)

    def take(m, slot, dst):
        wire.take((m, slot), dst)

    loads = [pltpu.make_async_copy(ins[m], held[m], local_sem.at[0, m]) for m in range(count)]
    stores = [pltpu.make_async_copy(held[m], outs[m].at[mine], local_sem.at[1, m]) for m in range(count)]

    last = count - 1

    def start():
        for m in range(last):
            rows = pl.ds(pl.multiple_of((me.b * 4 + me.a) * 16, 16), 16)
            push(m, 0, ins[m].at[rows], outs[m].at[mine, rows], across)
        for t in range(FF_STEPS):
            columns = pl.ds(FF_TILE * t, FF_TILE)
            push(last, t, ins[last].at[:, columns], outs[last].at[mine, :, columns], across)
        for load in loads:
            load.start()

    def spread_own():
        for m in range(count):
            loads[m].wait()
            stores[m].start()
            push(m, 2 * FF_STEPS if m == last else 9, ins[m], outs[m].at[mine], twin)

    def stage_z(m):
        take(m, 0, piece(m, me.a))
        push(m, 1, piece(m, me.a), piece(m, me.a), a_next)
        push(m, 2, piece(m, me.a), piece(m, me.a), a_prev)

    def stage_a(m):
        left, right = ring(me.a, -1), ring(me.a, 1)
        take(m, 1, piece(m, left))
        push(m, 3, piece(m, left, 0), piece(m, left, 0), a_next)
        take(m, 2, piece(m, right))
        push(m, 4, piece(m, right, 1), piece(m, right, 1), a_prev)

    def stage_b(m):
        far = ring(me.a, 2)
        take(m, 3, piece(m, far, 0))
        take(m, 4, piece(m, far, 1))
        push(m, 5, block(m, me.b), block(m, me.b), b_next)
        push(m, 6, block(m, me.b), block(m, me.b), b_prev)
        push(m, 10, block(m, me.b), block(m, me.b), twin)

    def stage_c(m):
        left, right = ring(me.b, -1), ring(me.b, 1)
        take(m, 5, block(m, left))
        push(m, 7, block(m, left, 0), block(m, left, 0), b_next)
        push(m, 11, block(m, left), block(m, left), twin)
        take(m, 6, block(m, right))
        push(m, 8, block(m, right, 1), block(m, right, 1), b_prev)
        push(m, 12, block(m, right), block(m, right), twin)

    def stage_d(m):
        far = ring(me.b, 2)
        take(m, 7, block(m, far, 0))
        take(m, 8, block(m, far, 1))
        push(m, 13, block(m, far), block(m, far), twin)

    def pass_tile(t):
        tile = outs[last].at[other, :, pl.ds(FF_TILE * t, FF_TILE)]
        take(last, t, tile)
        push(last, FF_STEPS + t, tile, tile, twin)

    def finish_tile(t):
        take(last, FF_STEPS + t, outs[last].at[twin_other, :, pl.ds(FF_TILE * t, FF_TILE)])

    def finish(m):
        take(m, 2 * FF_STEPS if m == last else 9, outs[m].at[twin_mine])
        stores[m].wait()
        if m < last:
            for slot, step in ((10, 0), (11, -1), (12, 1), (13, 2)):
                rows = pl.ds(pl.multiple_of(ring(me.a, step) * 64, 64), 64)
                take(m, slot, outs[m].at[twin_other, rows])

    turns = pipeline((stage_z, stage_a, stage_b, stage_c, stage_d), last)
    return start, spread_own, turns, pass_tile, finish_tile, finish, wire


def group_spot(me, head):
    return me.move(a=lax.rem(head, 4), zl=head // 4)


def group_head(me):
    return me.a + 4 * me.zl


def peer_of(head, k):
    return lax.rem(head + k, 8)


def group_neighbours(me):
    head = group_head(me)
    return [group_spot(me, peer_of(head, k)) for k in range(1, 8)] + [
        me.move(b=ring(me.b, d)) for d in (1, 2, 3)
    ]


def dma(*shape):
    return pltpu.SemaphoreType.DMA(shape)


TILE = 512
CHUNK = 256
SCORE_SCALE = 128.0**-0.5


def dot_nt(left, right):
    return lax.dot_general(left, right, (((1,), (1,)), ((), ())), preferred_element_type=F32)


def dot_nn(left, right):
    return lax.dot_general(left, right, (((1,), (0,)), ((), ())), preferred_element_type=F32)


def stack_heads(read, target):
    for s in range(8):
        rows = read(s)
        for part in range(2):
            for head in range(2):
                at = part * 1024 + s * 128 + head * 64
                target[at : at + 64, :] = rows[part * 64 : part * 64 + 64, head * 128 : head * 128 + 128]


def unstack_heads(stacked, s, out):
    for part in range(2):
        for head in range(2):
            at = part * 1024 + s * 128 + head * 64
            out[s, part * 64 : part * 64 + 64, head * 128 : head * 128 + 128] = stacked[at : at + 64, :]


def low_block(pair, me, j, s):
    a = lax.rem(s, 4)
    first = me.core == 0
    return pair[0, (s // 4) * 16 + jnp.where(first, j * 4 + a, a * 4 + j)]


def key_positions(pair, me, j, part, target):
    line = lax.broadcasted_iota(jnp.int32, (64, CHUNK), 0)
    for s in range(8):
        low = low_block(pair, me, j, s)
        block = low if part == 0 else 63 - low
        target[s * 64 : s * 64 + 64, :] = line + block * 64


def query_positions(pair, me, target):
    line = lax.rem(lax.broadcasted_iota(jnp.int32, (8, 128), 1), 64)
    for s in range(8):
        low = low_block(pair, me, me.b, s)
        target[:, s * 128 : s * 128 + 128] = line + low * 64
        target[:, 1024 + s * 128 : 1152 + s * 128] = line + (63 - low) * 64


def rope_tables():
    frequency = ROPE_BASE ** (-np.arange(0, 128, 2, dtype=np.float64) / 128)
    frequency = np.concatenate([frequency, frequency])
    sign = np.where(np.arange(128) < 64, -1.0, 1.0)
    inner = np.arange(64, dtype=np.float64)[:, None] * frequency
    outer = inner * 64.0
    make = lambda angles: jnp.asarray(np.stack([np.cos(angles), np.sin(angles) * sign]), F32)
    return make(inner), make(outer)


def rope_rows(inner, outer, low):
    cosines, sines = [], []
    for block in (low, 63 - low):
        cos_b, sin_b = outer[0, pl.ds(block, 1), :], outer[1, pl.ds(block, 1), :]
        cosines.append(cos_b * inner[0] - sin_b * inner[1])
        sines.append(sin_b * inner[0] + cos_b * inner[1])
    return jnp.concatenate(cosines, axis=0), jnp.concatenate(sines, axis=0)


def mean_last(value):
    return jnp.mean(value, axis=-1, keepdims=True)


def norm_scale(value):
    return lax.rsqrt(mean_last(value * value) + EPSILON)


def tile_rows(kv, j, part, start):
    return kv[j, :, part * 64 : part * 64 + 64, start : start + 128].reshape(TILE, 128)


def tile_probs(scores, masked, key_pos, query_pos, columns, shift=None):
    logits = scores * (LOG2E * SCORE_SCALE)
    if shift is not None:
        logits = logits - shift
    probs = jnp.exp2(logits)
    if masked:
        probs = jnp.where(key_pos[...] <= query_pos[0:1, columns], probs, 0.0)
    return probs


def mix_tile(me, j, part, pair, kv, query_pos, queries, key_pos, acc, total):
    key_positions(pair, me, j, part, key_pos)
    keys = tile_rows(kv, j, part, 0)
    values_t = tile_rows(kv, j, part, 128).T
    for chunk in range(4 * part, 8):
        columns = pl.ds(chunk * CHUNK, CHUNK)
        masked = part == 1 or chunk < 4
        probs = tile_probs(dot_nt(keys, queries[columns, :]), masked, key_pos, query_pos, columns)
        total[:, columns] += jnp.sum(probs.reshape(TILE // 8, 8, CHUNK), axis=0)
        acc[:, columns] += dot_nn(values_t, probs.astype(BF16))


def finish_mix(out, mixed_t, log_total, stacked, total):
    for chunk in range(8):
        columns = pl.ds(chunk * CHUNK, CHUNK)
        full = jnp.sum(total[:, columns], axis=0, keepdims=True)
        log_total[:, columns] = jnp.broadcast_to(jnp.log2(full), (8, CHUNK))
        mixed = mixed_t[:, columns] / full
        mixed_t[:, columns] = mixed
        stacked[columns, :] = mixed.T.astype(BF16)
    for s in range(8):
        unstack_heads(stacked, s, out)


def grad_tile(
    me, j, part, pair, kv, query_pos, queries, cots, deltas, log_total, key_pos, probs_all, score_cots, acc, dkv
):
    key_positions(pair, me, j, part, key_pos)
    keys = tile_rows(kv, j, part, 0)
    values = tile_rows(kv, j, part, 128)
    keys_t = keys.T
    key_cot, value_cot = 0.0, 0.0
    for first in range(part, 2):
        for chunk in range(4 * first, 4 * first + 4):
            columns = pl.ds(chunk * CHUNK, CHUNK)
            local = pl.ds((chunk - 4 * first) * CHUNK, CHUNK)
            masked = part == first
            scores = dot_nt(keys, queries[columns, :])
            prob_cot = dot_nt(values, cots[columns, :])
            probs = tile_probs(scores, masked, key_pos, query_pos, columns, log_total[0:1, columns])
            score_cot = (probs * (prob_cot - deltas[0:1, columns])).astype(BF16)
            probs_all[:, local] = probs.astype(BF16)
            score_cots[:, local] = score_cot
            acc[:, columns] += dot_nn(keys_t, score_cot)
        rows = pl.ds(1024 * first, 1024)
        key_cot = key_cot + dot_nn(score_cots[...], queries[rows, :])
        value_cot = value_cot + dot_nn(probs_all[...], cots[rows, :])
    key_cot = key_cot * SCORE_SCALE
    at = part * 64
    dkv[j, :, at : at + 64, 0:128] = key_cot.astype(BF16).reshape(8, 64, 128)
    dkv[j, :, at : at + 64, 128:256] = value_cot.astype(BF16).reshape(8, 64, 128)


def start_grad(rows, mixed_t, cots_in, queries, cots, deltas, acc):
    stack_heads(lambda s: rows[s, :, :256], queries)
    stack_heads(lambda s: cots_in[s], cots)
    for chunk in range(8):
        columns = pl.ds(chunk * CHUNK, CHUNK)
        product = cots[columns, :].astype(F32).T * mixed_t[:, columns]
        deltas[:, columns] = jnp.broadcast_to(jnp.sum(product, axis=0, keepdims=True), (8, CHUNK))
    acc[...] = jnp.zeros_like(acc)


class FeedForward:
    def __init__(self, x, attn_out, down_cot, gain, outs, full, scratch):
        self.x, self.attn_out, self.down_cot, self.gain = x, attn_out, down_cot, gain
        self.outs, self.full = outs, full
        self.w_out, self.tiles, self.middle, self.total, self.cot_total, self.sems = scratch

    def out_copy(self):
        return pltpu.make_async_copy(self.full[0], self.w_out, self.sems.at[6])

    def tile_copies(self, t):
        columns = pl.ds(FF_TILE * t, FF_TILE)
        return [
            pltpu.make_async_copy(
                self.full[m].at[:, :, columns], self.tiles.at[t % 2, i], self.sems.at[t % 2 * 3 + i]
            )
            for i, m in enumerate((1, 2, 6))
        ]

    def load_out(self):
        self.out_copy().start()

    def load_tile(self, t):
        for copy in self.tile_copies(t):
            copy.start()

    def begin(self):
        self.out_copy().wait()
        value = self.x[...].astype(F32) + dot_nt(self.attn_out[...], self.w_out[...].reshape(1024, 2048))
        self.middle[...] = value
        self.total[...] = value
        self.outs[1][...] = (value * norm_scale(value) * self.gain[...]).astype(BF16)
        self.cot_total[...] = jnp.zeros_like(self.cot_total)

    def tile(self, t):
        mlp_in, gate_cot, up_cot, hidden = self.outs[1:5]
        for copy in self.tile_copies(t):
            copy.wait()
        w_gate, w_up, w_down = (self.tiles[t % 2, i].reshape(1024, FF_TILE) for i in range(3))
        gate = dot_nn(mlp_in[...], w_gate)
        up = dot_nn(mlp_in[...], w_up)
        sigmoid = jax.nn.sigmoid(gate)
        silu = gate * sigmoid
        hidden_tile = (silu * up).astype(BF16)
        hidden_cot = dot_nn(self.down_cot[...], w_down)
        gate_tile = (hidden_cot * up * sigmoid * (1.0 + gate * (1.0 - sigmoid))).astype(BF16)
        up_tile = (hidden_cot * silu).astype(BF16)
        columns = pl.ds(FF_TILE * t, FF_TILE)
        gate_cot[:, columns] = gate_tile
        up_cot[:, columns] = up_tile
        hidden[:, columns] = hidden_tile
        self.total[...] += dot_nt(hidden_tile, w_down)
        self.cot_total[...] += dot_nt(gate_tile, w_gate) + dot_nt(up_tile, w_up)

    def end(self):
        result, _, _, _, _, branch_cot, middle_cot, attended_cot, gain_part = self.outs
        result[...] = self.total[...].astype(BF16)
        value = self.middle[...]
        scale = norm_scale(value)
        normed = value * scale
        mlp_in_cot = self.cot_total[...]
        gain_part[...] = jnp.sum(mlp_in_cot * normed, axis=0, keepdims=True)
        scaled = mlp_in_cot * self.gain[...]
        cot = self.down_cot[...].astype(F32) + scale * (scaled - normed * mean_last(scaled * normed))
        middle_cot[...] = cot
        branch_cot[...] = cot.astype(BF16)
        attended_cot[...] = dot_nn(cot.astype(BF16), self.w_out[...].reshape(1024, 2048)).astype(BF16)


def head_columns(head):
    return (
        (pl.ds(pl.multiple_of(head * 256, 256), 256), pl.ds(0, 256)),
        (pl.ds(pl.multiple_of(head * 128, 128), 128), pl.ds(256, 128)),
        (pl.ds(pl.multiple_of(head * 128, 128), 128), pl.ds(384, 128)),
    )


def project_rows(s, low, xs, heads_w, inner, outer, query_gain, key_gain, raw, rows):
    product = dot_nn(xs[s], heads_w[...].reshape(1024, 512))
    cosine, sine = rope_rows(inner, outer, low)
    raw[s] = product[:, :384]
    for i, gain in enumerate((query_gain, query_gain, key_gain)):
        value = product[:, i * 128 : i * 128 + 128]
        value = value * norm_scale(value) * gain[...]
        value = value * cosine + pltpu.roll(value, 64, 1) * sine
        rows[s, :, i * 128 : i * 128 + 128] = value.astype(BF16)
    rows[s, :, 384:] = product[:, 384:].astype(BF16)


GATHER_AT = {
    "row 7": 2, "tile 00": 1, "tile 01": 1, "tile 11": 1, "tile 31": 1, "tile 21": 1,
    "feed 0": 1, "feed 2": 1, "feed 4": 1,
}


def forward_body(
    pair, x, attn_gain, query_gain, key_gain, inner, outer, down_cot, mlp_gain, *refs
):
    shards, refs = refs[:7], refs[7:]
    results, refs = refs[:15], refs[15:]
    full, refs = refs[:7], refs[7:]
    held, result_sem, refs = refs[:15], refs[15], refs[16:]
    attn_out, rows, raw, kv, mixed_t, log_total = held[:6]
    feed_outs = held[6:]
    stores = [
        pltpu.make_async_copy(source, target, result_sem.at[i])
        for i, (source, target) in enumerate(zip(held, results))
    ]
    feed_scratch, refs = refs[:6], refs[6:]
    (
        xs, heads_w, queries, stacked, query_pos, key_pos, total, mixed,
        x_send, x_recv, w_send, w_recv, w_load, kv_send, kv_recv, back_send, back_recv,
    ), scratch = refs[:17], refs[17:]
    me = here()
    head = group_head(me)
    twin, across = me.sibling(), me.across()
    across_twin = across.sibling()
    others = [me.move(b=ring(me.b, d)) for d in (1, 2, 3)]
    along = [me.move(a=ring(me.a, d)) for d in (1, 2, 3)]
    z_low = me.move(zl=1 - me.zl)
    greet([twin, across, across_twin] + group_neighbours(me))
    start, spread_own, turns, pass_tile, finish_tile, finish, gather_wire = gather_turns(
        me, shards, full, scratch
    )
    turns = list(turns)

    def step(place):
        for _ in range(GATHER_AT.get(place, 0)):
            turns.pop(0)()

    x_wire = Wire(x_send, x_recv, twin)
    w_wire = Wire(w_send, w_recv, twin)
    kv_wire = Wire(kv_send, kv_recv, twin)
    back_wire = Wire(back_send, back_recv, twin)
    mine = me.zh * 2 + me.core
    qkv_shards = shards[3:6]
    loads = []
    for i, (source, target) in enumerate(head_columns(head)):
        load = pltpu.make_async_copy(qkv_shards[i].at[:, source], heads_w.at[mine, :, target], w_load.at[i])
        load.start()
        loads.append(load)
    for t, spot in enumerate((across, across_twin, twin)):
        for i, (source, target) in enumerate(head_columns(group_head(spot))):
            w_wire.push((t, i), qkv_shards[i].at[:, source], heads_w.at[mine, :, target], spot)
    inputs = x[...].astype(F32)
    xs[head] = (inputs * norm_scale(inputs) * attn_gain[...]).astype(BF16)
    x_wire.push(3, xs.at[head], xs.at[head], z_low)
    for d in (1, 3, 2):
        x_wire.push(d - 1, xs.at[head], xs.at[head], along[d - 1])
    start()
    query_positions(pair, me, query_pos)
    mixed_t[...] = jnp.zeros_like(mixed_t)
    total[...] = jnp.zeros_like(total)
    low_head = me.a + 4 * (1 - me.zl)
    x_wire.take(3, xs.at[low_head])
    for d in (1, 3, 2):
        x_wire.push(3 + d, xs.at[low_head], xs.at[low_head], along[d - 1])
    spread_own()
    for load in loads:
        load.wait()
    for t, f in enumerate(
        ((1 - me.zh) * 2 + me.core, (1 - me.zh) * 2 + 1 - me.core, me.zh * 2 + 1 - me.core)
    ):
        for i, (_, target) in enumerate(head_columns(head)):
            w_wire.take((t, i), heads_w.at[f, :, target])
    arrivals = [(None, head), (None, low_head)]
    for zl, first in ((me.zl, 0), (1 - me.zl, 4)):
        for d in (1, 3, 2):
            arrivals.append((first + d - 1, ring(me.a, -d) + 4 * zl))
    for k, (slot, s) in enumerate(arrivals):
        if slot is not None:
            x_wire.take(slot, xs.at[s])
        project_rows(
            s, low_block(pair, me, me.b, s), xs, heads_w, inner, outer, query_gain, key_gain, raw, rows
        )
        for d in range(3):
            kv_wire.push((k, d), rows.at[s, :, pl.ds(256, 256)], kv.at[me.b, s], others[d])
        kv[me.b, s] = rows[s, :, 256:]
        step(f"row {k}")
    stack_heads(lambda s: rows[s, :, :256], queries)
    for d in (0, 1, 3, 2):
        j = ring(me.b, -d)
        if d:
            for k, (_, s) in enumerate(arrivals):
                kv_wire.take((k, d - 1), kv.at[j, s])
        for part in range(2):
            mix_tile(me, j, part, pair, kv, query_pos, queries, key_pos, mixed_t, total)
            step(f"tile {d}{part}")
    finish_mix(mixed, mixed_t, log_total, stacked, total)

    for i in range(1, 6):
        stores[i].start()

    def place(origin):
        return attn_out.at[:, pl.ds(pl.multiple_of(origin * 256, 256), 256)]

    for k in range(1, 8):
        peer = peer_of(head, k)
        back_wire.push(k - 1, mixed.at[peer], place(head), group_spot(me, peer))
    attn_out[:, pl.ds(pl.multiple_of(head * 256, 256), 256)] = mixed[head]
    step("back")
    feed = FeedForward(x, attn_out, down_cot, mlp_gain, feed_outs, full, feed_scratch)
    finish(0)
    feed.load_out()
    finish(1)
    finish(2)
    finish(6)
    pass_tile(0)
    pass_tile(1)
    finish_tile(0)
    feed.load_tile(0)
    for k in range(7):
        back_wire.take(k, place(peer_of(head, 7 - k)))
    stores[0].start()
    feed.begin()
    for t in range(FF_STEPS):
        if t + 2 < FF_STEPS:
            pass_tile(t + 2)
        if t + 1 < FF_STEPS:
            finish_tile(t + 1)
            feed.load_tile(t + 1)
        feed.tile(t)
        step(f"feed {t}")
    feed.end()
    for store in stores[6:]:
        store.start()
    step("end")
    assert not turns
    for m in (3, 4, 5):
        finish(m)
    for store in stores:
        store.wait()
    for wire in (x_wire, w_wire, kv_wire, back_wire, gather_wire):
        wire.close()


def attention_forward(pair, x, gains, tables, down_cot, mlp_gain, weights):
    narrow = jax.ShapeDtypeStruct((128, 1024), BF16)
    wide = jax.ShapeDtypeStruct((128, FF_STEPS * FF_TILE), BF16)
    results = [
        jax.ShapeDtypeStruct((128, 2048), BF16),
        jax.ShapeDtypeStruct((8, 128, 512), BF16),
        jax.ShapeDtypeStruct((8, 128, 384), F32),
        jax.ShapeDtypeStruct((4, 8, 128, 256), BF16),
        jax.ShapeDtypeStruct((128, 2048), F32),
        jax.ShapeDtypeStruct((8, 2048), F32),
        narrow, narrow, wide, wide, wide, narrow,
        jax.ShapeDtypeStruct((128, 1024), F32),
        jax.ShapeDtypeStruct((128, 2048), BF16),
        jax.ShapeDtypeStruct((1, 1024), F32),
    ]
    outs = pl.pallas_call(
        forward_body,
        out_shape=results
        + [jax.ShapeDtypeStruct((4,) + w.shape, w.dtype) for w in weights],
        in_specs=[SMEM] + [VMEM] * 8 + [HBM] * 7,
        out_specs=[HBM] * 22,
        scratch_shapes=[pltpu.VMEM(result.shape, result.dtype) for result in results]
        + [
            dma(len(results)),
            pltpu.VMEM((4, 256, 2048), BF16),
            pltpu.VMEM((2, 3, 4, 256, FF_TILE), BF16),
            pltpu.VMEM((128, 1024), F32),
            pltpu.VMEM((128, 1024), F32),
            pltpu.VMEM((128, 1024), F32),
            dma(7),
            pltpu.VMEM((8, 128, 1024), BF16),
            pltpu.VMEM((4, 256, 512), BF16),
            pltpu.VMEM((2048, 128), BF16),
            pltpu.VMEM((2048, 128), BF16),
            pltpu.VMEM((8, 2048), jnp.int32),
            pltpu.VMEM((TILE, CHUNK), jnp.int32),
            pltpu.VMEM((8, 2048), F32),
            pltpu.VMEM((8, 128, 256), BF16),
            dma(7), dma(7), dma(3, 3), dma(3, 3), dma(3), dma(8, 3), dma(8, 3), dma(7), dma(7),
        ]
        + gather_scratch(weights),
        compiler_params=comm_params(1),
        name="attention_forward",
    )(pair, x, *gains, *tables, down_cot, mlp_gain, *weights)
    return outs[:6], outs[6:15], [whole_rows(out) for out in outs[15:]]


def whole_rows(out):
    return out.reshape(4 * out.shape[1], out.shape[2])


PAIR_TILE = 512


def half_of(ref, half):
    width = ref.shape[-1] // 2
    return ref.at[:, :, pl.ds(half * width, width)]


def add_into(target, *sources):
    for zh in range(target.shape[0]):

        @pl.loop(0, target.shape[1] // 16)
        def _(r):
            at = pl.ds(pl.multiple_of(r * 16, 16), 16)
            total = target[zh, at, :].astype(F32)
            for source in sources:
                total = total + source[zh, at, :].astype(F32)
            target[zh, at, :] = total.astype(BF16)


class PairGrad:
    def __init__(self, me, left, right, left_scratch, twin_right, grad, wire, slot):
        self.me, self.left, self.right, self.wire, self.slot = me, left, right, wire, slot
        self.landing, self.left_t = left_scratch
        self.twin_right, self.grad = twin_right, grad

    def send(self):
        me = self.me
        twin = me.sibling()
        self.wire.push(self.slot + 2, self.right, self.twin_right, twin)
        for zh in range(0 if self.left is None else 2):
            columns = pl.ds(pl.multiple_of((zh * 2 + 1 - me.core) * 256, 256), 256)
            self.wire.push(self.slot + zh, self.left.at[:, columns], self.landing.at[zh], twin)

    def multiply(self):
        me = self.me
        for zh in range(0 if self.left is None else 2):
            columns = pl.ds(pl.multiple_of((zh * 2 + me.core) * 256, 256), 256)
            self.left_t[zh * 256 : zh * 256 + 256, 0:128] = self.left[:, columns].T
            self.wire.take(self.slot + zh, self.landing.at[zh])
            self.left_t[zh * 256 : zh * 256 + 256, 128:256] = self.landing[zh].T
        self.wire.take(self.slot + 2, self.twin_right)

        @pl.loop(0, self.twin_right.shape[1] // PAIR_TILE)
        def _(t):
            columns = pl.ds(pl.multiple_of(t * PAIR_TILE, PAIR_TILE), PAIR_TILE)
            right = jnp.concatenate([self.right[:, columns], self.twin_right[:, columns]], axis=0)
            product = dot_nn(self.left_t[...], right).astype(BF16)
            self.grad[:, :, columns] = product.reshape(2, 256, PAIR_TILE)


REDUCE_SLOTS = 13


def reduce_scratch(widths, z_first):
    scratch = []
    for k, width in enumerate(widths):
        half = width // 2
        if k in z_first:
            shapes = [
                (1, 128, half), (1, 128, half), (1, 256, half), (1, 256, half),
                (3, 1, 64, half), (1, 64, half), (3, 1, 16, half), (1, 16, half),
            ]
        else:
            shapes = [
                (2, 64, half), (2, 64, half), (2, 64, width), (2, 64, width),
                (3, 2, 16, width), (2, 16, width), (4, 16, width), (1, 16, width),
            ]
        scratch += [pltpu.VMEM(shape, BF16) for shape in shapes]
    count = len(widths)
    return scratch + [dma(count, REDUCE_SLOTS), dma(count, REDUCE_SLOTS)]


def reduce_stages(me, grads, pieces, scratch, z_first):
    wire = Wire(scratch[-2], scratch[-1], me.sibling())
    z = me.zh * 2 + me.zl
    z_low, across, z_high = me.move(zl=1 - me.zl), me.across(), me.move(zh=1 - me.zh)

    def z_spot(step):
        far = lax.rem(z + step + 4, 4)
        return me.move(zl=lax.rem(far, 2), zh=far // 2)

    def rows(ref, i, size):
        return ref.at[:, pl.ds(pl.multiple_of(i * size, size), size)]

    def ring_stages(k, slot, ahead, behind, block, bufs, half):
        far_a, far_b, in_a, in_b = bufs

        def send():
            wire.push((k, slot), half(block(2), 0), far_a, ahead)
            wire.push((k, slot + 1), half(block(2), 1), far_b, behind)
            wire.push((k, slot + 2), half(block(1), 1), half(in_a, 1), ahead)
            wire.push((k, slot + 3), half(block(-1), 0), half(in_b, 0), behind)

        def relay():
            wire.take((k, slot), far_a)
            add_into(far_a, half(block(1), 0))
            wire.push((k, slot + 4), far_a, half(in_a, 0), ahead)
            wire.take((k, slot + 1), far_b)
            add_into(far_b, half(block(-1), 1))
            wire.push((k, slot + 5), far_b, half(in_b, 1), behind)

        def collect():
            wire.take((k, slot + 2), half(in_a, 1))
            wire.take((k, slot + 3), half(in_b, 0))
            wire.take((k, slot + 4), half(in_a, 0))
            wire.take((k, slot + 5), half(in_b, 1))
            add_into(in_a, in_b, block(0))

        return send, relay, collect

    def direct_send(k, slot, axis, size, source, land):
        position = getattr(me, axis)
        for d in (1, 3, 2):
            spot = me.move(**{axis: ring(position, d)})
            wire.push((k, slot + d - 1), rows(source, ring(position, d), size), land.at[d - 1], spot)

    def direct_sum(k, slot, axis, size, source, land, target):
        for d in (1, 3, 2):
            wire.take((k, slot + d - 1), land.at[d - 1])
        own = rows(source, getattr(me, axis), size)
        for lead in range(target.shape[0]):

            @pl.loop(0, size // 16)
            def _(r):
                at = pl.ds(pl.multiple_of(r * 16, 16), 16)
                total = own[lead, at, :].astype(F32)
                for d in range(3):
                    total = total + land[d, lead, at, :].astype(F32)
                target[lead, at, :] = total.astype(BF16)

    def plain(k):
        grad, bufs = grads[k], scratch[8 * k : 8 * k + 8]
        in_a, a_land, total, z_land = bufs[2], bufs[4], bufs[5], bufs[6]
        send, relay, collect = ring_stages(
            k, 0, me.move(b=ring(me.b, 1)), me.move(b=ring(me.b, -1)),
            lambda step: rows(grad, ring(me.b, step), 64), bufs[:4], half_of,
        )

        def third():
            collect()
            direct_send(k, 6, "a", 16, in_a, a_land)

        def fourth():
            direct_sum(k, 6, "a", 16, in_a, a_land, total)
            wire.push((k, 9), total.at[1 - me.zh], z_land.at[z], across)
            wire.push((k, 10), total.at[1 - me.zh], z_land.at[z], z_high)
            wire.push((k, 11), total.at[me.zh], z_land.at[z], z_low)
            z_land[z] = total[me.zh]

        def fifth():
            for slot, spot in ((9, across), (10, z_high), (11, z_low)):
                wire.take((k, slot), z_land.at[spot.zh * 2 + spot.zl])
            total = z_land[0].astype(F32)
            for i in range(1, 4):
                total = total + z_land[i].astype(F32)
            pieces[k][0] = total.astype(BF16)

        return [send, relay, third, fourth, fifth]

    def first_z(k):
        grad, bufs = grads[k], scratch[8 * k : 8 * k + 8]
        in_a, b_land, b_sum, a_land, a_sum = bufs[2], bufs[4], bufs[5], bufs[6], bufs[7]
        width = grad.shape[2] // 2

        def columns(ref, zl):
            return ref.at[:, :, pl.ds(pl.multiple_of(zl * width, width), width)]

        def block(step):
            far = lax.rem(z + step + 4, 4)
            return columns(grad.at[pl.ds(far // 2, 1)], lax.rem(far, 2))

        send, relay, collect = ring_stages(
            k, 0, z_spot(1), z_spot(-1), block, bufs[:4],
            lambda view, i: view.at[:, pl.ds(128 * i, 128)],
        )

        def third():
            collect()
            direct_send(k, 6, "b", 64, in_a, b_land)

        def fourth():
            direct_sum(k, 6, "b", 64, in_a, b_land, b_sum)
            direct_send(k, 9, "a", 16, b_sum, a_land)

        def fifth():
            direct_sum(k, 9, "a", 16, b_sum, a_land, a_sum)
            place = columns(pieces[k], me.zl)
            place[...] = a_sum[...]
            wire.push((k, 12), a_sum, place, z_low)

        def sixth():
            wire.take((k, 12), columns(pieces[k], 1 - me.zl))

        return [send, relay, third, fourth, fifth, sixth]

    lists = [first_z(k) if k in z_first else plain(k) for k in range(len(grads))]
    return lists, wire


def replicate_stages(me, pieces, outs, send, recv, load_sem):
    wire = Wire(send, recv, me.sibling())
    loads = {}

    def cut(k, row, rows, half=None):
        width = outs[k].shape[1] // 2
        at = pl.ds(pl.multiple_of(row, 16), rows)
        if half is None:
            return outs[k].at[at]
        return outs[k].at[at, pl.ds(half * width, width)]

    b_next, b_prev = me.move(b=ring(me.b, 1)), me.move(b=ring(me.b, -1))

    def a_row(step):
        return (me.b * 4 + ring(me.a, step)) * 16

    def b_row(step):
        return ring(me.b, step) * 64

    def a_send(k):
        place = cut(k, a_row(0), 16)
        for d in (1, 3, 2):
            wire.push((k, d - 1), pieces[k].at[0], place, me.move(a=ring(me.a, d)))
        loads[k] = pltpu.make_async_copy(pieces[k].at[0], place, load_sem.at[k])
        loads[k].start()

    def b_send(k):
        for d in (1, 3, 2):
            wire.take((k, d - 1), cut(k, a_row(-d), 16))
        loads[k].wait()
        mine = cut(k, b_row(0), 64)
        wire.push((k, 4), mine, mine, b_next)
        wire.push((k, 5), mine, mine, b_prev)

    def b_relay(k):
        wire.take((k, 4), cut(k, b_row(-1), 64))
        wire.push((k, 6), cut(k, b_row(-1), 64, 0), cut(k, b_row(-1), 64, 0), b_next)
        wire.take((k, 5), cut(k, b_row(1), 64))
        wire.push((k, 7), cut(k, b_row(1), 64, 1), cut(k, b_row(1), 64, 1), b_prev)

    def b_collect(k):
        wire.take((k, 6), cut(k, b_row(2), 64, 0))
        wire.take((k, 7), cut(k, b_row(2), 64, 1))

    stages = (a_send, b_send, b_relay, b_collect)
    lists = [[functools.partial(stage, k) for stage in stages] for k in range(len(pieces))]
    return lists, wire


class Plan:
    def __init__(self, **lists):
        self.lists = {name: list(stages) for name, stages in lists.items()}

    def run(self, names):
        for name in names:
            self.lists[name].pop(0)()

    def check(self):
        assert not any(self.lists.values())


def gain_turns(me, gains, gains_out, gain_slots, gain_send, gain_recv):
    first = me.core == 0
    x, y = jnp.where(first, me.a, me.b), jnp.where(first, me.b, me.a)
    z = me.zh * 2 + me.zl
    wire = Wire(gain_send, gain_recv, me.sibling())

    def pick(d, on_x):
        use_a = first if on_x else jnp.logical_not(first)
        return me.move(
            a=jnp.where(use_a, ring(me.a, d), me.a), b=jnp.where(use_a, me.b, ring(me.b, d))
        )

    def z_spot(d):
        far = lax.rem(z + d, 4)
        return me.move(zl=lax.rem(far, 2), zh=far // 2)

    def push(stage, position, spots):
        for d, spot in enumerate(spots):
            slot = gain_slots.at[stage, position]
            wire.push((stage, d), slot, slot, spot)

    def take(stage, position, size):
        for d in range(size - 1):
            wire.take((stage, d), gain_slots.at[stage, lax.rem(position + size - 1 - d, size)])

    def total(stage):
        return (gain_slots[stage, 0] + gain_slots[stage, 1]) + (gain_slots[stage, 2] + gain_slots[stage, 3])

    def turn0():
        gain_slots[0, me.core] = gains[...]
        push(0, me.core, [me.sibling()])

    def turn1():
        take(0, me.core, 2)
        gain_slots[1, x] = gain_slots[0, 0] + gain_slots[0, 1]
        push(1, x, [pick(d, True) for d in (1, 2, 3)])

    def turn2():
        take(1, x, 4)
        gain_slots[2, y] = total(1)
        push(2, y, [pick(d, False) for d in (1, 2, 3)])

    def turn3():
        take(2, y, 4)
        gain_slots[3, z] = total(2)
        push(3, z, [z_spot(d) for d in (1, 2, 3)])

    def turn4():
        take(3, z, 4)
        gains_out[...] = total(3)

    return [turn0, turn1, turn2, turn3, turn4], wire.close


def unrope(s, low, grads, raw, inner, outer, gain, column, gain_part):
    cosine, sine = rope_rows(inner, outer, low)
    value = raw[s, :, column : column + 128]
    scale = norm_scale(value)
    hat = value * scale
    hat_cot = grads * cosine - pltpu.roll(grads, 64, 1) * sine
    gain_part[...] += jnp.sum((hat_cot * hat).reshape(16, 8, 128), axis=0)
    scaled = hat_cot * gain[...]
    return (scale * (scaled - hat * mean_last(scaled * hat))).astype(BF16)


WIDTHS = (3072, 3072, 3072, 2048, 2048, 2048)
Z_FIRST = (2, 3, 4)
BETWEEN = {
    "cots": "ddgguouo",
    "tiles": "odug",
    "own tile": "",
    "rows 2": "",
    "rows 4": "u",
    "rows 6": "",
    "rows 0": "gudog",
    "proj": "qqdkkguukqodgukqd",
    "weights": "dgo",
    "input": "kosqodsqukskoqqkudqkgsoqgokqsd",
}


def backward_body(*refs):
    (
        pair, attn_gain, query_gain, key_gain, inner, outer, mlp_gain_part, wq, wk, wv,
    ), sources, refs = refs[:10], refs[10:25], refs[25:]
    (input_cot, gains_out), outs, refs = refs[:2], refs[2:8], refs[8:]
    (
        cots_in, dkv, queries, cots, deltas, query_pos, key_pos, probs_all, score_cots, acc, held, stacked, message,
        attn_in, proj, head_gains, gains, gain_slots,
        cot_send, cot_recv, p_send, p_recv, m_send, m_recv, w_send, w_recv, out_send, out_recv, out_load, w_load,
        gain_send, gain_recv,
    ), refs = refs[:32], refs[32:]
    held_inputs, input_sem, refs = refs[:15], refs[15], refs[16:]
    inputs_in = [
        pltpu.make_async_copy(source, target, input_sem.at[i])
        for i, (source, target) in enumerate(zip(sources, held_inputs))
    ]
    for load in inputs_in:
        load.start()
    (
        parts, down_cot, hidden, mlp_in, gate_cot, up_cot, branch_cot, attn_out, x,
        rows, mixed_t, log_total, kv, raw, middle_cot,
    ) = held_inputs
    pieces, grads, refs = refs[:6], list(refs[6:11]), refs[11:]
    grads.append(grads[2].at[:, :, pl.ds(0, WIDTHS[5])])
    me = here()
    head = group_head(me)
    twin = me.sibling()
    others = [me.move(b=ring(me.b, d)) for d in (1, 2, 3)]
    greet([twin, me.across(), me.move(zh=1 - me.zh)] + group_neighbours(me))
    cot_wire = Wire(cot_send, cot_recv, twin)
    p_wire = Wire(p_send, p_recv, twin)
    m_wire = Wire(m_send, m_recv, twin)
    w_wire = Wire(w_send, w_recv, twin)

    def of_head(ref, h):
        return ref.at[:, pl.ds(pl.multiple_of(h * 256, 256), 256)]

    for load in inputs_in[:9]:
        load.wait()
    for k in range(1, 8):
        peer = peer_of(head, k)
        cot_wire.push(k - 1, of_head(parts, peer), cots_in.at[head], group_spot(me, peer))
    lefts = (mlp_in, None, down_cot, branch_cot, attn_in, None)
    rights = (
        gate_cot, up_cot, hidden, attn_out, proj.at[:, pl.ds(0, 2048)], proj.at[:, pl.ds(2048, 2048)]
    )
    held_lefts, twin_rights, refs = refs[:8], refs[8:14], refs[14:]
    pairs = []
    for i, share in enumerate((0, 0, 1, 2, 3, 3)):
        pairs.append(
            PairGrad(
                me, lefts[i], rights[i], held_lefts[2 * share : 2 * share + 2], twin_rights[i], grads[i], w_wire, 3 * i
            )
        )
    sums, sum_wire = reduce_stages(me, grads, pieces, refs, Z_FIRST)
    copies, out_wire = replicate_stages(me, pieces, outs, out_send, out_recv, out_load)
    small, gain_finish = gain_turns(me, gains, gains_out, gain_slots, gain_send, gain_recv)
    plan = Plan(s=small, **{
        name: [pairs[i].multiply] + sums[i] + copies[i] for i, name in enumerate("gudoqk")
    })
    for i in (2, 0, 1, 3):
        pairs[i].send()
    query_positions(pair, me, query_pos)
    cots_in[head] = parts[:, pl.ds(pl.multiple_of(head * 256, 256), 256)]
    head_gains[...] = jnp.zeros_like(head_gains)
    inputs = x[...].astype(F32)
    scale = norm_scale(inputs)
    normed = inputs * scale
    attn_in[...] = (normed * attn_gain[...]).astype(BF16)
    plan.run(BETWEEN["cots"])
    for k in range(7):
        cot_wire.take(k, cots_in.at[peer_of(head, 7 - k)])
    for load in inputs_in[9:]:
        load.wait()
    start_grad(rows, mixed_t, cots_in, queries, cots, deltas, acc)
    for d in (2, 1, 3, 0):
        j = ring(me.b, d)
        if d == 0:
            plan.run(BETWEEN["tiles"])
        for part in range(2):
            grad_tile(
                me, j, part, pair, kv, query_pos, queries, cots, deltas, log_total, key_pos,
                probs_all, score_cots, acc, dkv,
            )
        if d:
            for k in range(8):
                peer = peer_of(head, k)
                p_wire.push((k, d - 1), dkv.at[j, peer], held.at[d - 1, peer], others[d - 1])
    for chunk in range(8):
        columns = pl.ds(chunk * CHUNK, CHUNK)
        stacked[columns, :] = (acc[:, columns] * SCORE_SCALE).T
    plan.run(BETWEEN["own tile"])

    def places(h):
        return (
            (pl.ds(0, 256), pl.ds(pl.multiple_of(h * 256, 256), 256)),
            (pl.ds(256, 128), pl.ds(pl.multiple_of(2048 + h * 128, 128), 128)),
            (pl.ds(384, 128), pl.ds(pl.multiple_of(3072 + h * 128, 128), 128)),
        )

    for k in (1, 2, 3, 4, 5, 6, 7, 0):
        s = peer_of(head, k)
        low = low_block(pair, me, me.b, s)
        for d in range(3):
            p_wire.take((k, d), held.at[d, s])
        for h in range(2):
            turned = jnp.concatenate(
                [
                    stacked[pl.ds(pl.multiple_of(part * 1024 + s * 128 + h * 64, 64), 64), :]
                    for part in range(2)
                ],
                axis=0,
            )
            message[s, :, h * 128 : h * 128 + 128] = unrope(
                s, low, turned, raw, inner, outer, query_gain, h * 128, head_gains.at[0]
            )
        total = (
            dkv[me.b, s].astype(F32)
            + held[0, s].astype(F32)
            + held[1, s].astype(F32)
            + held[2, s].astype(F32)
        )
        message[s, :, 256:384] = unrope(
            s, low, total[:, :128], raw, inner, outer, key_gain, 256, head_gains.at[1]
        )
        message[s, :, 384:] = total[:, 128:].astype(BF16)
        if k:
            for i, (source, target) in enumerate(places(head)):
                m_wire.push((k - 1, i), message.at[s, :, source], proj.at[:, target], group_spot(me, s))
        if k % 2 == 0:
            plan.run(BETWEEN[f"rows {k}"])
    for source, target in places(head):
        proj[:, target] = message[head, :, source]
    for k in range(7):
        for i, (_, target) in enumerate(places(peer_of(head, 7 - k))):
            m_wire.take((k, i), proj.at[:, target])
    for i in (4, 5):
        pairs[i].send()
    for k in range(3):
        sum_wire.settle(k)
    plan.run(BETWEEN["proj"])

    loads = []
    value_rows = (score_cots, probs_all)
    for i in range(4):
        at = pl.ds(256 * i, 256)
        target = grads[i // 2].at[i % 2]
        loads.append((wq.at[at], target.at[:, pl.ds(0, 2048)]))
        loads.append((wk.at[at], target.at[:, pl.ds(2048, 1024)]))
        loads.append((wv.at[at], value_rows[i // 2].at[pl.ds(i % 2 * 256, 256)]))
    loads = [pltpu.make_async_copy(*pair_, w_load.at[i]) for i, pair_ in enumerate(loads)]
    for load in loads:
        load.start()
    plan.run(BETWEEN["weights"])
    for load in loads:
        load.wait()
    attn_in_cot = jnp.concatenate(
        [
            dot_nt(proj[:, :3072], grads[i // 2][i % 2])
            + dot_nt(proj[:, 3072:], value_rows[i // 2][i % 2 * 256 : i % 2 * 256 + 256, :])
            for i in range(4)
        ],
        axis=1,
    )
    scaled = attn_in_cot * attn_gain[...]
    input_cot[...] = middle_cot[...] + scale * (scaled - normed * mean_last(scaled * normed))
    gains[...] = jnp.zeros_like(gains)
    gains[0:1, :] = jnp.sum(attn_in_cot * normed, axis=0, keepdims=True)
    gains[1:2, :] = mlp_gain_part[...]
    for i in range(2):
        gains[2 + i : 3 + i, 0:128] = jnp.sum(head_gains[i], axis=0, keepdims=True)
    plan.run(BETWEEN["input"])
    plan.check()
    gain_finish()
    for wire in (cot_wire, p_wire, m_wire, w_wire, sum_wire, out_wire):
        wire.close()


def attention_backward(pair, x, gains, tables, kept, attended_cot, lefts, rights, middle_cot, mlp_gain_part, weights):
    heads = (8, 128, 256)
    count = len(WIDTHS)
    attn_out = rights[3]
    attended, raw, kv, mixed_t, log_total = kept
    held = (
        attended_cot, lefts[1], rights[2], lefts[0], rights[0], rights[1], lefts[2], attn_out, x,
        attended, mixed_t, log_total, kv, raw, middle_cot,
    )
    outs = pl.pallas_call(
        backward_body,
        out_shape=[jax.ShapeDtypeStruct((128, 1024), F32), jax.ShapeDtypeStruct((4, 1024), F32)]
        + [jax.ShapeDtypeStruct((256, width), BF16) for width in WIDTHS],
        in_specs=[SMEM] + [VMEM] * 6 + [HBM] * 18,
        out_specs=[VMEM] * 2 + [HBM] * count,
        scratch_shapes=[
            pltpu.VMEM(heads, BF16),
            pltpu.VMEM((4,) + heads, BF16),
            pltpu.VMEM((2048, 128), BF16),
            pltpu.VMEM((2048, 128), BF16),
            pltpu.VMEM((8, 2048), F32),
            pltpu.VMEM((8, 2048), jnp.int32),
            pltpu.VMEM((TILE, CHUNK), jnp.int32),
            pltpu.VMEM((TILE, 1024), BF16),
            pltpu.VMEM((TILE, 1024), BF16),
            pltpu.VMEM((128, 2048), F32),
            pltpu.VMEM((3,) + heads, BF16),
            pltpu.VMEM((2048, 128), F32),
            pltpu.VMEM((8, 128, 512), BF16),
            pltpu.VMEM((128, 1024), BF16),
            pltpu.VMEM((128, 4096), BF16),
            pltpu.VMEM((2, 8, 128), F32),
            pltpu.VMEM((4, 1024), F32),
            pltpu.VMEM((4, 4, 4, 1024), F32),
            dma(7), dma(7), dma(8, 3), dma(8, 3), dma(7, 3), dma(7, 3), dma(18), dma(18),
            dma(count, 8), dma(count, 8), dma(count), dma(12), dma(4, 3), dma(4, 3),
        ]
        + [pltpu.VMEM(value.shape, value.dtype) for value in held]
        + [dma(len(held))]
        + [pltpu.VMEM((1, 16, width), BF16) for width in WIDTHS]
        + [pltpu.VMEM((2, 256, width), BF16) for width in WIDTHS[:5]]
        + [pltpu.VMEM((2, 128, 256), BF16), pltpu.VMEM((512, 256), BF16)] * 4
        + [pltpu.VMEM((128, width), BF16) for width in WIDTHS]
        + reduce_scratch(WIDTHS, Z_FIRST),
        compiler_params=comm_params(2, 62 * 1024 * 1024),
        name="attention_backward",
    )(pair, *gains, *tables, mlp_gain_part, *weights, *held)
    return outs[0], outs[1], outs[2:]


WIDEN_STEPS = 8


def widen_body(
    result, input_cot, gate, up, down, out, query, key_value, gains,
    result_out, input_out, query_out, key_out, value_out, out_out, gate_out, up_out, down_out, g0, g1, g2, g3,
):
    result_out[0] = result[...]
    input_out[0] = input_cot[...]
    for source, target in ((query, query_out), (out, out_out), (gate, gate_out), (up, up_out), (down, down_out)):
        target[...] = source[...].astype(F32)
    key_out[...] = key_value[:, :1024].astype(F32)
    value_out[...] = key_value[:, 1024:].astype(F32)
    for i, target in enumerate((g0, g1, g2, g3)):
        target[...] = gains[i : i + 1, : target.shape[1]]


def widen_results(result, input_cot, grads, gains):
    def rows(array_shape):
        block = (array_shape[0] // WIDEN_STEPS,) + array_shape[1:]
        return pl.BlockSpec(block, lambda t: (t, 0))

    def split(array_shape):
        block = (1, array_shape[1] // WIDEN_STEPS, array_shape[2])
        return pl.BlockSpec(block, lambda t: (0, t, 0))

    def whole(array_shape):
        return pl.BlockSpec(array_shape, lambda t: (0, 0))

    tokens = (1, 128, 1024)
    widths = (2048, 1024, 1024, 2048, 3072, 3072, 3072)
    lengths = (1024, 1024, 128, 128)
    outs = pl.pallas_call(
        widen_body,
        grid=(WIDEN_STEPS,),
        out_shape=[jax.ShapeDtypeStruct(tokens, BF16), jax.ShapeDtypeStruct(tokens, F32)]
        + [jax.ShapeDtypeStruct((256, width), F32) for width in widths]
        + [jax.ShapeDtypeStruct((1, length), F32) for length in lengths],
        in_specs=[rows((128, 1024)), rows((128, 1024))]
        + [rows(grad.shape) for grad in grads]
        + [whole(gains.shape)],
        out_specs=[split(tokens), split(tokens)]
        + [rows((256, width)) for width in widths]
        + [whole((1, length)) for length in lengths],
        compiler_params=pltpu.CompilerParams(vmem_limit_bytes=VMEM_LIMIT),
        name="widen_results",
    )(result, input_cot, *grads, gains)
    return tuple(outs[:9]) + tuple(out[0] for out in outs[9:])


def shards(
    tokens,
    query_weight,
    key_weight,
    value_weight,
    out_weight,
    gate_weight,
    up_weight,
    down_weight,
    attn_gain,
    mlp_gain,
    query_gain,
    key_gain,
    pair_order,
    out_grad,
):
    tables = rope_tables()
    attn_row, query_row, key_row = attn_gain[None], query_gain[None], key_gain[None]
    down_cot = out_grad[0]
    (attn_out, *kept), feed, full = attention_forward(
        pair_order,
        tokens[0],
        (attn_row, query_row, key_row),
        tables,
        down_cot,
        mlp_gain[None],
        [out_weight, gate_weight, up_weight, query_weight, key_weight, value_weight, down_weight],
    )
    result, mlp_in, gate_cot, up_cot, hidden, branch_cot, middle_cot, attended_cot, mlp_gain_part = feed
    full_qkv = full[3:6]
    input_cot, gains, grads = attention_backward(
        pair_order,
        tokens[0],
        (attn_row, query_row, key_row),
        tables,
        kept,
        attended_cot,
        (mlp_in, down_cot, branch_cot),
        (gate_cot, up_cot, hidden, attn_out),
        middle_cot,
        mlp_gain_part,
        full_qkv,
    )
    return widen_results(result, input_cot, grads, gains)


def solution(mesh):
    rows, split, whole = P("fsdp", None), P("fsdp", "ctx", None), P()
    return jax.shard_map(
        shards,
        mesh=mesh,
        in_specs=(split,) + (rows,) * 7 + (whole,) * 4 + (rows, split),
        out_specs=(split, split) + (rows,) * 7 + (whole,) * 4,
        check_vma=False,
    )
```
